32 devices in a mesh: groups: 2 (over y), tp: 4 (over x, core), sub: 4 (over z).
Axes of the slice: x: 2, y: 2, z: 4, core: 2. Of those that a mesh axis runs over, the one named last changes fastest.
Arguments:
- gate_pre: bfloat16 [1536, 32768], P('groups', ('tp', 'sub')), parts along dimension 0, may hold values from -8 to 8
- up_pre: bfloat16 [1536, 32768], P('groups', ('tp', 'sub')), parts along dimension 0, may hold values from -8 to 8
- down_weight: bfloat16 [32768, 16384], P('tp', 'sub'), may hold values from -0.046875 to 0.046875
- residual: bfloat16 [1536, 16384], P('groups', ('sub', 'tp')), parts along dimension 0, may hold values from -20 to 20
- signs: int32 [16384], P('sub'), may hold values from -1 to 1, as said below
- row_slot: int32 [1536], P('groups'), parts along dimension 0, may hold values from 0 to 767, each once
- norm_gain: float32 [16384], P('sub'), may hold values from 0.1 to 1.9
Outputs:
- stream: bfloat16 [1536, 16384], P('groups', ('sub', 'tp')), parts along dimension 0
- normed: bfloat16 [1536, 16384], P('groups', 'sub'), parts along dimension 0
The draws below stay inside these ranges and needn't reach their ends.
There are 2 independent parts, one for each index of `groups`. The reference program is written for one: setup_inputs(seed, part) draws one part's arguments, and reference() takes and returns one part's arrays. A program takes and returns all parts, laid end to end along the dimension named above; an argument that names none is the same for every part. Nothing has to cross between parts.
Inputs may be any that keep to these rules, and one draw needn't show every extreme that they name: `row_slot`: a permutation of the slots. `signs`: every entry is -1 or 1.
All inputs are finite; a program needn't handle non-finite values.
Results may differ from the reference program's by a relative error of at most 0.0056.
Values may be sent and summed in bfloat16 or wider, within the bound.
No kernel may reach another device: no remote copies, remote signals or barrier semaphores. Data moves between devices by JAX's collectives and lax.ppermute only.
A program may use at most 256 MiB of HBM per device.

```python
import jax
import jax.numpy as jnp
from jax import lax

D = 16384
FF = 32768
ROWS = 768
N_TP = 4


def draw_residual(key, part):
    key = jax.random.fold_in(key, 11)
    first = jax.random.fold_in(key, 0)
    columns = jnp.arange(D, dtype=jnp.float32) / D
    rising = 1.0 + 4.0 * columns
    values = jnp.clip(jax.random.normal(first, (ROWS, D), jnp.float32), -4.0, 4.0) * rising
    return values.astype(jnp.bfloat16)


def draw_signs(key, part):
    key = jax.random.fold_in(key, 12)
    return (2 * jax.random.randint(key, (D,), 0, 2) - 1).astype(jnp.int32)


def strengthened(entries, stream_key, source, target, shards_of, factor):
    def block_of(position):
        return (jnp.arange(entries.shape[position]) // (entries.shape[position] // shards_of)).reshape((-1,) + (1,) * (entries.ndim - 1 - position))

    near = jax.random.permutation(stream_key, shards_of)[block_of(target)]
    second = (block_of(target) + shards_of // 2) % shards_of
    return jnp.where((block_of(source) == near) | (block_of(source) == second), factor * entries, entries)


def steps_of(key, dims, cuts, smallest, largest):
    loudness, own = 1.0, jax.random.fold_in(key, 6)
    for position, parts in cuts:
        draws = jnp.exp(jax.random.uniform(jax.random.fold_in(own, position), (parts,), jnp.float32, smallest / len(cuts), largest / len(cuts)))
        loudness = loudness * jnp.repeat(draws, dims[position] // parts).reshape([-1 if axis == position else 1 for axis in range(len(dims))])
    return loudness


def noise(key, dims, scale, limit, shards=(), kind=jnp.bfloat16):
    array = scale * jax.random.normal(key, dims, jnp.float32)
    if shards:
        array = array * steps_of(key, dims, shards, -0.22, 0.18)
    return jnp.clip(array, -limit, limit).astype(kind)


def heavy_noise(stream_key, dims, deviation, most, cuts, heavy, kind=jnp.bfloat16):
    result = deviation * jax.random.normal(stream_key, dims, jnp.float32)
    if cuts:
        result = result * steps_of(stream_key, dims, cuts, -0.22, 0.18)
    return jnp.clip(strengthened(result, jax.random.fold_in(stream_key, 3), *heavy), -most, most).astype(kind)


def setup_inputs(seed: int = 0, part: int = 0) -> dict:
    seeds = jax.random.split(jax.random.key(seed), 8)
    part_splits = jax.random.split(jax.random.fold_in(seeds[7], part), 8)
    gate_pre = noise(part_splits[0], (ROWS, FF), 2.0, 8.0, ((1, 16),))
    up_pre = noise(part_splits[1], (ROWS, FF), 2.0, 8.0, ((1, 16),))
    down_weight = heavy_noise(seeds[2], (FF, D), FF ** -0.5, 0.046875, ((0, 4), (1, 4)), (0, 1, 4, 2.0))
    residual = draw_residual(jax.random.fold_in(jax.random.fold_in(seeds[7], part), 71), part)
    signs = draw_signs(jax.random.fold_in(seeds[7], 71), part)
    row_slot = jax.random.permutation(part_splits[5], ROWS).astype(jnp.int32)
    norm_gain = jnp.clip(1.0 + 0.18 * jax.random.normal(seeds[6], (D,), jnp.float32), 0.1, 1.9)
    return dict(gate_pre=gate_pre, up_pre=up_pre, down_weight=down_weight, residual=residual, signs=signs, row_slot=row_slot, norm_gain=norm_gain)


def hadamard():
    index = jnp.arange(128, dtype=jnp.int32)
    common = index[:, None] & index[None, :]
    parity = sum((common >> shift & 1 for shift in range(7)))
    return jnp.where(parity % 2 == 0, 1.0, -1.0).astype(jnp.float32) * 0.08838834764831845

def reference(gate_pre, up_pre, down_weight, residual, signs, row_slot, norm_gain):
    hidden = (jax.nn.silu(gate_pre.astype(jnp.float32)) * up_pre.astype(jnp.float32)).astype(jnp.bfloat16)
    matrix = hadamard()
    sign_blocks = signs.astype(jnp.float32).reshape(D // 128, 128)
    width = FF // N_TP

    def add_block(block, total):
        start = (block * width).astype(jnp.int32)
        piece = lax.dynamic_slice_in_dim(hidden, start, width, 1)
        rows = lax.dynamic_slice_in_dim(down_weight, start, width, 0)
        partial_value = jnp.dot(piece, rows, preferred_element_type=jnp.float32)
        signed = partial_value.reshape(ROWS, D // 128, 128) * sign_blocks
        rotated = jnp.einsum('rbk,kj->rbj', signed, matrix, precision=lax.Precision.HIGHEST)
        return total + rotated
    delta = lax.fori_loop(0, N_TP, add_block, jnp.zeros((ROWS, D // 128, 128), jnp.float32))
    mine = jnp.take(residual, row_slot, axis=0)
    stream = (mine.astype(jnp.float32) + delta.reshape(ROWS, D)).astype(jnp.bfloat16)
    wide = stream.astype(jnp.float32)
    meansq = lax.optimization_barrier(jnp.mean(wide * wide, axis=1))
    normed = (wide * lax.rsqrt(meansq + 1e-05)[:, None] * norm_gain).astype(jnp.bfloat16)
    return (stream, normed)
```

```python
import functools

import jax
import jax.numpy as jnp
from jax import lax
from jax.experimental import pallas as pl
from jax.experimental.pallas import tpu as pltpu
from jax.sharding import PartitionSpec as P

D = 16384
H_SCALE = 0.08838834764831845
VMEM = 48 * 1024 * 1024
TOKEN = (8, 128)


def hadamard_signs():
    index = jnp.arange(128, dtype=jnp.int32)
    common = index[:, None] & index[None, :]
    parity = sum((common >> shift & 1 for shift in range(7)))
    return jnp.where(parity % 2 == 0, 1.0, -1.0).astype(jnp.bfloat16)


def row_chunks(rows, tp):
    if tp == 4 and rows == 768:
        return [128] * 6
    return [rows // 2] * 2


def block_of(width, most):
    size = min(width, most)
    while width % size:
        size //= 2
    return size


def hidden_kernel(more, gate, up, *refs):
    out, token = refs[more:]
    value = gate[...].astype(jnp.float32)
    value = value / (1.0 + jnp.exp(-value)) * up[...].astype(jnp.float32)
    out[...] = value.astype(jnp.bfloat16)
    token[...] = jnp.zeros(TOKEN, jnp.float32)


def hidden_chunk(gate, up, start, rows, after):
    columns = gate.shape[1]
    place = start // rows
    line = pl.BlockSpec((rows, columns), lambda i: (place, 0))
    small = pl.BlockSpec(TOKEN, lambda i: (0, 0))
    return pl.pallas_call(
        functools.partial(hidden_kernel, len(after)),
        grid=(1,),
        in_specs=[line, line] + [small] * len(after),
        out_specs=[pl.BlockSpec((rows, columns), lambda i: (0, 0)), small],
        out_shape=[
            jax.ShapeDtypeStruct((rows, columns), jnp.bfloat16),
            jax.ShapeDtypeStruct(TOKEN, jnp.float32),
        ],
        compiler_params=pltpu.CompilerParams(vmem_limit_bytes=VMEM),
        name="hidden_chunk",
    )(gate, up, *after)


def matmul_kernel(tp, after, where, piece, weight, *refs):
    outs = refs[after : after + tp]
    token, total = refs[after + tp :]
    step = pl.program_id(0)
    me = where[1]
    width = total.shape[2]
    value = piece[...]
    for t in range(tp):
        product = jnp.dot(
            value, weight[:, t * width : (t + 1) * width], preferred_element_type=jnp.float32
        )

        @pl.when(step == 0)
        def _():
            total[t] = product

        @pl.when(step != 0)
        def _():
            total[t] += product

    @pl.when(step == pl.num_programs(0) - 1)
    def _():
        for d in range(tp):
            outs[d][...] = total[me ^ d].astype(outs[d].dtype)
        token[...] = jnp.zeros(TOKEN, jnp.float32)


def matmul_chunk(where, gathered, weight, tp, parts, after, arrived):
    rows = gathered.shape[0] // parts
    depth = gathered.shape[1]
    block = block_of(depth, 512)
    per = depth // block
    columns = weight.shape[1]
    width = columns // tp
    whole = pl.BlockSpec((rows, width), lambda j, s: (0, 0))
    return pl.pallas_call(
        functools.partial(matmul_kernel, tp, len(after) + len(arrived)),
        grid_spec=pltpu.PrefetchScalarGridSpec(
            num_scalar_prefetch=1,
            grid=(parts * per,),
            in_specs=[
                pl.BlockSpec((rows, block), lambda j, s: (j // per, j % per)),
                pl.BlockSpec((block, columns), lambda j, s: (j, 0)),
            ]
            + [pl.BlockSpec(TOKEN, lambda j, s: (0, 0))] * len(after)
            + [pl.BlockSpec(memory_space=pl.ANY)] * len(arrived),
            out_specs=[whole] * tp + [pl.BlockSpec(TOKEN, lambda j, s: (0, 0))],
            scratch_shapes=[pltpu.VMEM((tp, rows, width), jnp.float32)],
        ),
        out_shape=[jax.ShapeDtypeStruct((rows, width), jnp.float32)]
        + [jax.ShapeDtypeStruct((rows, width), jnp.bfloat16)] * (tp - 1)
        + [jax.ShapeDtypeStruct(TOKEN, jnp.float32)],
        compiler_params=pltpu.CompilerParams(vmem_limit_bytes=VMEM),
        cost_estimate=pl.CostEstimate(
            flops=2 * rows * parts * depth * columns,
            bytes_accessed=2 * weight.size,
            transcendentals=0,
        ),
        name="matmul_chunk",
    )(where, gathered, weight, *after, *arrived)


def stream_kernel(tp, more, *refs):
    own = refs[0]
    others = refs[1:tp]
    signs, matrix, residual = refs[tp : tp + 3]
    stream, chunk, squares = refs[tp + 3 + more :]
    total = own[...]
    for other in others:
        total = total + other[...].astype(jnp.float32)
    total = total * signs[...].astype(jnp.float32)
    rows, width = total.shape
    turn = matrix[...]
    for b in range(width // 128):
        piece = total[:, b * 128 : (b + 1) * 128]
        rotated = jnp.zeros((rows, 128), jnp.float32)
        for _ in range(3):
            part = piece.astype(jnp.bfloat16)
            rotated = rotated + jnp.dot(part, turn, preferred_element_type=jnp.float32)
            piece = piece - part.astype(jnp.float32)
        kept = residual[:, b * 128 : (b + 1) * 128].astype(jnp.float32)
        value = (kept + rotated * H_SCALE).astype(jnp.bfloat16)
        stream[:, b * 128 : (b + 1) * 128] = value
        chunk[:, b * 128 : (b + 1) * 128] = value
    local = chunk[...].astype(jnp.float32)
    squares[...] = lax.dot_general(
        jnp.ones((8, width), jnp.float32),
        local * local,
        (((1,), (1,)), ((), ())),
        precision=lax.Precision.HIGHEST,
        preferred_element_type=jnp.float32,
    )


def stream_chunk(pieces, signs, matrix, residual, so_far, start, after):
    tp = len(pieces)
    rows, width = pieces[0].shape
    place = start // rows
    vm = pl.BlockSpec((rows, width), lambda i: (0, 0))
    line = pl.BlockSpec((rows, width), lambda i: (place, 0))
    operands = [*pieces, signs, matrix, residual]
    specs = (
        [vm] * tp
        + [
            pl.BlockSpec((1, width), lambda i: (0, 0)),
            pl.BlockSpec((128, 128), lambda i: (0, 0)),
            line,
        ]
    )
    aliases = {}
    if so_far is not None:
        aliases = {len(operands): 0}
        operands.append(so_far)
        specs.append(pl.BlockSpec(memory_space=pl.ANY))
    operands += after
    specs += [pl.BlockSpec(TOKEN, lambda i: (0, 0))] * len(after)
    return pl.pallas_call(
        functools.partial(stream_kernel, tp, len(aliases) + len(after)),
        grid=(1,),
        in_specs=specs,
        out_specs=[line, vm, pl.BlockSpec((8, rows), lambda i: (0, 0))],
        out_shape=[
            jax.ShapeDtypeStruct(residual.shape, jnp.bfloat16),
            jax.ShapeDtypeStruct((rows, width), jnp.bfloat16),
            jax.ShapeDtypeStruct((8, rows), jnp.float32),
        ],
        input_output_aliases=aliases,
        compiler_params=pltpu.CompilerParams(vmem_limit_bytes=VMEM),
        name="stream_chunk",
    )(*operands)


def norm_kernel(tp, more, where, *refs):
    pieces = refs[:tp]
    squares = refs[tp : 2 * tp]
    gain = refs[2 * tp]
    out, token = refs[2 * tp + 1 + more :]
    token[...] = jnp.zeros(TOKEN, jnp.float32)
    me = where[1]
    total = squares[0][...]
    for other in squares[1:]:
        total = total + other[...]
    inverse = lax.rsqrt(total / D + 1e-05)
    scale = jnp.transpose(inverse)[:, 0:1]
    width = pieces[0].shape[1]
    for d in range(tp):
        at = pl.ds(pl.multiple_of((me ^ d) * width, width), width)
        value = pieces[d][...].astype(jnp.float32) * scale * gain[:, at]
        out[:, at] = value.astype(jnp.bfloat16)


def norm_chunk(where, pieces, squares, gain, so_far, start, all_rows, after):
    tp = len(pieces)
    rows, width = pieces[0].shape
    place = start // rows
    vm = pl.BlockSpec((rows, width), lambda i, s: (0, 0))
    operands = [*pieces, *squares, gain]
    specs = (
        [vm] * tp
        + [pl.BlockSpec((8, rows), lambda i, s: (0, 0))] * tp
        + [pl.BlockSpec((1, tp * width), lambda i, s: (0, 0))]
    )
    aliases = {}
    if so_far is not None:
        aliases = {1 + len(operands): 0}
        operands.append(so_far)
        specs.append(pl.BlockSpec(memory_space=pl.ANY))
    operands += after
    specs += [pl.BlockSpec(TOKEN, lambda i, s: (0, 0))] * len(after)
    return pl.pallas_call(
        functools.partial(norm_kernel, tp, len(aliases) + len(after)),
        grid_spec=pltpu.PrefetchScalarGridSpec(
            num_scalar_prefetch=1,
            grid=(1,),
            in_specs=specs,
            out_specs=[
                pl.BlockSpec((rows, tp * width), lambda i, s: (place, 0)),
                pl.BlockSpec(TOKEN, lambda i, s: (0, 0)),
            ],
        ),
        out_shape=[
            jax.ShapeDtypeStruct((all_rows, tp * width), jnp.bfloat16),
            jax.ShapeDtypeStruct(TOKEN, jnp.float32),
        ],
        input_output_aliases=aliases,
        compiler_params=pltpu.CompilerParams(vmem_limit_bytes=VMEM),
        name="norm_chunk",
    )(where, *operands)


def shards(sub, tp, gate_pre, up_pre, down_weight, residual, signs, row_slot, norm_gain):
    rows = gate_pre.shape[0]
    width = residual.shape[1]
    place = lax.axis_index("sub").astype(jnp.int32)
    me = lax.axis_index("tp").astype(jnp.int32)
    where = jnp.stack([place, me])
    matrix = hadamard_signs()
    mine = jnp.take(residual, row_slot, axis=0, mode="clip")
    signs_own = lax.dynamic_slice_in_dim(signs, me * width, width, 0).reshape(1, width)
    gain = norm_gain.reshape(1, -1)

    def swap(value, d):
        return lax.ppermute(value, "tp", [(i, i ^ d) for i in range(tp)])

    sizes = row_chunks(rows, tp)
    starts = [sum(sizes[:c]) for c in range(len(sizes))]
    last = len(sizes) - 1
    gathered = []
    after = []
    for start, size in zip(starts, sizes):
        own, token = hidden_chunk(gate_pre, up_pre, start, size, after)
        gathered.append(lax.all_gather(own, "sub", axis=0, tiled=True))
        after = [token]
    stream = normed = None
    chunks, squares = [], []

    def exchange(local):
        along = local
        for d in range(1, sub):
            along = along + lax.ppermute(local, "sub", [(i, (i + d) % sub) for i in range(sub)])
        return [along] + [swap(along, d) for d in range(1, tp)]

    def normalise(group, totals, normed, after):
        for c in group:
            at = starts[c] - starts[group[0]]
            part = [t[:, at : at + sizes[c]] for t in totals]
            normed, token = norm_chunk(
                where, chunks[c], part, gain, normed, starts[c], rows, after
            )
            after = [token]
        return normed, after

    early = list(range(last))
    for c in range(len(sizes)):
        if c == last:
            totals = exchange(jnp.concatenate(squares, axis=1))
        arrived = chunks[c - 2][1:] if c >= 2 else []
        *sums, token = matmul_chunk(where, gathered[c], down_weight, tp, sub, after, arrived)
        after = [token]
        pieces = [sums[0]] + [swap(sums[d], d) for d in range(1, tp)]
        if c == last:
            normed, after = normalise(early, totals, normed, after)
        stream, chunk, local = stream_chunk(
            pieces, signs_own, matrix, mine, stream, starts[c], after
        )
        after = [local]
        chunks.append([chunk] + [swap(chunk, d) for d in range(1, tp)])
        squares.append(local)
    normed, _ = normalise([last], exchange(local), normed, [])
    return (stream, normed)


def solution(mesh):
    return jax.shard_map(
        functools.partial(shards, mesh.shape["sub"], mesh.shape["tp"]),
        mesh=mesh,
        in_specs=(
            P("groups", ("tp", "sub")),
            P("groups", ("tp", "sub")),
            P("tp", "sub"),
            P("groups", ("sub", "tp")),
            P("sub"),
            P("groups"),
            P("sub"),
        ),
        out_specs=(P("groups", ("sub", "tp")), P("groups", "sub")),
        check_vma=False,
    )
```

```python
import functools

import jax
import jax.numpy as jnp
import numpy as np
from jax import lax
from jax.experimental import pallas as pl
from jax.experimental.pallas import tpu as pltpu
from jax.sharding import PartitionSpec as P

D = 16384
H_SCALE = 0.08838834764831845
VMEM = 48 * 1024 * 1024
TOKEN = (8, 128)


def hadamard_signs():
    index = jnp.arange(128, dtype=jnp.int32)
    common = index[:, None] & index[None, :]
    parity = sum((common >> shift & 1 for shift in range(7)))
    return jnp.where(parity % 2 == 0, 1.0, -1.0).astype(jnp.bfloat16)


def row_groups(rows, tp, sub):
    if rows == 768 and tp == 4 and sub == 4:
        return [[256], [256], [128, 128]]
    return [[rows // 2], [rows // 2]]


def block_of(width, most):
    size = min(width, most)
    while width % size:
        size //= 2
    return size


def params():
    return pltpu.CompilerParams(vmem_limit_bytes=VMEM)


def anywhere():
    return pl.BlockSpec(memory_space=pl.ANY)


def token_spec():
    return pl.BlockSpec(TOKEN, lambda *_: (0, 0))


TOKEN_SHAPE = jax.ShapeDtypeStruct(TOKEN, jnp.float32)


def hidden_kernel(more, gate, up, *refs):
    out, token = refs[more:]
    value = gate[...].astype(jnp.float32)
    value = value / (1.0 + jnp.exp(-value)) * up[...].astype(jnp.float32)
    out[...] = value.astype(jnp.bfloat16)
    token[...] = jnp.zeros(TOKEN, jnp.float32)


def hidden_rows(gate, up, start, rows, after):
    columns = gate.shape[1]
    place = start // rows
    line = pl.BlockSpec((rows, columns), lambda i: (place, 0))
    return pl.pallas_call(
        functools.partial(hidden_kernel, len(after)),
        grid=(1,),
        in_specs=[line, line] + [token_spec()] * len(after),
        out_specs=[pl.BlockSpec((rows, columns), lambda i: (0, 0)), token_spec()],
        out_shape=[jax.ShapeDtypeStruct((rows, columns), jnp.bfloat16), TOKEN_SHAPE],
        compiler_params=params(),
        name="hidden_rows",
    )(gate, up, *after)


def stage_table(sub, stages):
    found = []
    for place in range(sub):
        entries, source = [], 0
        for d in stages:
            if d == 0:
                entries.append((source, place))
                source += 1
                continue
            if place >= d:
                entries.append((source, place - d))
            if place + d < sub:
                entries.append((source + 1, place + d))
            source += 2
        found.append(entries)
    most = max(len(entries) for entries in found)
    table = np.zeros((sub, 1 + 2 * most), np.int32)
    for place, entries in enumerate(found):
        table[place, 0] = len(entries)
        for p in range(most):
            if entries:
                source, piece = entries[min(p, len(entries) - 1)]
                table[place, 1 + p] = source
                table[place, 1 + most + p] = piece
    return table, most


def matmul_kernel(plan, info, *refs):
    most, per, block, tp, spans, sources, prior_at, final, skip, threads = plan
    parts = len(spans)
    count = sources * parts
    inputs = [refs[s * parts : (s + 1) * parts] for s in range(sources)]
    weights = refs[count : count + tp]
    at = count + tp
    prior = refs[at] if prior_at is not None else None
    at += (prior_at is not None) + skip
    outs = refs[at : at + 1 + final]
    token = refs[at + 1 + final]
    scratch = refs[at + 2 + final + threads :]
    held, total, sems = scratch[:3]
    step = pl.program_id(0)
    me = info[0]
    pieces = info[1]
    active = step < pieces * per

    @pl.when(step == 0)
    def _():
        for p in range(most):
            for s in range(sources):

                @pl.when((p < pieces) & (info[2 + p] == s))
                def _():
                    for n, (first, size) in enumerate(spans):
                        for q in range(per):
                            pltpu.make_async_copy(
                                inputs[s][n].at[:, q * block : (q + 1) * block],
                                held.at[p * per + q, first : first + size],
                                sems.at[p * per + q, n],
                            ).start()

        if prior is not None:
            pltpu.make_async_copy(
                prior.at[:, prior_at : prior_at + total.shape[1]], scratch[3], scratch[4].at[0]
            ).start()

        @pl.when(pieces == 0)
        def _():
            total[...] = jnp.zeros_like(total)

    @pl.when(active)
    def _():
        for n, (first, size) in enumerate(spans):
            pltpu.make_async_copy(
                inputs[0][n].at[:, 0:block], held.at[step, first : first + size], sems.at[step, n]
            ).wait()
        value = held[step]
        for t in range(tp):
            product = jnp.dot(value, weights[t][...], preferred_element_type=jnp.float32)

            @pl.when(step == 0)
            def _():
                total[t] = product

            @pl.when(step != 0)
            def _():
                total[t] += product

    @pl.when(step == most * per - 1)
    def _():
        if prior is not None:
            pltpu.make_async_copy(
                prior.at[:, prior_at : prior_at + total.shape[1]], scratch[3], scratch[4].at[0]
            ).wait()

        def result(t):
            value = total[t]
            return value if prior is None else value + scratch[3][t]

        if final:
            keep, send = outs
            for k in range(tp // 2):
                keep[k] = result(me ^ (2 * k))
                send[k] = result(me ^ (2 * k + 1)).astype(jnp.bfloat16)
        else:
            for t in range(tp):
                outs[0][t] = result(t)
        token[...] = jnp.zeros(TOKEN, jnp.float32)


def matmul_stage(place, me, stages, sub, tp, inputs, weight, prior, prior_at, final, after, wait, thread):
    sizes = [part.shape[0] for part in inputs[0]]
    rows = sum(sizes)
    spans = [(sum(sizes[:n]), size) for n, size in enumerate(sizes)]
    depth = inputs[0][0].shape[1]
    block = block_of(depth, 512)
    per = depth // block
    columns = weight.shape[1]
    width = columns // tp
    table, most = stage_table(sub, stages)
    info = jnp.concatenate([me[None], jnp.asarray(table)[place]])
    flat = [part for source in inputs for part in source]

    def row_block(j, s):
        last = jnp.maximum(s[1] * per - 1, 0)
        j = jnp.minimum(j, last)
        return s[2 + most + j // per] * per + j % per

    operands = [*flat] + [weight] * tp
    specs = [anywhere()] * len(flat) + [
        pl.BlockSpec((block, width), lambda j, s, t=t: (row_block(j, s), t)) for t in range(tp)
    ]
    scratch = [
        pltpu.VMEM((most * per, rows, block), jnp.bfloat16),
        pltpu.VMEM((tp, rows, width), jnp.float32),
        pltpu.SemaphoreType.DMA((most * per, len(sizes))),
    ]
    if prior is not None:
        operands.append(prior)
        specs.append(anywhere())
        scratch += [pltpu.VMEM((tp, rows, width), jnp.float32), pltpu.SemaphoreType.DMA((1,))]
    operands += [*after, *wait]
    specs += [token_spec()] * len(after) + [anywhere()] * len(wait)
    whole = lambda n: pl.BlockSpec((n, rows, width), lambda j, s: (0, 0, 0))
    if final:
        out_specs = [whole(tp // 2)] * 2
        out_shape = [
            jax.ShapeDtypeStruct((tp // 2, rows, width), jnp.float32),
            jax.ShapeDtypeStruct((tp // 2, rows, width), jnp.bfloat16),
        ]
    else:
        out_specs = [whole(tp)]
        out_shape = [jax.ShapeDtypeStruct((tp, rows, width), jnp.float32)]
    out_specs.append(token_spec())
    out_shape.append(TOKEN_SHAPE)
    aliases = {}
    for index in thread:
        aliases[1 + index] = len(out_shape)
        out_specs.append(anywhere())
        out_shape.append(jax.ShapeDtypeStruct(flat[index].shape, flat[index].dtype))
    plan = (
        most,
        per,
        block,
        tp,
        spans,
        len(inputs),
        None if prior is None else prior_at,
        final,
        len(after) + len(wait),
        len(thread),
    )
    return pl.pallas_call(
        functools.partial(matmul_kernel, plan),
        grid_spec=pltpu.PrefetchScalarGridSpec(
            num_scalar_prefetch=1,
            grid=(most * per,),
            in_specs=specs,
            out_specs=out_specs,
            scratch_shapes=scratch,
        ),
        out_shape=out_shape,
        input_output_aliases=aliases,
        compiler_params=params(),
        cost_estimate=pl.CostEstimate(
            flops=2 * rows * most * depth * columns,
            bytes_accessed=2 * most * depth * columns,
            transcendentals=0,
        ),
        name="matmul_stage",
    )(info, *operands)


def halve_kernel(more, keep, got, *refs):
    outs = refs[more:]
    send, token = outs[0], outs[-1]
    half = send.shape[0]
    for k in range(half):
        value = keep[2 * k + 1] + got[2 * k + 1].astype(jnp.float32)
        send[k] = value.astype(jnp.bfloat16)
        if len(outs) == 3:
            outs[1][k] = keep[2 * k] + got[2 * k].astype(jnp.float32)
    token[...] = jnp.zeros(TOKEN, jnp.float32)


def halve(keep, got, both, after):
    count, rows, width = keep.shape
    half = count // 2
    spec = lambda n: pl.BlockSpec((n, rows, width), lambda i: (0, 0, 0))
    out_shape = [jax.ShapeDtypeStruct((half, rows, width), jnp.bfloat16)]
    if both:
        out_shape.append(jax.ShapeDtypeStruct((half, rows, width), jnp.float32))
    return pl.pallas_call(
        functools.partial(halve_kernel, len(after)),
        grid=(1,),
        in_specs=[spec(count)] * 2 + [token_spec()] * len(after),
        out_specs=[spec(half)] * (1 + both) + [token_spec()],
        out_shape=out_shape + [TOKEN_SHAPE],
        compiler_params=params(),
        name="halve",
    )(keep, got, *after)


def stream_kernel(terms, more, *refs):
    signs, matrix, residual = refs[terms : terms + 3]
    stream, chunk, squares = refs[terms + 3 + more :]
    total = refs[0][...]
    for other in refs[1:terms]:
        total = total + other[...].astype(jnp.float32)
    total = total * signs[...].astype(jnp.float32)
    rows, width = total.shape
    turn = matrix[...]
    for b in range(width // 128):
        piece = total[:, b * 128 : (b + 1) * 128]
        rotated = jnp.zeros((rows, 128), jnp.float32)
        for _ in range(3):
            part = piece.astype(jnp.bfloat16)
            rotated = rotated + jnp.dot(part, turn, preferred_element_type=jnp.float32)
            piece = piece - part.astype(jnp.float32)
        kept = residual[:, b * 128 : (b + 1) * 128].astype(jnp.float32)
        value = (kept + rotated * H_SCALE).astype(jnp.bfloat16)
        stream[:, b * 128 : (b + 1) * 128] = value
        chunk[:, b * 128 : (b + 1) * 128] = value
    local = chunk[...].astype(jnp.float32)
    squares[...] = lax.dot_general(
        jnp.ones((8, width), jnp.float32),
        local * local,
        (((1,), (1,)), ((), ())),
        precision=lax.Precision.HIGHEST,
        preferred_element_type=jnp.float32,
    )


def stream_rows(terms, signs, matrix, residual, so_far, start, after):
    _, rows, width = terms[0].shape
    place = start // rows
    line = pl.BlockSpec((rows, width), lambda i: (place, 0))
    operands = [*terms, signs, matrix, residual]
    specs = [pl.BlockSpec((None, rows, width), lambda i: (0, 0, 0))] * len(terms) + [
        pl.BlockSpec((1, width), lambda i: (0, 0)),
        pl.BlockSpec((128, 128), lambda i: (0, 0)),
        line,
    ]
    aliases = {}
    if so_far is not None:
        aliases = {len(operands): 0}
        operands.append(so_far)
        specs.append(anywhere())
    operands += after
    specs += [token_spec()] * len(after)
    return pl.pallas_call(
        functools.partial(stream_kernel, len(terms), len(aliases) + len(after)),
        grid=(1,),
        in_specs=specs,
        out_specs=[
            line,
            pl.BlockSpec((rows, width), lambda i: (0, 0)),
            pl.BlockSpec((8, rows), lambda i: (0, 0)),
        ],
        out_shape=[
            jax.ShapeDtypeStruct(residual.shape, jnp.bfloat16),
            jax.ShapeDtypeStruct((rows, width), jnp.bfloat16),
            jax.ShapeDtypeStruct((8, rows), jnp.float32),
        ],
        input_output_aliases=aliases,
        compiler_params=params(),
        name="stream_rows",
    )(*operands)


def norm_kernel(places, more, info, *refs):
    tp = len(places)
    pieces = refs[:tp]
    first, second, gain = refs[tp : tp + 3]
    out, token = refs[tp + 3 + more :]
    token[...] = jnp.zeros(TOKEN, jnp.float32)
    inverse = lax.rsqrt((first[...] + second[...]) / D + 1e-05)
    scale = jnp.transpose(inverse)[:, 0:1]
    width = pieces[0].shape[1]
    for e, piece in zip(places, pieces):
        at = pl.ds(pl.multiple_of((info[0] ^ e) * width, width), width)
        value = piece[...].astype(jnp.float32) * scale * gain[:, at]
        out[:, at] = value.astype(jnp.bfloat16)


def norm_rows(me, pieces, squares, column, gain, so_far, start, all_rows, after):
    tp = len(pieces)
    rows, width = pieces[0][1].shape
    place = start // rows
    small = pl.BlockSpec((8, rows), lambda i, s: (0, column // rows))
    operands = [piece for _, piece in pieces] + [*squares, gain]
    specs = (
        [pl.BlockSpec((rows, width), lambda i, s: (0, 0))] * tp
        + [small] * 2
        + [pl.BlockSpec((1, tp * width), lambda i, s: (0, 0))]
    )
    aliases = {}
    if so_far is not None:
        aliases = {1 + len(operands): 0}
        operands.append(so_far)
        specs.append(anywhere())
    operands += after
    specs += [token_spec()] * len(after)
    return pl.pallas_call(
        functools.partial(norm_kernel, [e for e, _ in pieces], len(aliases) + len(after)),
        grid_spec=pltpu.PrefetchScalarGridSpec(
            num_scalar_prefetch=1,
            grid=(1,),
            in_specs=specs,
            out_specs=[
                pl.BlockSpec((rows, tp * width), lambda i, s: (place, 0)),
                token_spec(),
            ],
        ),
        out_shape=[jax.ShapeDtypeStruct((all_rows, tp * width), jnp.bfloat16), TOKEN_SHAPE],
        input_output_aliases=aliases,
        compiler_params=params(),
        name="norm_rows",
    )(me[None], *operands)


def shards(sub, tp, gate_pre, up_pre, down_weight, residual, signs, row_slot, norm_gain):
    rows = gate_pre.shape[0]
    width = residual.shape[1]
    place = lax.axis_index("sub").astype(jnp.int32)
    me = lax.axis_index("tp").astype(jnp.int32)
    matrix = hadamard_signs()
    mine = jnp.take(residual, row_slot, axis=0, mode="clip")
    signs_own = lax.dynamic_slice_in_dim(signs, me * width, width, 0).reshape(1, width)
    gain = norm_gain.reshape(1, -1)
    bits = [1 << b for b in range(tp.bit_length() - 1)]

    groups = row_groups(rows, tp, sub)
    sizes = [size for group in groups for size in group]
    units = len(sizes)
    starts = [sum(sizes[:u]) for u in range(units)]
    members, u = [], 0
    for group in groups:
        members.append(list(range(u, u + len(group))))
        u += len(group)
    last = len(groups) - 1

    def swap(value, d):
        return lax.ppermute(value, "tp", [(i, i ^ d) for i in range(tp)])

    def onward(pair, d):
        up = lax.ppermute(pair[0], "sub", [(i, i + 1) for i in range(d - 1, sub - 1)])
        down = lax.ppermute(pair[1], "sub", [(i, i - 1) for i in range(1, sub - d + 1)])
        return [up, down]

    own = [None] * units
    came = {}
    sums = [None] * len(groups)

    def make(g, after):
        for u in members[g]:
            own[u], token = hidden_rows(gate_pre, up_pre, starts[u], sizes[u], after)
            after = [token]
            came[1, u] = onward([own[u], own[u]], 1)
        return after

    def forward(g, d):
        for u in members[g]:
            if (d + 1, u) not in came and d + 1 < sub:
                came[d + 1, u] = onward(came[d, u], d + 1)

    def multiply(g, us, stages, final, after, wait, thread):
        inputs, handed = [], []
        for d in stages:
            if d == 0:
                inputs.append([own[u] for u in us])
                continue
            for side in range(2):
                if d == thread:
                    handed += [(d, u, side, len(inputs) * len(us) + n) for n, u in enumerate(us)]
                inputs.append([came[d, u][side] for u in us])
        outs = matmul_stage(
            place,
            me,
            stages,
            sub,
            tp,
            inputs,
            down_weight,
            sums[g],
            starts[us[0]] - starts[members[g][0]],
            final,
            after,
            wait,
            [index for _, _, _, index in handed],
        )
        for (d, u, side, _), value in zip(handed, outs[len(outs) - len(handed) :]):
            came[d, u][side] = value
        if final:
            return outs[0], outs[1], [outs[2]]
        sums[g] = outs[0]
        return [outs[1]]

    terms, held = {}, {}
    streams = [None]
    pieces, squares = {}, {}

    def reduce_first(u, keep, send, after):
        got = swap(send, bits[0])
        for level, bit in enumerate(bits[1:]):
            both = keep.shape[0] > 2
            outs = halve(keep, got, both, after)
            after = [outs[-1]]
            if both:
                keep, got = outs[1], swap(outs[0], bit)
            else:
                terms[u] = [keep, got, swap(outs[0], bit)]
        return after

    def finish(u, after):
        streams[0], chunk, squares[u] = stream_rows(
            terms[u], signs_own, matrix, mine, streams[0], starts[u], after
        )
        found = [(0, chunk)]
        for bit in reversed(bits):
            found += [(e | bit, swap(value, bit)) for e, value in found]
        pieces[u] = found
        return [squares[u]]

    def exchange(local):
        along = local
        for d in range(1, sub):
            along = along + lax.ppermute(local, "sub", [(i, (i + d) % sub) for i in range(sub)])
        for bit in reversed(bits[1:]):
            along = along + swap(along, bit)
        return [along, swap(along, bits[0])]

    normed = [None]

    def normalise(us, totals, after):
        for u in us:
            normed[0], token = norm_rows(
                me,
                pieces[u],
                totals,
                starts[u] - starts[us[0]],
                gain,
                normed[0],
                starts[u],
                rows,
                after,
            )
            after = [token]
        return after

    early, middle, late = [0, 1], list(range(2, sub - 1)), [sub - 1]

    token = make(0, [])
    token = make(1, token)
    forward(0, 1)
    for g in range(len(groups)):
        token = multiply(g, members[g], early, False, token, [], 1 if g > 0 else None)
        if g + 2 < len(groups):
            token = make(g + 2, token)
        forward(g, 1)
        for d in middle[:-1]:
            forward(g, d)
        if g >= 1:
            token = multiply(g - 1, members[g - 1], middle, False, token, [], middle[-1])
            forward(g - 1, middle[-1])
    forward(last, middle[-1])
    for g in range(len(groups)):
        for u in members[g]:
            keep, send, token = multiply(g, [u], late, True, token, [], None)
            token = reduce_first(u, keep, send, token)
            if g == 0:
                token = multiply(last, members[last], middle, False, token, [], None)
            if u == units - 1:
                before = list(range(units - 1))
                totals = exchange(jnp.concatenate([squares[b] for b in before], axis=1))
                token = normalise(before, totals, token)
            token = finish(u, token)
    normalise([units - 1], exchange(squares[units - 1]), [])
    return (streams[0], normed[0])


def solution(mesh):
    return jax.shard_map(
        functools.partial(shards, mesh.shape["sub"], mesh.shape["tp"]),
        mesh=mesh,
        in_specs=(
            P("groups", ("tp", "sub")),
            P("groups", ("tp", "sub")),
            P("tp", "sub"),
            P("groups", ("sub", "tp")),
            P("sub"),
            P("groups"),
            P("sub"),
        ),
        out_specs=(P("groups", ("sub", "tp")), P("groups", "sub")),
        check_vma=False,
    )
```

```python
import functools

import jax
import jax.numpy as jnp
import numpy as np
from jax import lax
from jax.experimental import pallas as pl
from jax.experimental.pallas import tpu as pltpu
from jax.sharding import PartitionSpec as P

D = 16384
H_SCALE = 0.08838834764831845
VMEM = 48 * 1024 * 1024
TOKEN = (8, 128)


def hadamard_signs():
    index = jnp.arange(128, dtype=jnp.int32)
    common = index[:, None] & index[None, :]
    parity = sum((common >> shift & 1 for shift in range(7)))
    return jnp.where(parity % 2 == 0, 1.0, -1.0).astype(jnp.bfloat16)


def row_units(rows):
    return [rows // 3, rows // 3, rows // 3]


def block_of(width, most):
    size = min(width, most)
    while width % size:
        size //= 2
    return size


def lanes(rows):
    return -(-rows // 128) * 128


def params():
    return pltpu.CompilerParams(vmem_limit_bytes=VMEM)


def anywhere():
    return pl.BlockSpec(memory_space=pl.ANY)


def token_spec():
    return pl.BlockSpec(TOKEN, lambda *_: (0, 0))


TOKEN_SHAPE = jax.ShapeDtypeStruct(TOKEN, jnp.float32)


def hidden_kernel(more, gate, up, *refs):
    out, token = refs[more:]
    value = gate[...].astype(jnp.float32)
    value = value / (1.0 + jnp.exp(-value)) * up[...].astype(jnp.float32)
    out[...] = value.astype(jnp.bfloat16)
    token[...] = jnp.zeros(TOKEN, jnp.float32)


def hidden_rows(gate, up, start, rows, after):
    columns = gate.shape[1]
    place = start // rows
    line = pl.BlockSpec((rows, columns), lambda i: (place, 0))
    return pl.pallas_call(
        functools.partial(hidden_kernel, len(after)),
        grid=(1,),
        in_specs=[line, line] + [token_spec()] * len(after),
        out_specs=[pl.BlockSpec((rows, columns), lambda i: (0, 0)), token_spec()],
        out_shape=[jax.ShapeDtypeStruct((rows, columns), jnp.bfloat16), TOKEN_SHAPE],
        compiler_params=params(),
        cost_estimate=pl.CostEstimate(flops=1, bytes_accessed=1, transcendentals=0),
        name="hidden_rows",
    )(gate, up, *after)


def stage_table(sub, stages):
    found = []
    for place in range(sub):
        entries, source = [], 0
        for d in stages:
            if d == 0:
                entries.append((source, place))
                source += 1
                continue
            if place >= d:
                entries.append((source, place - d))
            if place + d < sub:
                entries.append((source + 1, place + d))
            source += 2
        found.append(entries)
    most = max(len(entries) for entries in found)
    table = np.zeros((sub, 1 + 2 * most), np.int32)
    for place, entries in enumerate(found):
        table[place, 0] = len(entries)
        for p in range(most):
            if entries:
                source, piece = entries[min(p, len(entries) - 1)]
                table[place, 1 + p] = source
                table[place, 1 + most + p] = piece
    return table, most


def matmul_kernel(plan, info, *refs):
    most, per, block, tp, spans, sources, gathered, prior_at, final, skip = plan
    parts = len(spans)
    count = 1 if gathered else sources * parts
    inputs = [refs[s * parts : (s + 1) * parts] for s in range(sources)]
    if gathered:
        size = spans[0][1]
        inputs = [[refs[0].at[s * size : (s + 1) * size]] for s in range(sources)]
    weights = refs[count : count + tp]
    at = count + tp
    prior = refs[at] if prior_at is not None else None
    at += (prior_at is not None) + skip
    number = 1 + tp // 2 if final else 1
    outs = refs[at : at + number]
    token = refs[at + number]
    scratch = refs[at + number + 1 :]
    held, total, sems = scratch[:3]
    step = pl.program_id(0)
    me = info[0]
    pieces = info[1]
    active = step < pieces * per

    @pl.when(step == 0)
    def _():
        for p in range(most):
            for s in range(sources):

                @pl.when((p < pieces) & (info[2 + p] == s))
                def _():
                    for n, (first, size) in enumerate(spans):
                        for q in range(per):
                            pltpu.make_async_copy(
                                inputs[s][n].at[:, q * block : (q + 1) * block],
                                held.at[p * per + q, first : first + size],
                                sems.at[p * per + q, n],
                            ).start()

        if prior is not None:
            pltpu.make_async_copy(
                prior.at[:, prior_at : prior_at + total.shape[1]], scratch[3], scratch[4].at[0]
            ).start()

        @pl.when(pieces == 0)
        def _():
            total[...] = jnp.zeros_like(total)

    @pl.when(active)
    def _():
        for n, (first, size) in enumerate(spans):
            pltpu.make_async_copy(
                inputs[0][n].at[:, 0:block], held.at[step, first : first + size], sems.at[step, n]
            ).wait()
        value = held[step]
        for t in range(tp):
            product = jnp.dot(value, weights[t][...], preferred_element_type=jnp.float32)

            @pl.when(step == 0)
            def _():
                total[t] = product

            @pl.when(step != 0)
            def _():
                total[t] += product

    @pl.when(step == most * per - 1)
    def _():
        if prior is not None:
            pltpu.make_async_copy(
                prior.at[:, prior_at : prior_at + total.shape[1]], scratch[3], scratch[4].at[0]
            ).wait()

        def result(t):
            value = total[t]
            return value if prior is None else value + scratch[3][t]

        if final:
            for k in range(tp // 2):
                outs[0][k] = result(me ^ (2 * k))
                outs[1 + k][...] = result(me ^ (2 * k + 1)).astype(jnp.bfloat16)
        else:
            if prior is not None:
                total[...] += scratch[3][...]
            copy = pltpu.make_async_copy(total, outs[0], scratch[-1].at[0])
            copy.start()
            copy.wait()
        token[...] = jnp.zeros(TOKEN, jnp.float32)


def matmul_stage(place, me, stages, sub, tp, inputs, weight, prior, prior_at, final, after):
    gathered = not isinstance(inputs, list)
    if gathered:
        flat = [inputs]
        sizes = [inputs.shape[0] // sub]
    else:
        flat = [part for source in inputs for part in source]
        sizes = [part.shape[0] for part in inputs[0]]
    rows = sum(sizes)
    spans = [(sum(sizes[:n]), size) for n, size in enumerate(sizes)]
    depth = flat[0].shape[1]
    block = block_of(depth, 512)
    per = depth // block
    columns = weight.shape[1]
    width = columns // tp
    if gathered:
        most = sub
        info = jnp.concatenate([me[None], jnp.asarray([sub, *range(sub), *range(sub)], jnp.int32)])
    else:
        table, most = stage_table(sub, stages)
        info = jnp.concatenate([me[None], jnp.asarray(table)[place]])

    def row_block(j, s):
        last = jnp.maximum(s[1] * per - 1, 0)
        j = jnp.minimum(j, last)
        return s[2 + most + j // per] * per + j % per

    operands = [*flat] + [weight] * tp
    specs = [anywhere()] * len(flat) + [
        pl.BlockSpec((block, width), lambda j, s, t=t: (row_block(j, s), t)) for t in range(tp)
    ]
    scratch = [
        pltpu.VMEM((most * per, rows, block), jnp.bfloat16),
        pltpu.VMEM((tp, rows, width), jnp.float32),
        pltpu.SemaphoreType.DMA((most * per, len(sizes))),
    ]
    if prior is not None:
        operands.append(prior)
        specs.append(anywhere())
        scratch += [pltpu.VMEM((tp, rows, width), jnp.float32), pltpu.SemaphoreType.DMA((1,))]
    if not final:
        scratch.append(pltpu.SemaphoreType.DMA((1,)))
    operands += after
    specs += [token_spec()] * len(after)
    if final:
        out_specs = [pl.BlockSpec((tp // 2, rows, width), lambda j, s: (0, 0, 0))]
        out_specs += [pl.BlockSpec((rows, width), lambda j, s: (0, 0))] * (tp // 2)
        out_shape = [jax.ShapeDtypeStruct((tp // 2, rows, width), jnp.float32)]
        out_shape += [jax.ShapeDtypeStruct((rows, width), jnp.bfloat16)] * (tp // 2)
    else:
        out_specs = [anywhere()]
        out_shape = [jax.ShapeDtypeStruct((tp, rows, width), jnp.float32)]
    out_specs.append(token_spec())
    out_shape.append(TOKEN_SHAPE)
    plan = (
        most,
        per,
        block,
        tp,
        spans,
        sub if gathered else len(inputs),
        gathered,
        None if prior is None else prior_at,
        final,
        len(after),
    )
    return pl.pallas_call(
        functools.partial(matmul_kernel, plan),
        grid_spec=pltpu.PrefetchScalarGridSpec(
            num_scalar_prefetch=1,
            grid=(most * per,),
            in_specs=specs,
            out_specs=out_specs,
            scratch_shapes=scratch,
        ),
        out_shape=out_shape,
        compiler_params=params(),
        cost_estimate=pl.CostEstimate(flops=1, bytes_accessed=1, transcendentals=0),
        name="matmul_stage",
    )(info, *operands)


def gate_kernel(count, *refs):
    refs[-1][...] = jnp.zeros(TOKEN, jnp.float32)


def gate(values, after):
    count = len(values)
    outs = pl.pallas_call(
        functools.partial(gate_kernel, count),
        in_specs=[anywhere()] * count + [pl.BlockSpec(TOKEN, lambda: (0, 0))] * len(after),
        out_specs=[anywhere()] * count + [pl.BlockSpec(TOKEN, lambda: (0, 0))],
        out_shape=[jax.ShapeDtypeStruct(v.shape, v.dtype) for v in values] + [TOKEN_SHAPE],
        input_output_aliases={n: n for n in range(count)},
        compiler_params=params(),
        cost_estimate=pl.CostEstimate(flops=1, bytes_accessed=1, transcendentals=0),
        name="gate",
    )(*values, *after)
    return list(outs[:count]), [outs[count]]


def halve_kernel(cut, more, keep, *refs):
    half = keep.shape[0] // 2
    got = refs[: 2 * half]
    *outs, token = refs[2 * half + more :]
    size = keep.shape[1] // cut
    for k in range(half):
        value = (keep[2 * k + 1] + got[2 * k + 1][...].astype(jnp.float32)).astype(jnp.bfloat16)
        for n in range(cut):
            outs[k * cut + n][...] = value[n * size : (n + 1) * size]
        if half > 1:
            outs[half * cut][k] = keep[2 * k] + got[2 * k][...].astype(jnp.float32)
    token[...] = jnp.zeros(TOKEN, jnp.float32)


def halve(keep, got, cut, after):
    count, rows, width = keep.shape
    half = count // 2
    stack = lambda n: pl.BlockSpec((n, rows, width), lambda i: (0, 0, 0))
    flat = lambda n: pl.BlockSpec((n, width), lambda i: (0, 0))
    size = rows // cut
    out_specs = [flat(size)] * (half * cut)
    out_shape = [jax.ShapeDtypeStruct((size, width), jnp.bfloat16)] * (half * cut)
    if half > 1:
        out_specs.append(stack(half))
        out_shape.append(jax.ShapeDtypeStruct((half, rows, width), jnp.float32))
    outs = pl.pallas_call(
        functools.partial(halve_kernel, cut, len(after)),
        grid=(1,),
        in_specs=[stack(count)] + [flat(rows)] * count + [token_spec()] * len(after),
        out_specs=out_specs + [token_spec()],
        out_shape=out_shape + [TOKEN_SHAPE],
        compiler_params=params(),
        cost_estimate=pl.CostEstimate(flops=1, bytes_accessed=1, transcendentals=0),
        name="halve",
    )(keep, *got, *after)
    return outs[: half * cut], outs[half * cut] if half > 1 else None, outs[-1]


def stream_kernel(cut, more, *refs):
    keep, first, *last = refs[: 2 + cut]
    signs, matrix, residual = refs[2 + cut : 5 + cut]
    stream, chunk, squares = refs[5 + cut + more :]
    last = jnp.concatenate([part[...].astype(jnp.float32) for part in last], axis=0)
    total = keep[...] + first[...].astype(jnp.float32) + last
    total = total * signs[...].astype(jnp.float32)
    rows, width = total.shape
    turn = matrix[...]
    for b in range(width // 128):
        piece = total[:, b * 128 : (b + 1) * 128]
        rotated = jnp.zeros((rows, 128), jnp.float32)
        for _ in range(3):
            part = piece.astype(jnp.bfloat16)
            rotated = rotated + jnp.dot(part, turn, preferred_element_type=jnp.float32)
            piece = piece - part.astype(jnp.float32)
        kept = residual[:, b * 128 : (b + 1) * 128].astype(jnp.float32)
        value = (kept + rotated * H_SCALE).astype(jnp.bfloat16)
        stream[:, b * 128 : (b + 1) * 128] = value
        chunk[:, b * 128 : (b + 1) * 128] = value
    local = chunk[...].astype(jnp.float32)
    squares[...] = jnp.zeros_like(squares)
    squares[:, 0:rows] = lax.dot_general(
        jnp.ones((8, width), jnp.float32),
        local * local,
        (((1,), (1,)), ((), ())),
        precision=lax.Precision.HIGHEST,
        preferred_element_type=jnp.float32,
    )


def stream_rows(terms, signs, matrix, residual, so_far, start, after):
    keep, first, last = terms
    _, rows, width = keep.shape
    cut = len(last)
    place = start // rows
    line = pl.BlockSpec((rows, width), lambda i: (place, 0))
    flat = lambda n: pl.BlockSpec((n, width), lambda i: (0, 0))
    operands = [keep, first, *last, signs, matrix, residual]
    specs = [pl.BlockSpec((None, rows, width), lambda i: (0, 0, 0)), flat(rows)]
    specs += [flat(rows // cut)] * cut
    specs += [
        pl.BlockSpec((1, width), lambda i: (0, 0)),
        pl.BlockSpec((128, 128), lambda i: (0, 0)),
        line,
    ]
    aliases = {}
    if so_far is not None:
        aliases = {len(operands): 0}
        operands.append(so_far)
        specs.append(anywhere())
    operands += after
    specs += [token_spec()] * len(after)
    return pl.pallas_call(
        functools.partial(stream_kernel, cut, len(aliases) + len(after)),
        grid=(1,),
        in_specs=specs,
        out_specs=[
            line,
            pl.BlockSpec((rows, width), lambda i: (0, 0)),
            pl.BlockSpec((8, lanes(rows)), lambda i: (0, 0)),
        ],
        out_shape=[
            jax.ShapeDtypeStruct(residual.shape, jnp.bfloat16),
            jax.ShapeDtypeStruct((rows, width), jnp.bfloat16),
            jax.ShapeDtypeStruct((8, lanes(rows)), jnp.float32),
        ],
        input_output_aliases=aliases,
        compiler_params=params(),
        cost_estimate=pl.CostEstimate(flops=1, bytes_accessed=1, transcendentals=0),
        name="stream_rows",
    )(*operands)


def norm_kernel(places, more, info, *refs):
    tp = len(places)
    pieces = refs[:tp]
    first, second, gain = refs[tp : tp + 3]
    out, token = refs[tp + 3 + more :]
    token[...] = jnp.zeros(TOKEN, jnp.float32)
    inverse = lax.rsqrt((first[...] + second[...]) / D + 1e-05)
    rows, width = pieces[0].shape
    scale = jnp.transpose(inverse)[0:rows, 0:1]
    for e, piece in zip(places, pieces):
        at = pl.ds(pl.multiple_of((info[0] ^ e) * width, width), width)
        value = piece[...].astype(jnp.float32) * scale * gain[:, at]
        out[:, at] = value.astype(jnp.bfloat16)


def norm_rows(me, pieces, squares, column, gain, so_far, start, all_rows, after):
    tp = len(pieces)
    rows, width = pieces[0][1].shape
    place = start // rows
    small = pl.BlockSpec((8, lanes(rows)), lambda i, s: (0, column))
    operands = [piece for _, piece in pieces] + [*squares, gain]
    specs = (
        [pl.BlockSpec((rows, width), lambda i, s: (0, 0))] * tp
        + [small] * 2
        + [pl.BlockSpec((1, tp * width), lambda i, s: (0, 0))]
    )
    aliases = {}
    if so_far is not None:
        aliases = {1 + len(operands): 0}
        operands.append(so_far)
        specs.append(anywhere())
    operands += after
    specs += [token_spec()] * len(after)
    return pl.pallas_call(
        functools.partial(norm_kernel, [e for e, _ in pieces], len(aliases) + len(after)),
        grid_spec=pltpu.PrefetchScalarGridSpec(
            num_scalar_prefetch=1,
            grid=(1,),
            in_specs=specs,
            out_specs=[
                pl.BlockSpec((rows, tp * width), lambda i, s: (place, 0)),
                token_spec(),
            ],
        ),
        out_shape=[jax.ShapeDtypeStruct((all_rows, tp * width), jnp.bfloat16), TOKEN_SHAPE],
        input_output_aliases=aliases,
        compiler_params=params(),
        cost_estimate=pl.CostEstimate(flops=1, bytes_accessed=1, transcendentals=0),
        name="norm_rows",
    )(me[None], *operands)


def shards(sub, tp, gate_pre, up_pre, down_weight, residual, signs, row_slot, norm_gain):
    rows = gate_pre.shape[0]
    width = residual.shape[1]
    place = lax.axis_index("sub").astype(jnp.int32)
    me = lax.axis_index("tp").astype(jnp.int32)
    matrix = hadamard_signs()
    mine = jnp.take(residual, row_slot, axis=0, mode="clip")
    signs_own = lax.dynamic_slice_in_dim(signs, me * width, width, 0).reshape(1, width)
    gain = norm_gain.reshape(1, -1)
    bits = [1 << b for b in range(tp.bit_length() - 1)]

    sizes = row_units(rows)
    starts = [sum(sizes[:u]) for u in range(len(sizes))]

    def swap(value, d):
        return lax.ppermute(value, "tp", [(i, i ^ d) for i in range(tp)])

    def onward(pair, d):
        up = lax.ppermute(pair[0], "sub", [(i, i + 1) for i in range(d - 1, sub - 1)])
        down = lax.ppermute(pair[1], "sub", [(i, i - 1) for i in range(1, sub - d + 1)])
        return [up, down]

    def matmul(stages, inputs, prior, start, final, after):
        return matmul_stage(
            place, me, stages, sub, tp, inputs, down_weight, prior, start, final, after
        )

    terms, held = {}, {}
    streams = [None]
    pieces, squares = {}, {}

    def begin_sums(u, keep, *send):
        terms[u] = [keep, [swap(value, bits[0]) for value in send]]

    def halve_sums(u, after):
        keep, got = terms[u]
        for bit in bits[1:]:
            send, kept, token = halve(keep, got, 1, after)
            after = [token]
            arrived = [swap(value, bit) for value in send]
            if kept is None:
                terms[u] = [keep, got[0], arrived]
            else:
                keep, got = kept, arrived
        return after

    def finish(u, after):
        streams[0], chunk, squares[u] = stream_rows(
            terms[u], signs_own, matrix, mine, streams[0], starts[u], after
        )
        found = [(0, chunk)]
        for bit in reversed(bits):
            found += [(e | bit, swap(value, bit)) for e, value in found]
        pieces[u] = found
        return [squares[u]]

    def exchange(local):
        along = local
        for d in range(1, sub):
            along = along + lax.ppermute(local, "sub", [(i, (i + d) % sub) for i in range(sub)])
        for bit in reversed(bits[1:]):
            along = along + swap(along, bit)
        return [along, swap(along, bits[0])]

    normed = [None]

    def normalise(us, totals, after):
        for n, u in enumerate(us):
            normed[0], token = norm_rows(
                me,
                pieces[u],
                totals,
                n,
                gain,
                normed[0],
                starts[u],
                rows,
                after,
            )
            after = [token]
        return after

    early, middle, late = [0, 1], list(range(2, sub - 1)), [sub - 1]
    own = [None] * 3
    came = {}

    def make(u, after):
        own[u], token = hidden_rows(gate_pre, up_pre, starts[u], sizes[u], after)
        came[1, u] = onward([own[u], own[u]], 1)
        return [token]

    def pass_on(u, first, last):
        for d in range(first, last + 1):
            came[d, u] = onward(came[d - 1, u], d)

    def matmul(us, stages, prior, start, final, after):
        inputs = []
        for d in stages:
            if d == 0:
                inputs.append([own[u] for u in us])
            else:
                inputs += [[came[d, u][side] for u in us] for side in range(2)]
        return matmul_stage(
            place, me, stages, sub, tp, inputs, down_weight, prior, start, final, after
        )

    def hold(keys, after):
        values, token = gate([value for key in keys for value in came[key]], after)
        for n, key in enumerate(keys):
            came[key] = values[2 * n : 2 * n + 2]
        return token

    mid = middle[-1]
    token = make(0, [])
    token = make(1, token)
    token = hold([(1, 0)], token)
    pass_on(0, 2, mid)
    token = make(2, token)
    part, *token = matmul([0], early, None, 0, False, token)
    hold([(1, 1)], token)
    pass_on(1, 2, mid)
    token = hold([(mid, 0), (1, 2)], token)
    pass_on(0, sub - 1, sub - 1)
    parts, *token = matmul([1, 2], early, None, 0, False, token)
    token = hold([(1, 2), (mid, 1)], token)
    pass_on(2, 2, mid)
    *sums, token = matmul([0], middle + late, part, 0, True, token)
    begin_sums(0, *sums)
    token = hold([(mid, 1)], [token])
    pass_on(1, sub - 1, sub - 1)
    parts, *token = matmul([1, 2], middle, parts, 0, False, token)
    hold([(mid, 2)], token)
    pass_on(2, sub - 1, sub - 1)
    token = halve_sums(0, token)
    *sums, token = matmul([1], late, parts, 0, True, token)
    begin_sums(1, *sums)
    token = finish(0, [token])
    token = halve_sums(1, token)
    *sums, token = matmul([2], late, parts, sizes[1], True, token)
    begin_sums(2, *sums)
    token = finish(1, [token])
    token = halve_sums(2, token)
    totals = exchange(jnp.concatenate([squares[0], squares[1]], axis=1))
    token = normalise([0, 1], totals, token)
    finish(2, token)
    normalise([2], exchange(squares[2]), [])
    return (streams[0], normed[0])


def solution(mesh):
    return jax.shard_map(
        functools.partial(shards, mesh.shape["sub"], mesh.shape["tp"]),
        mesh=mesh,
        in_specs=(
            P("groups", ("tp", "sub")),
            P("groups", ("tp", "sub")),
            P("tp", "sub"),
            P("groups", ("sub", "tp")),
            P("sub"),
            P("groups"),
            P("sub"),
        ),
        out_specs=(P("groups", ("sub", "tp")), P("groups", "sub")),
        check_vma=False,
    )
```

```python
import functools

import jax
import jax.numpy as jnp
import numpy as np
from jax import lax
from jax.experimental import pallas as pl
from jax.experimental.pallas import tpu as pltpu
from jax.sharding import PartitionSpec as P

D = 16384
H_SCALE = 0.08838834764831845
VMEM = 48 * 1024 * 1024
TOKEN = (8, 128)


def hadamard_signs():
    index = jnp.arange(128, dtype=jnp.int32)
    common = index[:, None] & index[None, :]
    parity = sum((common >> shift & 1 for shift in range(7)))
    return jnp.where(parity % 2 == 0, 1.0, -1.0).astype(jnp.bfloat16)


def row_units(rows):
    return [rows // 3, rows // 3, rows // 3]


def lanes(rows):
    return -(-rows // 128) * 128


def params():
    return pltpu.CompilerParams(vmem_limit_bytes=VMEM)


def anywhere():
    return pl.BlockSpec(memory_space=pl.ANY)


def token_spec():
    return pl.BlockSpec(TOKEN, lambda *_: (0, 0))


TOKEN_SHAPE = jax.ShapeDtypeStruct(TOKEN, jnp.float32)


def hidden_kernel(more, gate, up, *refs):
    out, token = refs[more:]
    value = gate[...].astype(jnp.float32)
    value = value / (1.0 + jnp.exp(-value)) * up[...].astype(jnp.float32)
    out[...] = value.astype(jnp.bfloat16)
    token[...] = jnp.zeros(TOKEN, jnp.float32)


def hidden_rows(gate, up, start, rows, after):
    columns = gate.shape[1]
    place = start // rows
    line = pl.BlockSpec((rows, columns), lambda i: (place, 0))
    return pl.pallas_call(
        functools.partial(hidden_kernel, len(after)),
        grid=(1,),
        in_specs=[line, line] + [token_spec()] * len(after),
        out_specs=[pl.BlockSpec((rows, columns), lambda i: (0, 0)), token_spec()],
        out_shape=[jax.ShapeDtypeStruct((rows, columns), jnp.bfloat16), TOKEN_SHAPE],
        compiler_params=params(),
        cost_estimate=pl.CostEstimate(flops=1, bytes_accessed=1, transcendentals=0),
        name="hidden_rows",
    )(gate, up, *after)


def stage_table(sub, stages):
    found = []
    for place in range(sub):
        entries, source = [], 0
        for d in stages:
            if d == 0:
                entries.append((source, place))
                source += 1
                continue
            if place >= d:
                entries.append((source, place - d))
            if place + d < sub:
                entries.append((source + 1, place + d))
            source += 2
        found.append(entries)
    most = max(len(entries) for entries in found)
    table = np.zeros((sub, 1 + 2 * most), np.int32)
    for place, entries in enumerate(found):
        table[place, 0] = len(entries)
        for p in range(most):
            if entries:
                source, piece = entries[min(p, len(entries) - 1)]
                table[place, 1 + p] = source
                table[place, 1 + most + p] = piece
    return table, most


def matmul_kernel(plan, info, *refs):
    most, tp, spans, sources, prior_at, final, skip = plan
    parts = len(spans)
    count = sources * parts
    inputs = [refs[s * parts : (s + 1) * parts] for s in range(sources)]
    weight = refs[count]
    at = count + 1
    prior = refs[at] if prior_at is not None else None
    at += (prior_at is not None) + skip
    number = 1 + tp // 2 if final else 1
    outs = refs[at : at + number]
    token = refs[at + number]
    held, total, sems, early_sems, late_sems = refs[at + number + 1 :]
    rows = total.shape[1]
    step = pl.program_id(0)
    p = step // tp
    t = step % tp
    me = info[0]
    pieces = info[1]

    def load_prior(t):
        return pltpu.make_async_copy(
            prior.at[t, prior_at : prior_at + rows], total.at[t], early_sems.at[t]
        )

    def store(t):
        return pltpu.make_async_copy(total.at[t], outs[0].at[t], late_sems.at[t])

    @pl.when(step == 0)
    def _():
        for q in range(most):
            for s in range(sources):

                @pl.when((q < pieces) & (info[2 + q] == s))
                def _():
                    for n, (first, size) in enumerate(spans):
                        pltpu.make_async_copy(
                            inputs[s][n], held.at[q, first : first + size], sems.at[q, n]
                        ).start()

        if prior is not None:
            for k in range(tp):
                load_prior(k).start()

    if prior is not None:

        @pl.when(p == 0)
        def _():
            load_prior(t).wait()

    @pl.when(p < pieces)
    def _():
        @pl.when(t == 0)
        def _():
            for n, (first, size) in enumerate(spans):
                pltpu.make_async_copy(
                    inputs[0][n], held.at[p, first : first + size], sems.at[p, n]
                ).wait()

        product = jnp.dot(held[p], weight[...], preferred_element_type=jnp.float32)
        if prior is not None:
            total[t] += product
        else:

            @pl.when(p == 0)
            def _():
                total[t] = product

            @pl.when(p != 0)
            def _():
                total[t] += product

        if not final:

            @pl.when(p == pieces - 1)
            def _():
                store(t).start()

    @pl.when(step == most * tp - 1)
    def _():
        if final:
            for k in range(tp // 2):
                outs[0][k] = total[me ^ (2 * k)]
                outs[1 + k][...] = total[me ^ (2 * k + 1)].astype(jnp.bfloat16)
        else:
            for k in range(tp):
                store(k).wait()
        token[...] = jnp.zeros(TOKEN, jnp.float32)


def matmul_stage(place, me, stages, sub, tp, inputs, weight, prior, prior_at, final, after):
    flat = [part for source in inputs for part in source]
    sizes = [part.shape[0] for part in inputs[0]]
    rows = sum(sizes)
    spans = [(sum(sizes[:n]), size) for n, size in enumerate(sizes)]
    depth = flat[0].shape[1]
    columns = weight.shape[1]
    width = columns // tp
    table, most = stage_table(sub, stages)
    info = jnp.concatenate([me[None], jnp.asarray(table)[place]])

    def weight_block(j, s):
        j = jnp.minimum(j, jnp.maximum(s[1] * tp - 1, 0))
        return s[2 + most + j // tp], j % tp

    operands = [*flat, weight]
    specs = [anywhere()] * len(flat) + [pl.BlockSpec((depth, width), weight_block)]
    if prior is not None:
        operands.append(prior)
        specs.append(anywhere())
    operands += after
    specs += [token_spec()] * len(after)
    if final:
        out_specs = [pl.BlockSpec((tp // 2, rows, width), lambda j, s: (0, 0, 0))]
        out_specs += [pl.BlockSpec((rows, width), lambda j, s: (0, 0))] * (tp // 2)
        out_shape = [jax.ShapeDtypeStruct((tp // 2, rows, width), jnp.float32)]
        out_shape += [jax.ShapeDtypeStruct((rows, width), jnp.bfloat16)] * (tp // 2)
    else:
        out_specs = [anywhere()]
        out_shape = [jax.ShapeDtypeStruct((tp, rows, width), jnp.float32)]
    plan = (
        most,
        tp,
        spans,
        len(inputs),
        None if prior is None else prior_at,
        final,
        len(after),
    )
    return pl.pallas_call(
        functools.partial(matmul_kernel, plan),
        grid_spec=pltpu.PrefetchScalarGridSpec(
            num_scalar_prefetch=1,
            grid=(most * tp,),
            in_specs=specs,
            out_specs=out_specs + [token_spec()],
            scratch_shapes=[
                pltpu.VMEM((most, rows, depth), jnp.bfloat16),
                pltpu.VMEM((tp, rows, width), jnp.float32),
                pltpu.SemaphoreType.DMA((most, len(sizes))),
                pltpu.SemaphoreType.DMA((tp,)),
                pltpu.SemaphoreType.DMA((tp,)),
            ],
        ),
        out_shape=out_shape + [TOKEN_SHAPE],
        compiler_params=params(),
        cost_estimate=pl.CostEstimate(flops=1, bytes_accessed=1, transcendentals=0),
        name="matmul_stage",
    )(info, *operands)


def gate_kernel(count, *refs):
    refs[-1][...] = jnp.zeros(TOKEN, jnp.float32)


def gate(values, after):
    count = len(values)
    outs = pl.pallas_call(
        functools.partial(gate_kernel, count),
        grid=(1,),
        in_specs=[anywhere()] * count + [token_spec()] * len(after),
        out_specs=[anywhere()] * count + [token_spec()],
        out_shape=[jax.ShapeDtypeStruct(v.shape, v.dtype) for v in values] + [TOKEN_SHAPE],
        input_output_aliases={n: n for n in range(count)},
        compiler_params=params(),
        cost_estimate=pl.CostEstimate(flops=1, bytes_accessed=1, transcendentals=0),
        name="gate",
    )(*values, *after)
    return list(outs[:count]), [outs[count]]


def halve_kernel(cut, more, keep, *refs):
    half = keep.shape[0] // 2
    got = refs[: 2 * half]
    *outs, token = refs[2 * half + more :]
    size = keep.shape[1] // cut
    for k in range(half):
        value = (keep[2 * k + 1] + got[2 * k + 1][...].astype(jnp.float32)).astype(jnp.bfloat16)
        for n in range(cut):
            outs[k * cut + n][...] = value[n * size : (n + 1) * size]
        if half > 1:
            outs[half * cut][k] = keep[2 * k] + got[2 * k][...].astype(jnp.float32)
    token[...] = jnp.zeros(TOKEN, jnp.float32)


def halve(keep, got, cut, after):
    count, rows, width = keep.shape
    half = count // 2
    stack = lambda n: pl.BlockSpec((n, rows, width), lambda i: (0, 0, 0))
    flat = lambda n: pl.BlockSpec((n, width), lambda i: (0, 0))
    size = rows // cut
    out_specs = [flat(size)] * (half * cut)
    out_shape = [jax.ShapeDtypeStruct((size, width), jnp.bfloat16)] * (half * cut)
    if half > 1:
        out_specs.append(stack(half))
        out_shape.append(jax.ShapeDtypeStruct((half, rows, width), jnp.float32))
    outs = pl.pallas_call(
        functools.partial(halve_kernel, cut, len(after)),
        grid=(1,),
        in_specs=[stack(count)] + [flat(rows)] * count + [token_spec()] * len(after),
        out_specs=out_specs + [token_spec()],
        out_shape=out_shape + [TOKEN_SHAPE],
        compiler_params=params(),
        cost_estimate=pl.CostEstimate(flops=1, bytes_accessed=1, transcendentals=0),
        name="halve",
    )(keep, *got, *after)
    return outs[: half * cut], outs[half * cut] if half > 1 else None, outs[-1]


def stream_kernel(cut, more, *refs):
    keep, first, *last = refs[: 2 + cut]
    signs, matrix, residual = refs[2 + cut : 5 + cut]
    stream, chunk, squares = refs[5 + cut + more :]
    last = jnp.concatenate([part[...].astype(jnp.float32) for part in last], axis=0)
    total = keep[...] + first[...].astype(jnp.float32) + last
    total = total * signs[...].astype(jnp.float32)
    rows, width = total.shape
    turn = matrix[...]
    for b in range(width // 128):
        piece = total[:, b * 128 : (b + 1) * 128]
        rotated = jnp.zeros((rows, 128), jnp.float32)
        for _ in range(3):
            part = piece.astype(jnp.bfloat16)
            rotated = rotated + jnp.dot(part, turn, preferred_element_type=jnp.float32)
            piece = piece - part.astype(jnp.float32)
        kept = residual[:, b * 128 : (b + 1) * 128].astype(jnp.float32)
        value = (kept + rotated * H_SCALE).astype(jnp.bfloat16)
        stream[:, b * 128 : (b + 1) * 128] = value
        chunk[:, b * 128 : (b + 1) * 128] = value
    local = chunk[...].astype(jnp.float32)
    squares[...] = jnp.zeros_like(squares)
    squares[:, 0:rows] = lax.dot_general(
        jnp.ones((8, width), jnp.float32),
        local * local,
        (((1,), (1,)), ((), ())),
        precision=lax.Precision.HIGHEST,
        preferred_element_type=jnp.float32,
    )


def stream_rows(keep, first, last, signs, matrix, residual, so_far, start, after):
    _, rows, width = keep.shape
    cut = len(last)
    place = start // rows
    line = pl.BlockSpec((rows, width), lambda i: (place, 0))
    flat = lambda n: pl.BlockSpec((n, width), lambda i: (0, 0))
    operands = [keep, first, *last, signs, matrix, residual]
    specs = [pl.BlockSpec((None, rows, width), lambda i: (0, 0, 0)), flat(rows)]
    specs += [flat(rows // cut)] * cut
    specs += [
        pl.BlockSpec((1, width), lambda i: (0, 0)),
        pl.BlockSpec((128, 128), lambda i: (0, 0)),
        line,
    ]
    aliases = {}
    if so_far is not None:
        aliases = {len(operands): 0}
        operands.append(so_far)
        specs.append(anywhere())
    operands += after
    specs += [token_spec()] * len(after)
    return pl.pallas_call(
        functools.partial(stream_kernel, cut, len(aliases) + len(after)),
        grid=(1,),
        in_specs=specs,
        out_specs=[
            line,
            pl.BlockSpec((rows, width), lambda i: (0, 0)),
            pl.BlockSpec((8, lanes(rows)), lambda i: (0, 0)),
        ],
        out_shape=[
            jax.ShapeDtypeStruct(residual.shape, jnp.bfloat16),
            jax.ShapeDtypeStruct((rows, width), jnp.bfloat16),
            jax.ShapeDtypeStruct((8, lanes(rows)), jnp.float32),
        ],
        input_output_aliases=aliases,
        compiler_params=params(),
        cost_estimate=pl.CostEstimate(flops=1, bytes_accessed=1, transcendentals=0),
        name="stream_rows",
    )(*operands)


def norm_kernel(places, more, info, *refs):
    tp = len(places)
    pieces = refs[:tp]
    first, second, gain = refs[tp : tp + 3]
    out, token = refs[tp + 3 + more :]
    token[...] = jnp.zeros(TOKEN, jnp.float32)
    inverse = lax.rsqrt((first[...] + second[...]) / D + 1e-05)
    rows, width = pieces[0].shape
    scale = jnp.transpose(inverse)[0:rows, 0:1]
    for e, piece in zip(places, pieces):
        at = pl.ds(pl.multiple_of((info[0] ^ e) * width, width), width)
        value = piece[...].astype(jnp.float32) * scale * gain[:, at]
        out[:, at] = value.astype(jnp.bfloat16)


def norm_rows(me, pieces, squares, column, gain, so_far, start, all_rows, after):
    tp = len(pieces)
    rows, width = pieces[0][1].shape
    place = start // rows
    small = pl.BlockSpec((8, lanes(rows)), lambda i, s: (0, column))
    operands = [piece for _, piece in pieces] + [*squares, gain]
    specs = (
        [pl.BlockSpec((rows, width), lambda i, s: (0, 0))] * tp
        + [small] * 2
        + [pl.BlockSpec((1, tp * width), lambda i, s: (0, 0))]
    )
    aliases = {}
    if so_far is not None:
        aliases = {1 + len(operands): 0}
        operands.append(so_far)
        specs.append(anywhere())
    operands += after
    specs += [token_spec()] * len(after)
    return pl.pallas_call(
        functools.partial(norm_kernel, [e for e, _ in pieces], len(aliases) + len(after)),
        grid_spec=pltpu.PrefetchScalarGridSpec(
            num_scalar_prefetch=1,
            grid=(1,),
            in_specs=specs,
            out_specs=[
                pl.BlockSpec((rows, tp * width), lambda i, s: (place, 0)),
                token_spec(),
            ],
        ),
        out_shape=[jax.ShapeDtypeStruct((all_rows, tp * width), jnp.bfloat16), TOKEN_SHAPE],
        input_output_aliases=aliases,
        compiler_params=params(),
        cost_estimate=pl.CostEstimate(flops=1, bytes_accessed=1, transcendentals=0),
        name="norm_rows",
    )(me[None], *operands)


def shards(sub, tp, gate_pre, up_pre, down_weight, residual, signs, row_slot, norm_gain):
    rows = gate_pre.shape[0]
    width = residual.shape[1]
    place = lax.axis_index("sub").astype(jnp.int32)
    me = lax.axis_index("tp").astype(jnp.int32)
    matrix = hadamard_signs()
    mine = jnp.take(residual, row_slot, axis=0, mode="clip")
    signs_own = lax.dynamic_slice_in_dim(signs, me * width, width, 0).reshape(1, width)
    gain = norm_gain.reshape(1, -1)
    bits = [1 << b for b in range(tp.bit_length() - 1)]

    sizes = row_units(rows)
    starts = [sum(sizes[:u]) for u in range(len(sizes))]

    def swap(value, d):
        return lax.ppermute(value, "tp", [(i, i ^ d) for i in range(tp)])

    def onward(pair, d):
        up = lax.ppermute(pair[0], "sub", [(i, i + 1) for i in range(d - 1, sub - 1)])
        down = lax.ppermute(pair[1], "sub", [(i, i - 1) for i in range(1, sub - d + 1)])
        return [up, down]

    def matmul(stages, inputs, prior, start, final, after):
        return matmul_stage(
            place, me, stages, sub, tp, inputs, down_weight, prior, start, final, after
        )

    terms, held = {}, {}
    streams = [None]
    pieces, squares = {}, {}

    def begin_sums(u, keep, *send):
        terms[u] = [keep, [swap(value, bits[0]) for value in send]]

    def halve_sums(u, after):
        keep, got = terms[u]
        for bit in bits[1:]:
            send, kept, token = halve(keep, got, 1, after)
            after = [token]
            arrived = [swap(value, bit) for value in send]
            if kept is None:
                terms[u] = [keep, got[0], arrived]
            else:
                keep, got = kept, arrived
        return after

    def finish(u, after, pause=False):
        streams[0], chunk, squares[u] = stream_rows(
            *terms[u], signs_own, matrix, mine, streams[0], starts[u], after
        )
        found = [(0, chunk)]
        for bit in reversed(bits):
            if pause and bit == bits[0]:
                along.append(sum_along(jnp.concatenate([squares[b] for b in range(u + 1)], axis=1)))
                values, _ = gate([value for _, value in found[1:]], along)
                found[1:] = [(e, value) for (e, _), value in zip(found[1:], values)]
            found += [(e | bit, swap(value, bit)) for e, value in found]
        pieces[u] = found
        return [squares[u]]

    along = []

    def sum_along(local):
        total = local
        for d in range(1, sub):
            total = total + lax.ppermute(local, "sub", [(i, (i + d) % sub) for i in range(sub)])
        return total

    def sum_across(total):
        for bit in reversed(bits[1:]):
            total = total + swap(total, bit)
        return [total, swap(total, bits[0])]

    normed = [None]

    def normalise(us, totals, after):
        for n, u in enumerate(us):
            normed[0], token = norm_rows(
                me,
                pieces[u],
                totals,
                n,
                gain,
                normed[0],
                starts[u],
                rows,
                after,
            )
            after = [token]
        return after

    early, middle, late = [0, 1], list(range(2, sub - 1)), [sub - 1]
    own = [None] * 3
    came = {}

    def make(u, after):
        own[u], token = hidden_rows(gate_pre, up_pre, starts[u], sizes[u], after)
        came[1, u] = onward([own[u], own[u]], 1)
        return [token]

    def pass_on(u, first, last):
        for d in range(first, last + 1):
            came[d, u] = onward(came[d - 1, u], d)

    def matmul(us, stages, prior, start, final, after):
        inputs = []
        for d in stages:
            if d == 0:
                inputs.append([own[u] for u in us])
            else:
                inputs += [[came[d, u][side] for u in us] for side in range(2)]
        return matmul_stage(
            place, me, stages, sub, tp, inputs, down_weight, prior, start, final, after
        )

    def hold(keys, after):
        values, token = gate([value for key in keys for value in came[key]], after)
        for n, key in enumerate(keys):
            came[key] = values[2 * n : 2 * n + 2]
        return token

    mid = middle[-1]
    token = make(0, [])
    token = make(1, token)
    token = hold([(1, 0)], token)
    pass_on(0, 2, mid)
    token = make(2, token)
    part, *token = matmul([0], early, None, 0, False, token)
    hold([(1, 1)], token)
    pass_on(1, 2, mid)
    token = hold([(mid, 0), (1, 2)], token)
    pass_on(0, sub - 1, sub - 1)
    parts, *token = matmul([1, 2], early, None, 0, False, token)
    token = hold([(1, 2), (mid, 1)], token)
    pass_on(2, 2, mid)
    *sums, token = matmul([0], middle + late, part, 0, True, token)
    begin_sums(0, *sums)
    token = hold([(mid, 1)], [token])
    pass_on(1, sub - 1, sub - 1)
    parts, *token = matmul([1, 2], middle, parts, 0, False, token)
    hold([(mid, 2)], token)
    pass_on(2, sub - 1, sub - 1)
    token = halve_sums(0, token)
    *sums, token = matmul([1], late, parts, 0, True, token)
    begin_sums(1, *sums)
    token = finish(0, [token])
    token = halve_sums(1, token)
    *sums, token = matmul([2], late, parts, sizes[1], True, token)
    begin_sums(2, *sums)
    token = finish(1, [token])
    token = halve_sums(2, token)
    token = finish(2, token, True)
    normalise([0, 1, 2], sum_across(along[0]), token)
    return (streams[0], normed[0])


def solution(mesh):
    return jax.shard_map(
        functools.partial(shards, mesh.shape["sub"], mesh.shape["tp"]),
        mesh=mesh,
        in_specs=(
            P("groups", ("tp", "sub")),
            P("groups", ("tp", "sub")),
            P("tp", "sub"),
            P("groups", ("sub", "tp")),
            P("sub"),
            P("groups"),
            P("sub"),
        ),
        out_specs=(P("groups", ("sub", "tp")), P("groups", "sub")),
        check_vma=False,
    )
```

```python
import functools

import jax
import jax.numpy as jnp
import numpy as np
from jax import lax
from jax.experimental import pallas as pl
from jax.experimental.pallas import tpu as pltpu
from jax.sharding import PartitionSpec as P

D = 16384
H_SCALE = 0.08838834764831845
VMEM = 48 * 1024 * 1024
TOKEN = (8, 128)


def hadamard_signs():
    index = jnp.arange(128, dtype=jnp.int32)
    common = index[:, None] & index[None, :]
    parity = sum((common >> shift & 1 for shift in range(7)))
    return jnp.where(parity % 2 == 0, 1.0, -1.0).astype(jnp.bfloat16)


def row_units(rows):
    return [rows // 3, rows // 3, rows // 3]


def lanes(rows):
    return -(-rows // 128) * 128


def params():
    return pltpu.CompilerParams(vmem_limit_bytes=VMEM)


def anywhere():
    return pl.BlockSpec(memory_space=pl.ANY)


def token_spec():
    return pl.BlockSpec(TOKEN, lambda *_: (0, 0))


TOKEN_SHAPE = jax.ShapeDtypeStruct(TOKEN, jnp.float32)


def hidden_kernel(start, more, gate, up, *refs):
    out, token, held, sems = refs[more:]
    copies = [
        pltpu.make_async_copy(
            source.at[start : start + out.shape[0]], held.at[n], sems.at[n]
        )
        for n, source in enumerate((gate, up))
    ]
    for copy in copies:
        copy.start()
    for copy in copies:
        copy.wait()
    value = held[0].astype(jnp.float32)
    value = value / (1.0 + jnp.exp(-value)) * held[1].astype(jnp.float32)
    out[...] = value.astype(jnp.bfloat16)
    token[...] = jnp.zeros(TOKEN, jnp.float32)


def hidden_rows(gate, up, start, rows, after):
    columns = gate.shape[1]
    return pl.pallas_call(
        functools.partial(hidden_kernel, start, len(after)),
        grid=(1,),
        in_specs=[pl.BlockSpec(memory_space=pltpu.HBM)] * 2 + [token_spec()] * len(after),
        out_specs=[pl.BlockSpec((rows, columns), lambda i: (0, 0)), token_spec()],
        out_shape=[jax.ShapeDtypeStruct((rows, columns), jnp.bfloat16), TOKEN_SHAPE],
        scratch_shapes=[
            pltpu.VMEM((2, rows, columns), jnp.bfloat16),
            pltpu.SemaphoreType.DMA((2,)),
        ],
        compiler_params=params(),
        cost_estimate=pl.CostEstimate(flops=1, bytes_accessed=1, transcendentals=0),
        name="hidden_rows",
    )(gate, up, *after)


def stage_table(sub, stages):
    found = []
    for place in range(sub):
        entries, source = [], 0
        for d in stages:
            if d == 0:
                entries.append((source, place))
                source += 1
                continue
            if place >= d:
                entries.append((source, place - d))
            if place + d < sub:
                entries.append((source + 1, place + d))
            source += 2
        found.append(entries)
    most = max(len(entries) for entries in found)
    table = np.zeros((sub, 1 + 2 * most), np.int32)
    for place, entries in enumerate(found):
        table[place, 0] = len(entries)
        for p in range(most):
            if entries:
                source, piece = entries[min(p, len(entries) - 1)]
                table[place, 1 + p] = source
                table[place, 1 + most + p] = piece
    return table, most


def matmul_kernel(plan, info, *refs):
    most, tp, spans, sources, prior_at, final, skip = plan
    parts = len(spans)
    count = sources * parts
    inputs = [refs[s * parts : (s + 1) * parts] for s in range(sources)]
    weight = refs[count]
    at = count + 1
    prior = refs[at] if prior_at is not None else None
    at += (prior_at is not None) + skip
    number = 1 + tp // 2 if final else 1
    outs = refs[at : at + number]
    token = refs[at + number]
    held, total, sems, early_sems, late_sems = refs[at + number + 1 :]
    rows = total.shape[1]
    step = pl.program_id(0)
    p = step // tp
    t = step % tp
    me = info[0]
    pieces = info[1]

    def load_prior(t):
        return pltpu.make_async_copy(
            prior.at[t, prior_at : prior_at + rows], total.at[t], early_sems.at[t]
        )

    def store(t):
        return pltpu.make_async_copy(total.at[t], outs[0].at[t], late_sems.at[t])

    @pl.when(step == 0)
    def _():
        for q in range(most):
            for s in range(sources):

                @pl.when((q < pieces) & (info[2 + q] == s))
                def _():
                    for n, (first, size) in enumerate(spans):
                        pltpu.make_async_copy(
                            inputs[s][n], held.at[q, first : first + size], sems.at[q, n]
                        ).start()

        if prior is not None:
            for k in range(tp):
                load_prior(k).start()

    if prior is not None:

        @pl.when(p == 0)
        def _():
            load_prior(t).wait()

    @pl.when(p < pieces)
    def _():
        @pl.when(t == 0)
        def _():
            for n, (first, size) in enumerate(spans):
                pltpu.make_async_copy(
                    inputs[0][n], held.at[p, first : first + size], sems.at[p, n]
                ).wait()

        product = jnp.dot(held[p], weight[...], preferred_element_type=jnp.float32)
        if prior is not None:
            total[t] += product
        else:

            @pl.when(p == 0)
            def _():
                total[t] = product

            @pl.when(p != 0)
            def _():
                total[t] += product

        if not final:

            @pl.when(p == pieces - 1)
            def _():
                store(t).start()

    @pl.when(step == most * tp - 1)
    def _():
        if final:
            for k in range(tp // 2):
                outs[0][k] = total[me ^ (2 * k)]
                outs[1 + k][...] = total[me ^ (2 * k + 1)].astype(jnp.bfloat16)
        else:
            for k in range(tp):
                store(k).wait()
        token[...] = jnp.zeros(TOKEN, jnp.float32)


def matmul_stage(place, me, stages, sub, tp, inputs, weight, prior, prior_at, final, after):
    flat = [part for source in inputs for part in source]
    sizes = [part.shape[0] for part in inputs[0]]
    rows = sum(sizes)
    spans = [(sum(sizes[:n]), size) for n, size in enumerate(sizes)]
    depth = flat[0].shape[1]
    columns = weight.shape[1]
    width = columns // tp
    table, most = stage_table(sub, stages)
    info = jnp.concatenate([me[None], jnp.asarray(table)[place]])

    def weight_block(j, s):
        j = jnp.minimum(j, jnp.maximum(s[1] * tp - 1, 0))
        return s[2 + most + j // tp], j % tp

    operands = [*flat, weight]
    specs = [anywhere()] * len(flat) + [pl.BlockSpec((depth, width), weight_block)]
    if prior is not None:
        operands.append(prior)
        specs.append(anywhere())
    operands += after
    specs += [token_spec()] * len(after)
    if final:
        out_specs = [pl.BlockSpec((tp // 2, rows, width), lambda j, s: (0, 0, 0))]
        out_specs += [pl.BlockSpec((rows, width), lambda j, s: (0, 0))] * (tp // 2)
        out_shape = [jax.ShapeDtypeStruct((tp // 2, rows, width), jnp.float32)]
        out_shape += [jax.ShapeDtypeStruct((rows, width), jnp.bfloat16)] * (tp // 2)
    else:
        out_specs = [anywhere()]
        out_shape = [jax.ShapeDtypeStruct((tp, rows, width), jnp.float32)]
    plan = (
        most,
        tp,
        spans,
        len(inputs),
        None if prior is None else prior_at,
        final,
        len(after),
    )
    return pl.pallas_call(
        functools.partial(matmul_kernel, plan),
        grid_spec=pltpu.PrefetchScalarGridSpec(
            num_scalar_prefetch=1,
            grid=(most * tp,),
            in_specs=specs,
            out_specs=out_specs + [token_spec()],
            scratch_shapes=[
                pltpu.VMEM((most, rows, depth), jnp.bfloat16),
                pltpu.VMEM((tp, rows, width), jnp.float32),
                pltpu.SemaphoreType.DMA((most, len(sizes))),
                pltpu.SemaphoreType.DMA((tp,)),
                pltpu.SemaphoreType.DMA((tp,)),
            ],
        ),
        out_shape=out_shape + [TOKEN_SHAPE],
        compiler_params=params(),
        cost_estimate=pl.CostEstimate(flops=1, bytes_accessed=1, transcendentals=0),
        name="matmul_stage",
    )(info, *operands)


def gate_kernel(count, *refs):
    refs[-1][...] = jnp.zeros(TOKEN, jnp.float32)


def gate(values, after):
    count = len(values)
    outs = pl.pallas_call(
        functools.partial(gate_kernel, count),
        grid=(1,),
        in_specs=[anywhere()] * count + [token_spec()] * len(after),
        out_specs=[anywhere()] * count + [token_spec()],
        out_shape=[jax.ShapeDtypeStruct(v.shape, v.dtype) for v in values] + [TOKEN_SHAPE],
        input_output_aliases={n: n for n in range(count)},
        compiler_params=params(),
        cost_estimate=pl.CostEstimate(flops=1, bytes_accessed=1, transcendentals=0),
        name="gate",
    )(*values, *after)
    return list(outs[:count]), [outs[count]]


def halve_kernel(cut, more, keep, *refs):
    half = keep.shape[0] // 2
    got = refs[: 2 * half]
    *outs, token = refs[2 * half + more :]
    size = keep.shape[1] // cut
    for k in range(half):
        value = (keep[2 * k + 1] + got[2 * k + 1][...].astype(jnp.float32)).astype(jnp.bfloat16)
        for n in range(cut):
            outs[k * cut + n][...] = value[n * size : (n + 1) * size]
        if half > 1:
            outs[half * cut][k] = keep[2 * k] + got[2 * k][...].astype(jnp.float32)
    token[...] = jnp.zeros(TOKEN, jnp.float32)


def halve(keep, got, cut, after):
    count, rows, width = keep.shape
    half = count // 2
    stack = lambda n: pl.BlockSpec((n, rows, width), lambda i: (0, 0, 0))
    flat = lambda n: pl.BlockSpec((n, width), lambda i: (0, 0))
    size = rows // cut
    out_specs = [flat(size)] * (half * cut)
    out_shape = [jax.ShapeDtypeStruct((size, width), jnp.bfloat16)] * (half * cut)
    if half > 1:
        out_specs.append(stack(half))
        out_shape.append(jax.ShapeDtypeStruct((half, rows, width), jnp.float32))
    outs = pl.pallas_call(
        functools.partial(halve_kernel, cut, len(after)),
        grid=(1,),
        in_specs=[stack(count)] + [flat(rows)] * count + [token_spec()] * len(after),
        out_specs=out_specs + [token_spec()],
        out_shape=out_shape + [TOKEN_SHAPE],
        compiler_params=params(),
        cost_estimate=pl.CostEstimate(flops=1, bytes_accessed=1, transcendentals=0),
        name="halve",
    )(keep, *got, *after)
    return outs[: half * cut], outs[half * cut] if half > 1 else None, outs[-1]


def stream_kernel(cut, more, *refs):
    keep, first, *last = refs[: 2 + cut]
    signs, matrix, residual = refs[2 + cut : 5 + cut]
    stream, chunk, squares = refs[5 + cut + more :]
    last = jnp.concatenate([part[...].astype(jnp.float32) for part in last], axis=0)
    total = keep[...] + first[...].astype(jnp.float32) + last
    total = total * signs[...].astype(jnp.float32)
    rows, width = total.shape
    turn = matrix[...]
    for b in range(width // 128):
        piece = total[:, b * 128 : (b + 1) * 128]
        rotated = jnp.zeros((rows, 128), jnp.float32)
        for _ in range(3):
            part = piece.astype(jnp.bfloat16)
            rotated = rotated + jnp.dot(part, turn, preferred_element_type=jnp.float32)
            piece = piece - part.astype(jnp.float32)
        kept = residual[:, b * 128 : (b + 1) * 128].astype(jnp.float32)
        value = (kept + rotated * H_SCALE).astype(jnp.bfloat16)
        stream[:, b * 128 : (b + 1) * 128] = value
        chunk[:, b * 128 : (b + 1) * 128] = value
    local = chunk[...].astype(jnp.float32)
    squares[...] = jnp.zeros_like(squares)
    squares[:, 0:rows] = lax.dot_general(
        jnp.ones((8, width), jnp.float32),
        local * local,
        (((1,), (1,)), ((), ())),
        precision=lax.Precision.HIGHEST,
        preferred_element_type=jnp.float32,
    )


def stream_rows(keep, first, last, signs, matrix, residual, so_far, start, after):
    _, rows, width = keep.shape
    cut = len(last)
    place = start // rows
    line = pl.BlockSpec((rows, width), lambda i: (place, 0))
    flat = lambda n: pl.BlockSpec((n, width), lambda i: (0, 0))
    operands = [keep, first, *last, signs, matrix, residual]
    specs = [pl.BlockSpec((None, rows, width), lambda i: (0, 0, 0)), flat(rows)]
    specs += [flat(rows // cut)] * cut
    specs += [
        pl.BlockSpec((1, width), lambda i: (0, 0)),
        pl.BlockSpec((128, 128), lambda i: (0, 0)),
        line,
    ]
    aliases = {}
    if so_far is not None:
        aliases = {len(operands): 0}
        operands.append(so_far)
        specs.append(anywhere())
    operands += after
    specs += [token_spec()] * len(after)
    return pl.pallas_call(
        functools.partial(stream_kernel, cut, len(aliases) + len(after)),
        grid=(1,),
        in_specs=specs,
        out_specs=[
            line,
            pl.BlockSpec((rows, width), lambda i: (0, 0)),
            pl.BlockSpec((8, lanes(rows)), lambda i: (0, 0)),
        ],
        out_shape=[
            jax.ShapeDtypeStruct(residual.shape, jnp.bfloat16),
            jax.ShapeDtypeStruct((rows, width), jnp.bfloat16),
            jax.ShapeDtypeStruct((8, lanes(rows)), jnp.float32),
        ],
        input_output_aliases=aliases,
        compiler_params=params(),
        cost_estimate=pl.CostEstimate(flops=1, bytes_accessed=1, transcendentals=0),
        name="stream_rows",
    )(*operands)


def norm_kernel(places, more, info, *refs):
    tp = len(places)
    pieces = refs[:tp]
    first, second, gain = refs[tp : tp + 3]
    out, token = refs[tp + 3 + more :]
    token[...] = jnp.zeros(TOKEN, jnp.float32)
    inverse = lax.rsqrt((first[...] + second[...]) / D + 1e-05)
    rows, width = pieces[0].shape
    scale = jnp.transpose(inverse)[0:rows, 0:1]
    for e, piece in zip(places, pieces):
        at = pl.ds(pl.multiple_of((info[0] ^ e) * width, width), width)
        value = piece[...].astype(jnp.float32) * scale * gain[:, at]
        out[:, at] = value.astype(jnp.bfloat16)


def norm_rows(me, pieces, squares, column, gain, so_far, start, all_rows, after):
    tp = len(pieces)
    rows, width = pieces[0][1].shape
    place = start // rows
    small = pl.BlockSpec((8, lanes(rows)), lambda i, s: (0, column))
    operands = [piece for _, piece in pieces] + [*squares, gain]
    specs = (
        [pl.BlockSpec((rows, width), lambda i, s: (0, 0))] * tp
        + [small] * 2
        + [pl.BlockSpec((1, tp * width), lambda i, s: (0, 0))]
    )
    aliases = {}
    if so_far is not None:
        aliases = {1 + len(operands): 0}
        operands.append(so_far)
        specs.append(anywhere())
    operands += after
    specs += [token_spec()] * len(after)
    return pl.pallas_call(
        functools.partial(norm_kernel, [e for e, _ in pieces], len(aliases) + len(after)),
        grid_spec=pltpu.PrefetchScalarGridSpec(
            num_scalar_prefetch=1,
            grid=(1,),
            in_specs=specs,
            out_specs=[
                pl.BlockSpec((rows, tp * width), lambda i, s: (place, 0)),
                token_spec(),
            ],
        ),
        out_shape=[jax.ShapeDtypeStruct((all_rows, tp * width), jnp.bfloat16), TOKEN_SHAPE],
        input_output_aliases=aliases,
        compiler_params=params(),
        cost_estimate=pl.CostEstimate(flops=1, bytes_accessed=1, transcendentals=0),
        name="norm_rows",
    )(me[None], *operands)


def shards(sub, tp, gate_pre, up_pre, down_weight, residual, signs, row_slot, norm_gain):
    rows = gate_pre.shape[0]
    width = residual.shape[1]
    place = lax.axis_index("sub").astype(jnp.int32)
    me = lax.axis_index("tp").astype(jnp.int32)
    matrix = hadamard_signs()
    mine = jnp.take(residual, row_slot, axis=0, mode="clip")
    signs_own = lax.dynamic_slice_in_dim(signs, me * width, width, 0).reshape(1, width)
    gain = norm_gain.reshape(1, -1)
    bits = [1 << b for b in range(tp.bit_length() - 1)]

    sizes = row_units(rows)
    starts = [sum(sizes[:u]) for u in range(len(sizes))]

    def swap(value, d):
        return lax.ppermute(value, "tp", [(i, i ^ d) for i in range(tp)])

    def onward(pair, d):
        up = lax.ppermute(pair[0], "sub", [(i, i + 1) for i in range(d - 1, sub - 1)])
        down = lax.ppermute(pair[1], "sub", [(i, i - 1) for i in range(1, sub - d + 1)])
        return [up, down]

    def matmul(stages, inputs, prior, start, final, after):
        return matmul_stage(
            place, me, stages, sub, tp, inputs, down_weight, prior, start, final, after
        )

    terms, held = {}, {}
    streams = [None]
    pieces, squares = {}, {}

    def begin_sums(u, keep, *send):
        terms[u] = [keep, [swap(value, bits[0]) for value in send]]

    def halve_sums(u, after):
        keep, got = terms[u]
        for bit in bits[1:]:
            send, kept, token = halve(keep, got, 1, after)
            after = [token]
            arrived = [swap(value, bit) for value in send]
            if kept is None:
                terms[u] = [keep, got[0], arrived]
            else:
                keep, got = kept, arrived
        return after

    def finish(u, after):
        streams[0], chunk, squares[u] = stream_rows(
            *terms[u], signs_own, matrix, mine, streams[0], starts[u], after
        )
        pieces[u] = [(0, chunk)]
        for bit in reversed(bits[1:]):
            pieces[u] += [(e | bit, swap(value, bit)) for e, value in pieces[u]]
        return [squares[u]]

    def spread(u, after):
        values, token = gate([value for _, value in pieces[u][1:]], after)
        pieces[u][1:] = [(e, value) for (e, _), value in zip(pieces[u][1:], values)]
        pieces[u] += [(e | bits[0], swap(value, bits[0])) for e, value in pieces[u]]
        return token

    def sum_along(local):
        total = local
        for d in range(1, sub):
            total = total + lax.ppermute(local, "sub", [(i, (i + d) % sub) for i in range(sub)])
        return total

    def sum_across(total):
        for bit in reversed(bits[1:]):
            total = total + swap(total, bit)
        return [total, swap(total, bits[0])]

    normed = [None]

    def normalise(us, totals, after):
        for n, u in enumerate(us):
            normed[0], token = norm_rows(
                me,
                pieces[u],
                totals,
                sum(lanes(sizes[b]) for b in us[:n]) // lanes(sizes[u]),
                gain,
                normed[0],
                starts[u],
                rows,
                after,
            )
            after = [token]
        return after

    early, middle, late = [0, 1], list(range(2, sub - 1)), [sub - 1]
    own = [None] * 3
    came = {}

    def make(u, after):
        own[u], token = hidden_rows(gate_pre, up_pre, starts[u], sizes[u], after)
        came[1, u] = onward([own[u], own[u]], 1)
        return [token]

    def pass_on(u, first, last):
        for d in range(first, last + 1):
            came[d, u] = onward(came[d - 1, u], d)

    def matmul(us, stages, prior, start, final, after):
        inputs = []
        for d in stages:
            if d == 0:
                inputs.append([own[u] for u in us])
            else:
                inputs += [[came[d, u][side] for u in us] for side in range(2)]
        return matmul_stage(
            place, me, stages, sub, tp, inputs, down_weight, prior, start, final, after
        )

    def hold(keys, after):
        values, token = gate([value for key in keys for value in came[key]], after)
        for n, key in enumerate(keys):
            came[key] = values[2 * n : 2 * n + 2]
        return token

    mid = middle[-1]
    first = gate_pre[: sizes[0]].astype(jnp.float32), up_pre[: sizes[0]].astype(jnp.float32)
    own[0] = (jax.nn.silu(first[0]) * first[1]).astype(jnp.bfloat16)
    came[1, 0] = onward([own[0], own[0]], 1)
    token = make(1, [own[0]])
    (*came[1, 0], mine), token = gate([*came[1, 0], mine], token)
    pass_on(0, 2, mid)
    token = make(2, token)
    part, *token = matmul([0], early, None, 0, False, token)
    hold([(1, 1)], token)
    pass_on(1, 2, mid)
    token = hold([(mid, 0), (1, 2)], token)
    pass_on(0, sub - 1, sub - 1)
    parts, *token = matmul([1, 2], early, None, 0, False, token)
    token = hold([(1, 2), (mid, 1)], token)
    pass_on(2, 2, mid)
    *sums, token = matmul([0], middle + late, part, 0, True, token)
    begin_sums(0, *sums)
    token = hold([(mid, 1)], [token])
    pass_on(1, sub - 1, sub - 1)
    parts, *token = matmul([1, 2], middle, parts, 0, False, token)
    hold([(mid, 2)], token)
    pass_on(2, sub - 1, sub - 1)
    token = halve_sums(0, token)
    *sums, token = matmul([1], late, parts, 0, True, token)
    begin_sums(1, *sums)
    token = finish(0, [token])
    token = halve_sums(1, token)
    *sums, token = matmul([2], late, parts, sizes[1], True, token)
    begin_sums(2, *sums)
    token = spread(0, [token])
    token = finish(1, token)
    token = halve_sums(2, token)
    token = finish(2, token)
    along = sum_along(jnp.concatenate([squares[u] for u in range(3)], axis=1))
    spread(1, token)
    spread(2, [along])
    normalise([0, 1, 2], sum_across(along), token)
    return (streams[0], normed[0])


def solution(mesh):
    return jax.shard_map(
        functools.partial(shards, mesh.shape["sub"], mesh.shape["tp"]),
        mesh=mesh,
        in_specs=(
            P("groups", ("tp", "sub")),
            P("groups", ("tp", "sub")),
            P("tp", "sub"),
            P("groups", ("sub", "tp")),
            P("sub"),
            P("groups"),
            P("sub"),
        ),
        out_specs=(P("groups", ("sub", "tp")), P("groups", "sub")),
        check_vma=False,
    )
```

```python
import functools

import jax
import jax.numpy as jnp
import numpy as np
from jax import lax
from jax.experimental import pallas as pl
from jax.experimental.pallas import tpu as pltpu
from jax.sharding import PartitionSpec as P

D = 16384
H_SCALE = 0.08838834764831845
VMEM = 48 * 1024 * 1024
TOKEN = (8, 128)


def hadamard_signs():
    index = jnp.arange(128, dtype=jnp.int32)
    common = index[:, None] & index[None, :]
    parity = sum((common >> shift & 1 for shift in range(7)))
    return jnp.where(parity % 2 == 0, 1.0, -1.0).astype(jnp.bfloat16)


def row_units(rows):
    return [rows // 3, rows // 3, rows // 3]


def lanes(rows):
    return -(-rows // 128) * 128


def params():
    return pltpu.CompilerParams(vmem_limit_bytes=VMEM)


def anywhere():
    return pl.BlockSpec(memory_space=pl.ANY)


def token_spec():
    return pl.BlockSpec(TOKEN, lambda *_: (0, 0))


TOKEN_SHAPE = jax.ShapeDtypeStruct(TOKEN, jnp.float32)


def hidden_kernel(start, more, gate, up, *refs):
    out, token, held, sems = refs[more:]
    copies = [
        pltpu.make_async_copy(
            source.at[start : start + out.shape[0]], held.at[n], sems.at[n]
        )
        for n, source in enumerate((gate, up))
    ]
    for copy in copies:
        copy.start()
    for copy in copies:
        copy.wait()
    value = held[0].astype(jnp.float32)
    value = value / (1.0 + jnp.exp(-value)) * held[1].astype(jnp.float32)
    out[...] = value.astype(jnp.bfloat16)
    token[...] = jnp.zeros(TOKEN, jnp.float32)


def hidden_rows(gate, up, start, rows, after):
    columns = gate.shape[1]
    return pl.pallas_call(
        functools.partial(hidden_kernel, start, len(after)),
        grid=(1,),
        in_specs=[pl.BlockSpec(memory_space=pltpu.HBM)] * 2 + [token_spec()] * len(after),
        out_specs=[pl.BlockSpec((rows, columns), lambda i: (0, 0)), token_spec()],
        out_shape=[jax.ShapeDtypeStruct((rows, columns), jnp.bfloat16), TOKEN_SHAPE],
        scratch_shapes=[
            pltpu.VMEM((2, rows, columns), jnp.bfloat16),
            pltpu.SemaphoreType.DMA((2,)),
        ],
        compiler_params=params(),
        cost_estimate=pl.CostEstimate(flops=1, bytes_accessed=1, transcendentals=0),
        name="hidden_rows",
    )(gate, up, *after)


def stage_table(sub, stages):
    found = []
    for place in range(sub):
        entries, source = [], 0
        for d in stages:
            if d == 0:
                entries.append((source, place))
                source += 1
                continue
            if place >= d:
                entries.append((source, place - d))
            if place + d < sub:
                entries.append((source + 1, place + d))
            source += 2
        found.append(entries)
    most = max(len(entries) for entries in found)
    table = np.zeros((sub, 1 + 2 * most), np.int32)
    for place, entries in enumerate(found):
        table[place, 0] = len(entries)
        for p in range(most):
            if entries:
                source, piece = entries[min(p, len(entries) - 1)]
                table[place, 1 + p] = source
                table[place, 1 + most + p] = piece
    return table, most


def matmul_kernel(plan, info, *refs):
    most, tp, spans, sources, prior_at, final, skip = plan
    parts = len(spans)
    count = sources * parts
    inputs = [refs[s * parts : (s + 1) * parts] for s in range(sources)]
    weight = refs[count]
    at = count + 1
    prior = refs[at] if prior_at is not None else None
    at += (prior_at is not None) + skip
    number = tp if final else 1
    outs = refs[at : at + number]
    token = refs[at + number]
    held, total, sems, early_sems, late_sems = refs[at + number + 1 :]
    rows = total.shape[1]
    step = pl.program_id(0)
    p = step // tp
    t = step % tp
    me = info[0]
    pieces = info[1]

    def load_prior(t):
        return pltpu.make_async_copy(
            prior.at[t, prior_at : prior_at + rows], total.at[t], early_sems.at[t]
        )

    def store(t):
        return pltpu.make_async_copy(total.at[t], outs[0].at[t], late_sems.at[t])

    @pl.when(step == 0)
    def _():
        for q in range(most):
            for s in range(sources):

                @pl.when((q < pieces) & (info[2 + q] == s))
                def _():
                    for n, (first, size) in enumerate(spans):
                        pltpu.make_async_copy(
                            inputs[s][n], held.at[q, first : first + size], sems.at[q, n]
                        ).start()

        if prior is not None:
            for k in range(tp):
                load_prior(k).start()

    if prior is not None:

        @pl.when(p == 0)
        def _():
            load_prior(t).wait()

    @pl.when(p < pieces)
    def _():
        @pl.when(t == 0)
        def _():
            for n, (first, size) in enumerate(spans):
                pltpu.make_async_copy(
                    inputs[0][n], held.at[p, first : first + size], sems.at[p, n]
                ).wait()

        product = jnp.dot(held[p], weight[...], preferred_element_type=jnp.float32)
        if prior is not None:
            total[t] += product
        else:

            @pl.when(p == 0)
            def _():
                total[t] = product

            @pl.when(p != 0)
            def _():
                total[t] += product

        if not final:

            @pl.when(p == pieces - 1)
            def _():
                store(t).start()

    @pl.when(step == most * tp - 1)
    def _():
        if final:
            for k in range(tp // 2):
                outs[k][...] = total[me ^ (2 * k)]
                outs[tp // 2 + k][...] = total[me ^ (2 * k + 1)].astype(jnp.bfloat16)
        else:
            for k in range(tp):
                store(k).wait()
        token[...] = jnp.zeros(TOKEN, jnp.float32)


def matmul_stage(place, me, stages, sub, tp, inputs, weight, prior, prior_at, final, after):
    flat = [part for source in inputs for part in source]
    sizes = [part.shape[0] for part in inputs[0]]
    rows = sum(sizes)
    spans = [(sum(sizes[:n]), size) for n, size in enumerate(sizes)]
    depth = flat[0].shape[1]
    columns = weight.shape[1]
    width = columns // tp
    table, most = stage_table(sub, stages)
    info = jnp.concatenate([me[None], jnp.asarray(table)[place]])

    def weight_block(j, s):
        j = jnp.minimum(j, jnp.maximum(s[1] * tp - 1, 0))
        return s[2 + most + j // tp], j % tp

    operands = [*flat, weight]
    specs = [anywhere()] * len(flat) + [pl.BlockSpec((depth, width), weight_block)]
    if prior is not None:
        operands.append(prior)
        specs.append(anywhere())
    operands += after
    specs += [token_spec()] * len(after)
    if final:
        out_specs = [pl.BlockSpec((rows, width), lambda j, s: (0, 0))] * tp
        out_shape = [jax.ShapeDtypeStruct((rows, width), jnp.float32)] * (tp // 2)
        out_shape += [jax.ShapeDtypeStruct((rows, width), jnp.bfloat16)] * (tp // 2)
    else:
        out_specs = [anywhere()]
        out_shape = [jax.ShapeDtypeStruct((tp, rows, width), jnp.float32)]
    plan = (
        most,
        tp,
        spans,
        len(inputs),
        None if prior is None else prior_at,
        final,
        len(after),
    )
    return pl.pallas_call(
        functools.partial(matmul_kernel, plan),
        grid_spec=pltpu.PrefetchScalarGridSpec(
            num_scalar_prefetch=1,
            grid=(most * tp,),
            in_specs=specs,
            out_specs=out_specs + [token_spec()],
            scratch_shapes=[
                pltpu.VMEM((most, rows, depth), jnp.bfloat16),
                pltpu.VMEM((tp, rows, width), jnp.float32),
                pltpu.SemaphoreType.DMA((most, len(sizes))),
                pltpu.SemaphoreType.DMA((tp,)),
                pltpu.SemaphoreType.DMA((tp,)),
            ],
        ),
        out_shape=out_shape + [TOKEN_SHAPE],
        compiler_params=params(),
        cost_estimate=pl.CostEstimate(flops=1, bytes_accessed=1, transcendentals=0),
        name="matmul_stage",
    )(info, *operands)


def gate_kernel(count, *refs):
    refs[-1][...] = jnp.zeros(TOKEN, jnp.float32)


def gate(values, after):
    count = len(values)
    outs = pl.pallas_call(
        functools.partial(gate_kernel, count),
        grid=(1,),
        in_specs=[anywhere()] * count + [token_spec()] * len(after),
        out_specs=[anywhere()] * count + [token_spec()],
        out_shape=[jax.ShapeDtypeStruct(v.shape, v.dtype) for v in values] + [TOKEN_SHAPE],
        input_output_aliases={n: n for n in range(count)},
        compiler_params=params(),
        cost_estimate=pl.CostEstimate(flops=1, bytes_accessed=1, transcendentals=0),
        name="gate",
    )(*values, *after)
    return list(outs[:count]), [outs[count]]


def halve_kernel(half, more, *refs):
    keep = refs[: 2 * half] if half > 1 else [None, refs[0]]
    got = refs[len(keep) : len(keep) + 2 * half] if half > 1 else [None, refs[1]]
    outs = refs[(4 * half if half > 1 else 2) + more :]
    for k in range(half):
        value = keep[2 * k + 1][...] + got[2 * k + 1][...].astype(jnp.float32)
        outs[k][...] = value.astype(jnp.bfloat16)
        if half > 1:
            outs[half + k][...] = keep[2 * k][...] + got[2 * k][...].astype(jnp.float32)
    outs[-1][...] = jnp.zeros(TOKEN, jnp.float32)


def halve(keep, got, after):
    half = len(keep) // 2
    rows, width = keep[0].shape
    operands = [*keep, *got] if half > 1 else [keep[1], got[1]]
    flat = pl.BlockSpec((rows, width), lambda i: (0, 0))
    out_shape = [jax.ShapeDtypeStruct((rows, width), jnp.bfloat16)] * half
    if half > 1:
        out_shape += [jax.ShapeDtypeStruct((rows, width), jnp.float32)] * half
    outs = pl.pallas_call(
        functools.partial(halve_kernel, half, len(after)),
        grid=(1,),
        in_specs=[flat] * len(operands) + [token_spec()] * len(after),
        out_specs=[flat] * len(out_shape) + [token_spec()],
        out_shape=out_shape + [TOKEN_SHAPE],
        compiler_params=params(),
        cost_estimate=pl.CostEstimate(flops=1, bytes_accessed=1, transcendentals=0),
        name="halve",
    )(*operands, *after)
    return outs[:half], outs[half:-1], outs[-1]


def stream_kernel(more, keep, first, last, signs, matrix, residual, *refs):
    stream, chunk, squares = refs[more:]
    total = keep[...] + first[...].astype(jnp.float32) + last[...].astype(jnp.float32)
    total = total * signs[...].astype(jnp.float32)
    rows, width = total.shape
    turn = matrix[...]
    for b in range(width // 128):
        piece = total[:, b * 128 : (b + 1) * 128]
        rotated = jnp.zeros((rows, 128), jnp.float32)
        for _ in range(3):
            part = piece.astype(jnp.bfloat16)
            rotated = rotated + jnp.dot(part, turn, preferred_element_type=jnp.float32)
            piece = piece - part.astype(jnp.float32)
        kept = residual[:, b * 128 : (b + 1) * 128].astype(jnp.float32)
        value = (kept + rotated * H_SCALE).astype(jnp.bfloat16)
        stream[:, b * 128 : (b + 1) * 128] = value
        chunk[:, b * 128 : (b + 1) * 128] = value
    local = chunk[...].astype(jnp.float32)
    squares[...] = jnp.zeros_like(squares)
    squares[:, 0:rows] = lax.dot_general(
        jnp.ones((8, width), jnp.float32),
        local * local,
        (((1,), (1,)), ((), ())),
        precision=lax.Precision.HIGHEST,
        preferred_element_type=jnp.float32,
    )


def stream_rows(keep, first, last, signs, matrix, residual, so_far, start, after):
    rows, width = keep.shape
    place = start // rows
    line = pl.BlockSpec((rows, width), lambda i: (place, 0))
    operands = [keep, first, last, signs, matrix, residual]
    specs = [pl.BlockSpec((rows, width), lambda i: (0, 0))] * 3 + [
        pl.BlockSpec((1, width), lambda i: (0, 0)),
        pl.BlockSpec((128, 128), lambda i: (0, 0)),
        line,
    ]
    aliases = {}
    if so_far is not None:
        aliases = {len(operands): 0}
        operands.append(so_far)
        specs.append(anywhere())
    operands += after
    specs += [token_spec()] * len(after)
    return pl.pallas_call(
        functools.partial(stream_kernel, len(aliases) + len(after)),
        grid=(1,),
        in_specs=specs,
        out_specs=[
            line,
            pl.BlockSpec((rows, width), lambda i: (0, 0)),
            pl.BlockSpec((8, lanes(rows)), lambda i: (0, 0)),
        ],
        out_shape=[
            jax.ShapeDtypeStruct(residual.shape, jnp.bfloat16),
            jax.ShapeDtypeStruct((rows, width), jnp.bfloat16),
            jax.ShapeDtypeStruct((8, lanes(rows)), jnp.float32),
        ],
        input_output_aliases=aliases,
        compiler_params=params(),
        cost_estimate=pl.CostEstimate(flops=1, bytes_accessed=1, transcendentals=0),
        name="stream_rows",
    )(*operands)


def norm_kernel(places, more, info, *refs):
    tp = len(places)
    pieces = refs[:tp]
    first, second, gain = refs[tp : tp + 3]
    out, token = refs[tp + 3 + more :]
    token[...] = jnp.zeros(TOKEN, jnp.float32)
    inverse = lax.rsqrt((first[...] + second[...]) / D + 1e-05)
    rows, width = pieces[0].shape
    scale = jnp.transpose(inverse)[0:rows, 0:1]
    for e, piece in zip(places, pieces):
        at = pl.ds(pl.multiple_of((info[0] ^ e) * width, width), width)
        value = piece[...].astype(jnp.float32) * scale * gain[:, at]
        out[:, at] = value.astype(jnp.bfloat16)


def norm_rows(me, pieces, squares, column, gain, so_far, start, all_rows, after):
    tp = len(pieces)
    rows, width = pieces[0][1].shape
    place = start // rows
    small = pl.BlockSpec((8, lanes(rows)), lambda i, s: (0, column))
    operands = [piece for _, piece in pieces] + [*squares, gain]
    specs = (
        [pl.BlockSpec((rows, width), lambda i, s: (0, 0))] * tp
        + [small] * 2
        + [pl.BlockSpec((1, tp * width), lambda i, s: (0, 0))]
    )
    aliases = {}
    if so_far is not None:
        aliases = {1 + len(operands): 0}
        operands.append(so_far)
        specs.append(anywhere())
    operands += after
    specs += [token_spec()] * len(after)
    return pl.pallas_call(
        functools.partial(norm_kernel, [e for e, _ in pieces], len(aliases) + len(after)),
        grid_spec=pltpu.PrefetchScalarGridSpec(
            num_scalar_prefetch=1,
            grid=(1,),
            in_specs=specs,
            out_specs=[
                pl.BlockSpec((rows, tp * width), lambda i, s: (place, 0)),
                token_spec(),
            ],
        ),
        out_shape=[jax.ShapeDtypeStruct((all_rows, tp * width), jnp.bfloat16), TOKEN_SHAPE],
        input_output_aliases=aliases,
        compiler_params=params(),
        cost_estimate=pl.CostEstimate(flops=1, bytes_accessed=1, transcendentals=0),
        name="norm_rows",
    )(me[None], *operands)


def shards(sub, tp, gate_pre, up_pre, down_weight, residual, signs, row_slot, norm_gain):
    rows = gate_pre.shape[0]
    width = residual.shape[1]
    place = lax.axis_index("sub").astype(jnp.int32)
    me = lax.axis_index("tp").astype(jnp.int32)
    matrix = hadamard_signs()
    mine = jnp.take(residual, row_slot, axis=0, mode="clip")
    signs_own = lax.dynamic_slice_in_dim(signs, me * width, width, 0).reshape(1, width)
    gain = norm_gain.reshape(1, -1)
    bits = [1 << b for b in range(tp.bit_length() - 1)]

    sizes = row_units(rows)
    starts = [sum(sizes[:u]) for u in range(len(sizes))]

    def swap(value, d):
        return lax.ppermute(value, "tp", [(i, i ^ d) for i in range(tp)])

    def onward(pair, d):
        up = lax.ppermute(pair[0], "sub", [(i, i + 1) for i in range(d - 1, sub - 1)])
        down = lax.ppermute(pair[1], "sub", [(i, i - 1) for i in range(1, sub - d + 1)])
        return [up, down]

    def matmul(stages, inputs, prior, start, final, after):
        return matmul_stage(
            place, me, stages, sub, tp, inputs, down_weight, prior, start, final, after
        )

    terms, held = {}, {}
    streams = [None]
    pieces, squares = {}, {}

    def begin_sums(u, sums):
        terms[u] = [sums[: tp // 2], [swap(value, bits[0]) for value in sums[tp // 2 :]]]

    def halve_sums(u, after):
        keep, got = terms[u]
        for bit in bits[1:]:
            send, kept, token = halve(keep, got, after)
            after = [token]
            arrived = [swap(value, bit) for value in send]
            if kept:
                keep, got = kept, arrived
        terms[u] = [keep[0], got[0], arrived[0]]
        return after

    def finish(u, after):
        streams[0], chunk, squares[u] = stream_rows(
            *terms[u], signs_own, matrix, mine, streams[0], starts[u], after
        )
        pieces[u] = [(0, chunk)]
        for bit in reversed(bits[1:]):
            pieces[u] += [(e | bit, swap(value, bit)) for e, value in pieces[u]]
        return [squares[u]]

    def spread(u, after):
        token = after
        if after:
            values, token = gate([value for _, value in pieces[u][1:]], after)
            pieces[u][1:] = [(e, value) for (e, _), value in zip(pieces[u][1:], values)]
        pieces[u] += [(e | bits[0], swap(value, bits[0])) for e, value in pieces[u]]
        return token

    def sum_along(local):
        total = local
        for d in range(1, sub):
            total = total + lax.ppermute(local, "sub", [(i, (i + d) % sub) for i in range(sub)])
        return total

    def sum_across(total):
        for bit in reversed(bits[1:]):
            total = total + swap(total, bit)
        return [total, swap(total, bits[0])]

    normed = [None]

    def normalise(us, totals, after):
        for n, u in enumerate(us):
            normed[0], token = norm_rows(
                me,
                pieces[u],
                totals,
                sum(lanes(sizes[b]) for b in us[:n]) // lanes(sizes[u]),
                gain,
                normed[0],
                starts[u],
                rows,
                after,
            )
            after = [token]
        return after

    early, middle, late = [0, 1], list(range(2, sub - 1)), [sub - 1]
    own = [None] * 3
    came = {}

    def make(u, after):
        own[u], token = hidden_rows(gate_pre, up_pre, starts[u], sizes[u], after)
        came[1, u] = onward([own[u], own[u]], 1)
        return [token]

    def pass_on(u, first, last):
        for d in range(first, last + 1):
            came[d, u] = onward(came[d - 1, u], d)

    def matmul(us, stages, prior, start, final, after):
        inputs = []
        for d in stages:
            if d == 0:
                inputs.append([own[u] for u in us])
            else:
                inputs += [[came[d, u][side] for u in us] for side in range(2)]
        return matmul_stage(
            place, me, stages, sub, tp, inputs, down_weight, prior, start, final, after
        )

    def hold(keys, after):
        values, token = gate([value for key in keys for value in came[key]], after)
        for n, key in enumerate(keys):
            came[key] = values[2 * n : 2 * n + 2]
        return token

    mid = middle[-1]
    first = gate_pre[: sizes[0]].astype(jnp.float32), up_pre[: sizes[0]].astype(jnp.float32)
    own[0] = (jax.nn.silu(first[0]) * first[1]).astype(jnp.bfloat16)
    came[1, 0] = onward([own[0], own[0]], 1)
    token = make(1, [own[0]])
    (*came[1, 0], mine), token = gate([*came[1, 0], mine], token)
    pass_on(0, 2, mid)
    token = make(2, token)
    part, *token = matmul([0], early, None, 0, False, token)
    hold([(1, 1)], token)
    pass_on(1, 2, mid)
    token = hold([(mid, 0), (1, 2)], token)
    pass_on(0, sub - 1, sub - 1)
    parts, *token = matmul([1, 2], early, None, 0, False, token)
    token = hold([(1, 2), (mid, 1)], token)
    pass_on(2, 2, mid)
    *sums, token = matmul([0], middle + late, part, 0, True, token)
    begin_sums(0, sums)
    token = hold([(mid, 1)], [token])
    pass_on(1, sub - 1, sub - 1)
    parts, *token = matmul([1, 2], middle, parts, 0, False, token)
    hold([(mid, 2)], token)
    pass_on(2, sub - 1, sub - 1)
    token = halve_sums(0, token)
    *sums, token = matmul([1], late, parts, 0, True, token)
    begin_sums(1, sums)
    token = halve_sums(1, [token])
    token = finish(0, token)
    *sums, token = matmul([2], late, parts, sizes[1], True, token)
    begin_sums(2, sums)
    token = spread(0, [token])
    token = finish(1, token)
    token = halve_sums(2, token)
    along = sum_along(jnp.concatenate([squares[0], squares[1]], axis=1))
    token = finish(2, token)
    spread(1, [])
    token = normalise([0, 1], sum_across(along), token)
    along = sum_along(squares[2])
    spread(2, [along])
    normalise([2], sum_across(along), token)
    return (streams[0], normed[0])


def solution(mesh):
    return jax.shard_map(
        functools.partial(shards, mesh.shape["sub"], mesh.shape["tp"]),
        mesh=mesh,
        in_specs=(
            P("groups", ("tp", "sub")),
            P("groups", ("tp", "sub")),
            P("tp", "sub"),
            P("groups", ("sub", "tp")),
            P("sub"),
            P("groups"),
            P("sub"),
        ),
        out_specs=(P("groups", ("sub", "tp")), P("groups", "sub")),
        check_vma=False,
    )
```

```python
import functools

import jax
import jax.numpy as jnp
import numpy as np
from jax import lax
from jax.experimental import pallas as pl
from jax.experimental.pallas import tpu as pltpu
from jax.sharding import PartitionSpec as P

D = 16384
H_SCALE = 0.08838834764831845
VMEM = 48 * 1024 * 1024
TOKEN = (8, 128)


def hadamard_signs():
    index = jnp.arange(128, dtype=jnp.int32)
    common = index[:, None] & index[None, :]
    parity = sum((common >> shift & 1 for shift in range(7)))
    return jnp.where(parity % 2 == 0, 1.0, -1.0).astype(jnp.bfloat16)


def row_units(rows):
    return [rows // 3, rows // 3, rows // 3]


def lanes(rows):
    return -(-rows // 128) * 128


def params():
    return pltpu.CompilerParams(vmem_limit_bytes=VMEM)


def anywhere():
    return pl.BlockSpec(memory_space=pl.ANY)


def token_spec():
    return pl.BlockSpec(TOKEN, lambda *_: (0, 0))


TOKEN_SHAPE = jax.ShapeDtypeStruct(TOKEN, jnp.float32)


def hidden_kernel(start, more, gate, up, *refs):
    out, token, held, sems = refs[more:]
    copies = [
        pltpu.make_async_copy(
            source.at[start : start + out.shape[0]], held.at[n], sems.at[n]
        )
        for n, source in enumerate((gate, up))
    ]
    for copy in copies:
        copy.start()
    for copy in copies:
        copy.wait()
    value = held[0].astype(jnp.float32)
    value = value / (1.0 + jnp.exp(-value)) * held[1].astype(jnp.float32)
    out[...] = value.astype(jnp.bfloat16)
    token[...] = jnp.zeros(TOKEN, jnp.float32)


def hidden_rows(gate, up, start, rows, after):
    columns = gate.shape[1]
    return pl.pallas_call(
        functools.partial(hidden_kernel, start, len(after)),
        grid=(1,),
        in_specs=[pl.BlockSpec(memory_space=pltpu.HBM)] * 2 + [token_spec()] * len(after),
        out_specs=[pl.BlockSpec((rows, columns), lambda i: (0, 0)), token_spec()],
        out_shape=[jax.ShapeDtypeStruct((rows, columns), jnp.bfloat16), TOKEN_SHAPE],
        scratch_shapes=[
            pltpu.VMEM((2, rows, columns), jnp.bfloat16),
            pltpu.SemaphoreType.DMA((2,)),
        ],
        compiler_params=params(),
        cost_estimate=pl.CostEstimate(flops=1, bytes_accessed=1, transcendentals=0),
        name="hidden_rows",
    )(gate, up, *after)


def stage_table(sub, stages):
    found = []
    for place in range(sub):
        entries, source = [], 0
        for d in stages:
            if d == 0:
                entries.append((source, place))
                source += 1
                continue
            if place >= d:
                entries.append((source, place - d))
            if place + d < sub:
                entries.append((source + 1, place + d))
            source += 2
        found.append(entries)
    most = max(len(entries) for entries in found)
    table = np.zeros((sub, 1 + 2 * most), np.int32)
    for place, entries in enumerate(found):
        table[place, 0] = len(entries)
        for p in range(most):
            if entries:
                source, piece = entries[min(p, len(entries) - 1)]
                table[place, 1 + p] = source
                table[place, 1 + most + p] = piece
    return table, most


def matmul_kernel(plan, info, *refs):
    most, tp, spans, sources, prior_at, final, skip = plan
    parts = len(spans)
    count = sources * parts
    inputs = [refs[s * parts : (s + 1) * parts] for s in range(sources)]
    weight = refs[count]
    at = count + 1
    prior = refs[at] if prior_at is not None else None
    at += (prior_at is not None) + skip
    number = tp if final else 1
    outs = refs[at : at + number]
    token = refs[at + number]
    held, total, sems, early_sems, late_sems = refs[at + number + 1 :]
    rows = total.shape[1]
    step = pl.program_id(0)
    p = step // tp
    t = step % tp
    me = info[0]
    pieces = info[1]

    def load_prior(t):
        return pltpu.make_async_copy(
            prior.at[t, prior_at : prior_at + rows], total.at[t], early_sems.at[t]
        )

    def store(t):
        return pltpu.make_async_copy(total.at[t], outs[0].at[t], late_sems.at[t])

    @pl.when(step == 0)
    def _():
        for q in range(most):
            for s in range(sources):

                @pl.when((q < pieces) & (info[2 + q] == s))
                def _():
                    for n, (first, size) in enumerate(spans):
                        pltpu.make_async_copy(
                            inputs[s][n], held.at[q, first : first + size], sems.at[q, n]
                        ).start()

        if prior is not None:
            for k in range(tp):
                load_prior(k).start()

    if prior is not None:

        @pl.when(p == 0)
        def _():
            load_prior(t).wait()

    @pl.when(p < pieces)
    def _():
        @pl.when(t == 0)
        def _():
            for n, (first, size) in enumerate(spans):
                pltpu.make_async_copy(
                    inputs[0][n], held.at[p, first : first + size], sems.at[p, n]
                ).wait()

        product = jnp.dot(held[p], weight[...], preferred_element_type=jnp.float32)
        if prior is not None:
            total[t] += product
        else:

            @pl.when(p == 0)
            def _():
                total[t] = product

            @pl.when(p != 0)
            def _():
                total[t] += product

        if not final:

            @pl.when(p == pieces - 1)
            def _():
                store(t).start()

    @pl.when(step == most * tp - 1)
    def _():
        if final:
            for k in range(tp // 2):
                outs[k][...] = total[me ^ (2 * k)]
                outs[tp // 2 + k][...] = total[me ^ (2 * k + 1)].astype(jnp.bfloat16)
        else:
            for k in range(tp):
                store(k).wait()
        token[...] = jnp.zeros(TOKEN, jnp.float32)


def matmul_stage(place, me, stages, sub, tp, inputs, weight, prior, prior_at, final, after):
    flat = [part for source in inputs for part in source]
    sizes = [part.shape[0] for part in inputs[0]]
    rows = sum(sizes)
    spans = [(sum(sizes[:n]), size) for n, size in enumerate(sizes)]
    depth = flat[0].shape[1]
    columns = weight.shape[1]
    width = columns // tp
    table, most = stage_table(sub, stages)
    info = jnp.concatenate([me[None], jnp.asarray(table)[place]])

    def weight_block(j, s):
        j = jnp.minimum(j, jnp.maximum(s[1] * tp - 1, 0))
        return s[2 + most + j // tp], j % tp

    operands = [*flat, weight]
    specs = [anywhere()] * len(flat) + [pl.BlockSpec((depth, width), weight_block)]
    if prior is not None:
        operands.append(prior)
        specs.append(anywhere())
    operands += after
    specs += [token_spec()] * len(after)
    if final:
        out_specs = [pl.BlockSpec((rows, width), lambda j, s: (0, 0))] * tp
        out_shape = [jax.ShapeDtypeStruct((rows, width), jnp.float32)] * (tp // 2)
        out_shape += [jax.ShapeDtypeStruct((rows, width), jnp.bfloat16)] * (tp // 2)
    else:
        out_specs = [anywhere()]
        out_shape = [jax.ShapeDtypeStruct((tp, rows, width), jnp.float32)]
    plan = (
        most,
        tp,
        spans,
        len(inputs),
        None if prior is None else prior_at,
        final,
        len(after),
    )
    return pl.pallas_call(
        functools.partial(matmul_kernel, plan),
        grid_spec=pltpu.PrefetchScalarGridSpec(
            num_scalar_prefetch=1,
            grid=(most * tp,),
            in_specs=specs,
            out_specs=out_specs + [token_spec()],
            scratch_shapes=[
                pltpu.VMEM((most, rows, depth), jnp.bfloat16),
                pltpu.VMEM((tp, rows, width), jnp.float32),
                pltpu.SemaphoreType.DMA((most, len(sizes))),
                pltpu.SemaphoreType.DMA((tp,)),
                pltpu.SemaphoreType.DMA((tp,)),
            ],
        ),
        out_shape=out_shape + [TOKEN_SHAPE],
        compiler_params=params(),
        cost_estimate=pl.CostEstimate(flops=1, bytes_accessed=1, transcendentals=0),
        name="matmul_stage",
    )(info, *operands)


def gate_kernel(count, *refs):
    refs[-1][...] = jnp.zeros(TOKEN, jnp.float32)


def gate(values, after):
    count = len(values)
    outs = pl.pallas_call(
        functools.partial(gate_kernel, count),
        grid=(1,),
        in_specs=[anywhere()] * count + [token_spec()] * len(after),
        out_specs=[anywhere()] * count + [token_spec()],
        out_shape=[jax.ShapeDtypeStruct(v.shape, v.dtype) for v in values] + [TOKEN_SHAPE],
        input_output_aliases={n: n for n in range(count)},
        compiler_params=params(),
        cost_estimate=pl.CostEstimate(flops=1, bytes_accessed=1, transcendentals=0),
        name="gate",
    )(*values, *after)
    return list(outs[:count]), [outs[count]]


def halve_kernel(half, more, *refs):
    keep = refs[: 2 * half] if half > 1 else [None, refs[0]]
    got = refs[len(keep) : len(keep) + 2 * half] if half > 1 else [None, refs[1]]
    outs = refs[(4 * half if half > 1 else 2) + more :]
    for k in range(half):
        value = keep[2 * k + 1][...] + got[2 * k + 1][...].astype(jnp.float32)
        outs[k][...] = value.astype(jnp.bfloat16)
        if half > 1:
            outs[half + k][...] = keep[2 * k][...] + got[2 * k][...].astype(jnp.float32)
    outs[-1][...] = jnp.zeros(TOKEN, jnp.float32)


def halve(keep, got, after):
    half = len(keep) // 2
    rows, width = keep[0].shape
    operands = [*keep, *got] if half > 1 else [keep[1], got[1]]
    flat = pl.BlockSpec((rows, width), lambda i: (0, 0))
    out_shape = [jax.ShapeDtypeStruct((rows, width), jnp.bfloat16)] * half
    if half > 1:
        out_shape += [jax.ShapeDtypeStruct((rows, width), jnp.float32)] * half
    outs = pl.pallas_call(
        functools.partial(halve_kernel, half, len(after)),
        grid=(1,),
        in_specs=[flat] * len(operands) + [token_spec()] * len(after),
        out_specs=[flat] * len(out_shape) + [token_spec()],
        out_shape=out_shape + [TOKEN_SHAPE],
        compiler_params=params(),
        cost_estimate=pl.CostEstimate(flops=1, bytes_accessed=1, transcendentals=0),
        name="halve",
    )(*operands, *after)
    return outs[:half], outs[half:-1], outs[-1]


def stream_kernel(more, keep, first, last, signs, matrix, residual, *refs):
    stream, chunk, squares = refs[more:]
    total = keep[...] + first[...].astype(jnp.float32) + last[...].astype(jnp.float32)
    total = total * signs[...].astype(jnp.float32)
    rows, width = total.shape
    turn = matrix[...]
    for b in range(width // 128):
        piece = total[:, b * 128 : (b + 1) * 128]
        rotated = jnp.zeros((rows, 128), jnp.float32)
        for _ in range(3):
            part = piece.astype(jnp.bfloat16)
            rotated = rotated + jnp.dot(part, turn, preferred_element_type=jnp.float32)
            piece = piece - part.astype(jnp.float32)
        kept = residual[:, b * 128 : (b + 1) * 128].astype(jnp.float32)
        value = (kept + rotated * H_SCALE).astype(jnp.bfloat16)
        stream[:, b * 128 : (b + 1) * 128] = value
        chunk[:, b * 128 : (b + 1) * 128] = value
    local = chunk[...].astype(jnp.float32)
    squares[...] = jnp.zeros_like(squares)
    squares[:, 0:rows] = lax.dot_general(
        jnp.ones((8, width), jnp.float32),
        local * local,
        (((1,), (1,)), ((), ())),
        precision=lax.Precision.HIGHEST,
        preferred_element_type=jnp.float32,
    )


def stream_rows(keep, first, last, signs, matrix, residual, so_far, start, after):
    rows, width = keep.shape
    place = start // rows
    line = pl.BlockSpec((rows, width), lambda i: (place, 0))
    operands = [keep, first, last, signs, matrix, residual]
    specs = [pl.BlockSpec((rows, width), lambda i: (0, 0))] * 3 + [
        pl.BlockSpec((1, width), lambda i: (0, 0)),
        pl.BlockSpec((128, 128), lambda i: (0, 0)),
        line,
    ]
    aliases = {}
    if so_far is not None:
        aliases = {len(operands): 0}
        operands.append(so_far)
        specs.append(anywhere())
    operands += after
    specs += [token_spec()] * len(after)
    return pl.pallas_call(
        functools.partial(stream_kernel, len(aliases) + len(after)),
        grid=(1,),
        in_specs=specs,
        out_specs=[
            line,
            pl.BlockSpec((rows, width), lambda i: (0, 0)),
            pl.BlockSpec((8, lanes(rows)), lambda i: (0, 0)),
        ],
        out_shape=[
            jax.ShapeDtypeStruct(residual.shape, jnp.bfloat16),
            jax.ShapeDtypeStruct((rows, width), jnp.bfloat16),
            jax.ShapeDtypeStruct((8, lanes(rows)), jnp.float32),
        ],
        input_output_aliases=aliases,
        compiler_params=params(),
        cost_estimate=pl.CostEstimate(flops=1, bytes_accessed=1, transcendentals=0),
        name="stream_rows",
    )(*operands)


def norm_kernel(places, more, info, *refs):
    tp = len(places)
    pieces = refs[:tp]
    first, second, gain = refs[tp : tp + 3]
    out, token = refs[tp + 3 + more :]
    token[...] = jnp.zeros(TOKEN, jnp.float32)
    inverse = lax.rsqrt((first[...] + second[...]) / D + 1e-05)
    rows, width = pieces[0].shape
    scale = jnp.transpose(inverse)[0:rows, 0:1]
    for e, piece in zip(places, pieces):
        at = pl.ds(pl.multiple_of((info[0] ^ e) * width, width), width)
        value = piece[...].astype(jnp.float32) * scale * gain[:, at]
        out[:, at] = value.astype(jnp.bfloat16)


def norm_rows(me, pieces, squares, column, gain, so_far, start, all_rows, after):
    tp = len(pieces)
    rows, width = pieces[0][1].shape
    place = start // rows
    small = pl.BlockSpec((8, lanes(rows)), lambda i, s: (0, column))
    operands = [piece for _, piece in pieces] + [*squares, gain]
    specs = (
        [pl.BlockSpec((rows, width), lambda i, s: (0, 0))] * tp
        + [small] * 2
        + [pl.BlockSpec((1, tp * width), lambda i, s: (0, 0))]
    )
    aliases = {}
    if so_far is not None:
        aliases = {1 + len(operands): 0}
        operands.append(so_far)
        specs.append(anywhere())
    operands += after
    specs += [token_spec()] * len(after)
    return pl.pallas_call(
        functools.partial(norm_kernel, [e for e, _ in pieces], len(aliases) + len(after)),
        grid_spec=pltpu.PrefetchScalarGridSpec(
            num_scalar_prefetch=1,
            grid=(1,),
            in_specs=specs,
            out_specs=[
                pl.BlockSpec((rows, tp * width), lambda i, s: (place, 0)),
                token_spec(),
            ],
        ),
        out_shape=[jax.ShapeDtypeStruct((all_rows, tp * width), jnp.bfloat16), TOKEN_SHAPE],
        input_output_aliases=aliases,
        compiler_params=params(),
        cost_estimate=pl.CostEstimate(flops=1, bytes_accessed=1, transcendentals=0),
        name="norm_rows",
    )(me[None], *operands)


def shards(sub, tp, gate_pre, up_pre, down_weight, residual, signs, row_slot, norm_gain):
    rows = gate_pre.shape[0]
    width = residual.shape[1]
    place = lax.axis_index("sub").astype(jnp.int32)
    me = lax.axis_index("tp").astype(jnp.int32)
    matrix = hadamard_signs()
    mine = jnp.take(residual, row_slot, axis=0, mode="clip")
    signs_own = lax.dynamic_slice_in_dim(signs, me * width, width, 0).reshape(1, width)
    gain = norm_gain.reshape(1, -1)
    bits = [1 << b for b in range(tp.bit_length() - 1)]

    sizes = row_units(rows)
    starts = [sum(sizes[:u]) for u in range(len(sizes))]

    def swap(value, d):
        return lax.ppermute(value, "tp", [(i, i ^ d) for i in range(tp)])

    def onward(pair, d):
        up = lax.ppermute(pair[0], "sub", [(i, i + 1) for i in range(d - 1, sub - 1)])
        down = lax.ppermute(pair[1], "sub", [(i, i - 1) for i in range(1, sub - d + 1)])
        return [up, down]

    def matmul(stages, inputs, prior, start, final, after):
        return matmul_stage(
            place, me, stages, sub, tp, inputs, down_weight, prior, start, final, after
        )

    terms, held = {}, {}
    streams = [None]
    pieces, squares = {}, {}

    def begin_sums(u, sums):
        terms[u] = [sums[: tp // 2], [swap(value, bits[0]) for value in sums[tp // 2 :]]]

    def halve_sums(u, after):
        keep, got = terms[u]
        for bit in bits[1:]:
            send, kept, token = halve(keep, got, after)
            after = [token]
            arrived = [swap(value, bit) for value in send]
            if kept:
                keep, got = kept, arrived
        terms[u] = [keep[0], got[0], arrived[0]]
        return after

    def finish(u, after):
        streams[0], chunk, squares[u] = stream_rows(
            *terms[u], signs_own, matrix, mine, streams[0], starts[u], after
        )
        pieces[u] = [(0, chunk)]
        for bit in reversed(bits[1:]):
            pieces[u] += [(e | bit, swap(value, bit)) for e, value in pieces[u]]
        return [squares[u]]

    def spread(u, after):
        token = after
        if after:
            values, token = gate([value for _, value in pieces[u][1:]], after)
            pieces[u][1:] = [(e, value) for (e, _), value in zip(pieces[u][1:], values)]
        pieces[u] += [(e | bits[0], swap(value, bits[0])) for e, value in pieces[u]]
        return token

    def sum_along(local):
        total = local
        for d in range(1, sub):
            total = total + lax.ppermute(local, "sub", [(i, (i + d) % sub) for i in range(sub)])
        return total

    def sum_across(total):
        for bit in reversed(bits[1:]):
            total = total + swap(total, bit)
        return [total, swap(total, bits[0])]

    normed = [None]

    def normalise(us, totals, after):
        for n, u in enumerate(us):
            normed[0], token = norm_rows(
                me,
                pieces[u],
                totals,
                sum(lanes(sizes[b]) for b in us[:n]) // lanes(sizes[u]),
                gain,
                normed[0],
                starts[u],
                rows,
                after,
            )
            after = [token]
        return after

    early, middle, late = [0, 1], list(range(2, sub - 1)), [sub - 1]
    own = [None] * 3
    came = {}

    def make(u, after):
        own[u], token = hidden_rows(gate_pre, up_pre, starts[u], sizes[u], after)
        came[1, u] = onward([own[u], own[u]], 1)
        return [token]

    def pass_on(u, first, last):
        for d in range(first, last + 1):
            came[d, u] = onward(came[d - 1, u], d)

    def matmul(us, stages, prior, start, final, after):
        inputs = []
        for d in stages:
            if d == 0:
                inputs.append([own[u] for u in us])
            else:
                inputs += [[came[d, u][side] for u in us] for side in range(2)]
        return matmul_stage(
            place, me, stages, sub, tp, inputs, down_weight, prior, start, final, after
        )

    def hold(keys, after):
        values, token = gate([value for key in keys for value in came[key]], after)
        for n, key in enumerate(keys):
            came[key] = values[2 * n : 2 * n + 2]
        return token

    mid = middle[-1]
    first = gate_pre[: sizes[0]].astype(jnp.float32), up_pre[: sizes[0]].astype(jnp.float32)
    own[0] = (jax.nn.silu(first[0]) * first[1]).astype(jnp.bfloat16)
    came[1, 0] = onward([own[0], own[0]], 1)
    token = make(1, [own[0]])
    (*came[1, 0], mine), token = gate([*came[1, 0], mine], token)
    pass_on(0, 2, mid)
    token = make(2, token)
    part, *token = matmul([0], early, None, 0, False, token)
    hold([(1, 1)], token)
    pass_on(1, 2, mid)
    token = hold([(mid, 0), (1, 2)], token)
    pass_on(0, sub - 1, sub - 1)
    parts, *token = matmul([1, 2], early, None, 0, False, token)
    token = hold([(1, 2), (mid, 1)], token)
    pass_on(2, 2, mid)
    *sums, token = matmul([0], middle + late, part, 0, True, token)
    begin_sums(0, sums)
    token = hold([(mid, 1)], [token])
    pass_on(1, sub - 1, sub - 1)
    token = halve_sums(0, token)
    parts, *token = matmul([1, 2], middle, parts, 0, False, token)
    token = hold([(mid, 2)], token)
    pass_on(2, sub - 1, sub - 1)
    token = finish(0, token)
    *sums, token = matmul([1], late, parts, 0, True, token)
    begin_sums(1, sums)
    token = spread(0, [token])
    token = halve_sums(1, token)
    *sums, token = matmul([2], late, parts, sizes[1], True, token)
    begin_sums(2, sums)
    token = finish(1, [token])
    token = halve_sums(2, token)
    token = finish(2, token)
    along = sum_along(jnp.concatenate([squares[u] for u in range(3)], axis=1))
    spread(1, token)
    spread(2, [along])
    normalise([0, 1, 2], sum_across(along), token)
    return (streams[0], normed[0])


def solution(mesh):
    return jax.shard_map(
        functools.partial(shards, mesh.shape["sub"], mesh.shape["tp"]),
        mesh=mesh,
        in_specs=(
            P("groups", ("tp", "sub")),
            P("groups", ("tp", "sub")),
            P("tp", "sub"),
            P("groups", ("sub", "tp")),
            P("sub"),
            P("groups"),
            P("sub"),
        ),
        out_specs=(P("groups", ("sub", "tp")), P("groups", "sub")),
        check_vma=False,
    )
```

```python
import functools

import jax
import jax.numpy as jnp
import numpy as np
from jax import lax
from jax.experimental import pallas as pl
from jax.experimental.pallas import tpu as pltpu
from jax.sharding import PartitionSpec as P

D = 16384
H_SCALE = 0.08838834764831845
VMEM = 48 * 1024 * 1024
TOKEN = (8, 128)


def hadamard_signs():
    index = jnp.arange(128, dtype=jnp.int32)
    common = index[:, None] & index[None, :]
    parity = sum((common >> shift & 1 for shift in range(7)))
    return jnp.where(parity % 2 == 0, 1.0, -1.0).astype(jnp.bfloat16)


def row_units(rows):
    return [rows // 3, rows // 3, rows // 3]


def lanes(rows):
    return -(-rows // 128) * 128


def params():
    return pltpu.CompilerParams(vmem_limit_bytes=VMEM)


def anywhere():
    return pl.BlockSpec(memory_space=pl.ANY)


def token_spec():
    return pl.BlockSpec(TOKEN, lambda *_: (0, 0))


TOKEN_SHAPE = jax.ShapeDtypeStruct(TOKEN, jnp.float32)


def hidden_kernel(start, more, gate, up, *refs):
    out, token, held, sems = refs[more:]
    copies = [
        pltpu.make_async_copy(
            source.at[start : start + out.shape[0]], held.at[n], sems.at[n]
        )
        for n, source in enumerate((gate, up))
    ]
    for copy in copies:
        copy.start()
    for copy in copies:
        copy.wait()
    value = held[0].astype(jnp.float32)
    value = value / (1.0 + jnp.exp(-value)) * held[1].astype(jnp.float32)
    out[...] = value.astype(jnp.bfloat16)
    token[...] = jnp.zeros(TOKEN, jnp.float32)


def hidden_rows(gate, up, start, rows, after):
    columns = gate.shape[1]
    return pl.pallas_call(
        functools.partial(hidden_kernel, start, len(after)),
        grid=(1,),
        in_specs=[pl.BlockSpec(memory_space=pltpu.HBM)] * 2 + [token_spec()] * len(after),
        out_specs=[pl.BlockSpec((rows, columns), lambda i: (0, 0)), token_spec()],
        out_shape=[jax.ShapeDtypeStruct((rows, columns), jnp.bfloat16), TOKEN_SHAPE],
        scratch_shapes=[
            pltpu.VMEM((2, rows, columns), jnp.bfloat16),
            pltpu.SemaphoreType.DMA((2,)),
        ],
        compiler_params=params(),
        cost_estimate=pl.CostEstimate(flops=1, bytes_accessed=1, transcendentals=0),
        name="hidden_rows",
    )(gate, up, *after)


def stage_table(sub, stages):
    found = []
    for place in range(sub):
        entries, source = [], 0
        for d in stages:
            if d == 0:
                entries.append((source, place))
                source += 1
                continue
            if place >= d:
                entries.append((source, place - d))
            if place + d < sub:
                entries.append((source + 1, place + d))
            source += 2
        found.append(entries)
    most = max(len(entries) for entries in found)
    table = np.zeros((sub, 1 + 2 * most), np.int32)
    for place, entries in enumerate(found):
        table[place, 0] = len(entries)
        for p in range(most):
            if entries:
                source, piece = entries[min(p, len(entries) - 1)]
                table[place, 1 + p] = source
                table[place, 1 + most + p] = piece
    return table, most


def matmul_kernel(plan, info, *refs):
    base, most, tp, spans, sources, prior_at, final, skip = plan
    parts = len(spans)
    count = sources * parts
    inputs = [refs[s * parts : (s + 1) * parts] for s in range(sources)]
    weight = refs[count]
    at = count + 1
    prior = refs[at] if prior_at is not None else None
    at += (prior_at is not None) + skip
    number = tp if final else 1
    outs = refs[at : at + number]
    token = refs[at + number]
    held, total, sems, early_sems, late_sems = refs[at + number + 1 :]
    rows = total.shape[1]
    step = pl.program_id(0)
    p = step // tp
    t = step % tp
    me = info[0]
    pieces = info[base]

    def load_prior(t):
        return pltpu.make_async_copy(
            prior.at[t, prior_at : prior_at + rows], total.at[t], early_sems.at[t]
        )

    def store(t):
        return pltpu.make_async_copy(total.at[t], outs[0].at[t], late_sems.at[t])

    @pl.when(step == 0)
    def _():
        for q in range(most):
            for s in range(sources):

                @pl.when((q < pieces) & (info[base + 1 + q] == s))
                def _():
                    for n, (first, size) in enumerate(spans):
                        pltpu.make_async_copy(
                            inputs[s][n], held.at[q, first : first + size], sems.at[q, n]
                        ).start()

        if prior is not None:
            for k in range(tp):
                load_prior(k).start()

    if prior is not None:

        @pl.when(p == 0)
        def _():
            load_prior(t).wait()

    @pl.when(p < pieces)
    def _():
        @pl.when(t == 0)
        def _():
            for n, (first, size) in enumerate(spans):
                pltpu.make_async_copy(
                    inputs[0][n], held.at[p, first : first + size], sems.at[p, n]
                ).wait()

        product = jnp.dot(held[p], weight[...], preferred_element_type=jnp.float32)
        if prior is not None:
            total[t] += product
        else:

            @pl.when(p == 0)
            def _():
                total[t] = product

            @pl.when(p != 0)
            def _():
                total[t] += product

        if not final:

            @pl.when(p == pieces - 1)
            def _():
                store(t).start()

    @pl.when(step == most * tp - 1)
    def _():
        if final:
            for k in range(tp // 2):
                outs[k][...] = total[me ^ (2 * k)]
                outs[tp // 2 + k][...] = total[me ^ (2 * k + 1)].astype(jnp.bfloat16)
        else:
            for k in range(tp):
                store(k).wait()
        token[...] = jnp.zeros(TOKEN, jnp.float32)


def matmul_stage(info, base, most, tp, inputs, weight, prior, prior_at, final, after):
    flat = [part for source in inputs for part in source]
    sizes = [part.shape[0] for part in inputs[0]]
    rows = sum(sizes)
    spans = [(sum(sizes[:n]), size) for n, size in enumerate(sizes)]
    depth = flat[0].shape[1]
    columns = weight.shape[1]
    width = columns // tp

    def weight_block(j, s):
        j = jnp.minimum(j, jnp.maximum(s[base] * tp - 1, 0))
        return s[base + 1 + most + j // tp], j % tp

    operands = [*flat, weight]
    specs = [anywhere()] * len(flat) + [pl.BlockSpec((depth, width), weight_block)]
    if prior is not None:
        operands.append(prior)
        specs.append(anywhere())
    operands += after
    specs += [token_spec()] * len(after)
    if final:
        out_specs = [pl.BlockSpec((rows, width), lambda j, s: (0, 0))] * tp
        out_shape = [jax.ShapeDtypeStruct((rows, width), jnp.float32)] * (tp // 2)
        out_shape += [jax.ShapeDtypeStruct((rows, width), jnp.bfloat16)] * (tp // 2)
    else:
        out_specs = [anywhere()]
        out_shape = [jax.ShapeDtypeStruct((tp, rows, width), jnp.float32)]
    plan = (
        base,
        most,
        tp,
        spans,
        len(inputs),
        None if prior is None else prior_at,
        final,
        len(after),
    )
    return pl.pallas_call(
        functools.partial(matmul_kernel, plan),
        grid_spec=pltpu.PrefetchScalarGridSpec(
            num_scalar_prefetch=1,
            grid=(most * tp,),
            in_specs=specs,
            out_specs=out_specs + [token_spec()],
            scratch_shapes=[
                pltpu.VMEM((most, rows, depth), jnp.bfloat16),
                pltpu.VMEM((tp, rows, width), jnp.float32),
                pltpu.SemaphoreType.DMA((most, len(sizes))),
                pltpu.SemaphoreType.DMA((tp,)),
                pltpu.SemaphoreType.DMA((tp,)),
            ],
        ),
        out_shape=out_shape + [TOKEN_SHAPE],
        compiler_params=params(),
        cost_estimate=pl.CostEstimate(flops=1, bytes_accessed=1, transcendentals=0),
        name="matmul_stage",
    )(info, *operands)


def gate_kernel(count, *refs):
    refs[-1][...] = jnp.zeros(TOKEN, jnp.float32)


def gate(values, after):
    count = len(values)
    outs = pl.pallas_call(
        functools.partial(gate_kernel, count),
        grid=(1,),
        in_specs=[anywhere()] * count + [token_spec()] * len(after),
        out_specs=[anywhere()] * count + [token_spec()],
        out_shape=[jax.ShapeDtypeStruct(v.shape, v.dtype) for v in values] + [TOKEN_SHAPE],
        input_output_aliases={n: n for n in range(count)},
        compiler_params=params(),
        cost_estimate=pl.CostEstimate(flops=1, bytes_accessed=1, transcendentals=0),
        name="gate",
    )(*values, *after)
    return list(outs[:count]), [outs[count]]


def halve_kernel(half, more, *refs):
    keep = refs[: 2 * half] if half > 1 else [None, refs[0]]
    got = refs[len(keep) : len(keep) + 2 * half] if half > 1 else [None, refs[1]]
    outs = refs[(4 * half if half > 1 else 2) + more :]
    for k in range(half):
        value = keep[2 * k + 1][...] + got[2 * k + 1][...].astype(jnp.float32)
        outs[k][...] = value.astype(jnp.bfloat16)
        if half > 1:
            outs[half + k][...] = keep[2 * k][...] + got[2 * k][...].astype(jnp.float32)
    outs[-1][...] = jnp.zeros(TOKEN, jnp.float32)


def halve(keep, got, after):
    half = len(keep) // 2
    rows, width = keep[0].shape
    operands = [*keep, *got] if half > 1 else [keep[1], got[1]]
    flat = pl.BlockSpec((rows, width), lambda i: (0, 0))
    out_shape = [jax.ShapeDtypeStruct((rows, width), jnp.bfloat16)] * half
    if half > 1:
        out_shape += [jax.ShapeDtypeStruct((rows, width), jnp.float32)] * half
    outs = pl.pallas_call(
        functools.partial(halve_kernel, half, len(after)),
        grid=(1,),
        in_specs=[flat] * len(operands) + [token_spec()] * len(after),
        out_specs=[flat] * len(out_shape) + [token_spec()],
        out_shape=out_shape + [TOKEN_SHAPE],
        compiler_params=params(),
        cost_estimate=pl.CostEstimate(flops=1, bytes_accessed=1, transcendentals=0),
        name="halve",
    )(*operands, *after)
    return outs[:half], outs[half:-1], outs[-1]


def stream_kernel(more, keep, first, last, signs, matrix, residual, *refs):
    stream, chunk, squares = refs[more:]
    total = keep[...] + first[...].astype(jnp.float32) + last[...].astype(jnp.float32)
    total = total * signs[...].astype(jnp.float32)
    rows, width = total.shape
    turn = matrix[...]
    for b in range(width // 128):
        piece = total[:, b * 128 : (b + 1) * 128]
        rotated = jnp.zeros((rows, 128), jnp.float32)
        for _ in range(3):
            part = piece.astype(jnp.bfloat16)
            rotated = rotated + jnp.dot(part, turn, preferred_element_type=jnp.float32)
            piece = piece - part.astype(jnp.float32)
        kept = residual[:, b * 128 : (b + 1) * 128].astype(jnp.float32)
        value = (kept + rotated * H_SCALE).astype(jnp.bfloat16)
        stream[:, b * 128 : (b + 1) * 128] = value
        chunk[:, b * 128 : (b + 1) * 128] = value
    local = chunk[...].astype(jnp.float32)
    squares[...] = jnp.zeros_like(squares)
    squares[:, 0:rows] = lax.dot_general(
        jnp.ones((8, width), jnp.float32),
        local * local,
        (((1,), (1,)), ((), ())),
        precision=lax.Precision.HIGHEST,
        preferred_element_type=jnp.float32,
    )


def stream_rows(keep, first, last, signs, matrix, residual, so_far, start, after):
    rows, width = keep.shape
    place = start // rows
    line = pl.BlockSpec((rows, width), lambda i: (place, 0))
    operands = [keep, first, last, signs, matrix, residual]
    specs = [pl.BlockSpec((rows, width), lambda i: (0, 0))] * 3 + [
        pl.BlockSpec((1, width), lambda i: (0, 0)),
        pl.BlockSpec((128, 128), lambda i: (0, 0)),
        line,
    ]
    aliases = {}
    if so_far is not None:
        aliases = {len(operands): 0}
        operands.append(so_far)
        specs.append(anywhere())
    operands += after
    specs += [token_spec()] * len(after)
    return pl.pallas_call(
        functools.partial(stream_kernel, len(aliases) + len(after)),
        grid=(1,),
        in_specs=specs,
        out_specs=[
            line,
            pl.BlockSpec((rows, width), lambda i: (0, 0)),
            pl.BlockSpec((8, lanes(rows)), lambda i: (0, 0)),
        ],
        out_shape=[
            jax.ShapeDtypeStruct(residual.shape, jnp.bfloat16),
            jax.ShapeDtypeStruct((rows, width), jnp.bfloat16),
            jax.ShapeDtypeStruct((8, lanes(rows)), jnp.float32),
        ],
        input_output_aliases=aliases,
        compiler_params=params(),
        cost_estimate=pl.CostEstimate(flops=1, bytes_accessed=1, transcendentals=0),
        name="stream_rows",
    )(*operands)


def norm_kernel(places, more, info, *refs):
    tp = len(places)
    pieces = refs[:tp]
    first, second, gain = refs[tp : tp + 3]
    out, token, scale = refs[tp + 3 + more :]
    step = pl.program_id(0)

    @pl.when(step == 0)
    def _():
        inverse = lax.rsqrt((first[...] + second[...]) / D + 1e-05)
        scale[...] = jnp.transpose(inverse)
        token[...] = jnp.zeros(TOKEN, jnp.float32)

    rows, width = pieces[0].shape
    factor = scale[pl.ds(pl.multiple_of(step * rows, rows), rows), 0:1]
    for e, piece in zip(places, pieces):
        at = pl.ds(pl.multiple_of((info[0] ^ e) * width, width), width)
        value = piece[...].astype(jnp.float32) * factor * gain[:, at]
        out[:, at] = value.astype(jnp.bfloat16)


def norm_rows(info, pieces, squares, column, gain, so_far, start, all_rows, after):
    tp = len(pieces)
    rows, width = pieces[0][1].shape
    tiles = 4 if rows % 64 == 0 else 1
    tile = rows // tiles
    place = start // tile
    small = pl.BlockSpec((8, lanes(rows)), lambda i, s: (0, column))
    operands = [piece for _, piece in pieces] + [*squares, gain]
    specs = (
        [pl.BlockSpec((tile, width), lambda i, s: (i, 0))] * tp
        + [small] * 2
        + [pl.BlockSpec((1, tp * width), lambda i, s: (0, 0))]
    )
    aliases = {}
    if so_far is not None:
        aliases = {1 + len(operands): 0}
        operands.append(so_far)
        specs.append(anywhere())
    operands += after
    specs += [token_spec()] * len(after)
    return pl.pallas_call(
        functools.partial(norm_kernel, [e for e, _ in pieces], len(aliases) + len(after)),
        grid_spec=pltpu.PrefetchScalarGridSpec(
            num_scalar_prefetch=1,
            grid=(tiles,),
            in_specs=specs,
            out_specs=[
                pl.BlockSpec((tile, tp * width), lambda i, s: (place + i, 0)),
                token_spec(),
            ],
            scratch_shapes=[pltpu.VMEM((lanes(rows), 8), jnp.float32)],
        ),
        out_shape=[jax.ShapeDtypeStruct((all_rows, tp * width), jnp.bfloat16), TOKEN_SHAPE],
        input_output_aliases=aliases,
        compiler_params=params(),
        cost_estimate=pl.CostEstimate(flops=1, bytes_accessed=1, transcendentals=0),
        name="norm_rows",
    )(info, *operands)


def shards(sub, tp, gate_pre, up_pre, down_weight, residual, signs, row_slot, norm_gain):
    rows = gate_pre.shape[0]
    width = residual.shape[1]
    place = lax.axis_index("sub").astype(jnp.int32)
    me = lax.axis_index("tp").astype(jnp.int32)
    matrix = hadamard_signs()
    mine = jnp.take(residual, row_slot, axis=0, mode="clip")
    signs_own = lax.dynamic_slice_in_dim(signs, me * width, width, 0).reshape(1, width)
    gain = norm_gain.reshape(1, -1)
    bits = [1 << b for b in range(tp.bit_length() - 1)]

    sizes = row_units(rows)
    starts = [sum(sizes[:u]) for u in range(len(sizes))]

    def swap(value, d):
        return lax.ppermute(value, "tp", [(i, i ^ d) for i in range(tp)])

    def onward(pair, d):
        up = lax.ppermute(pair[0], "sub", [(i, i + 1) for i in range(d - 1, sub - 1)])
        down = lax.ppermute(pair[1], "sub", [(i, i - 1) for i in range(1, sub - d + 1)])
        return [up, down]

    def matmul(stages, inputs, prior, start, final, after):
        base, most = bases[tuple(stages)]
        return matmul_stage(
            info, base, most, tp, inputs, down_weight, prior, start, final, after
        )

    terms, held = {}, {}
    streams = [None]
    pieces, squares = {}, {}

    def begin_sums(u, sums):
        terms[u] = [sums[: tp // 2], [swap(value, bits[0]) for value in sums[tp // 2 :]]]

    def halve_sums(u, after):
        keep, got = terms[u]
        for bit in bits[1:]:
            send, kept, token = halve(keep, got, after)
            after = [token]
            arrived = [swap(value, bit) for value in send]
            if kept:
                keep, got = kept, arrived
        terms[u] = [keep[0], got[0], arrived[0]]
        return after

    def finish(u, after):
        streams[0], chunk, squares[u] = stream_rows(
            *terms[u], signs_own, matrix, mine, streams[0], starts[u], after
        )
        pieces[u] = [(0, chunk)]
        for bit in reversed(bits[1:]):
            pieces[u] += [(e | bit, swap(value, bit)) for e, value in pieces[u]]
        return [squares[u]]

    def spread(u, after):
        token = after
        if after:
            values, token = gate([value for _, value in pieces[u][1:]], after)
            pieces[u][1:] = [(e, value) for (e, _), value in zip(pieces[u][1:], values)]
        pieces[u] += [(e | bits[0], swap(value, bits[0])) for e, value in pieces[u]]
        return token

    def sum_along(local):
        total = local
        for d in range(1, sub):
            total = total + lax.ppermute(local, "sub", [(i, (i + d) % sub) for i in range(sub)])
        return total

    def sum_across(total):
        for bit in reversed(bits[1:]):
            total = total + swap(total, bit)
        return [total, swap(total, bits[0])]

    normed = [None]

    def normalise(us, totals, after):
        for n, u in enumerate(us):
            normed[0], token = norm_rows(
                info,
                pieces[u],
                totals,
                sum(lanes(sizes[b]) for b in us[:n]) // lanes(sizes[u]),
                gain,
                normed[0],
                starts[u],
                rows,
                after,
            )
            after = [token]
        return after

    early, middle, late = [0, 1], list(range(2, sub - 1)), [sub - 1]
    bases, tables, base = {}, [], 1
    for stages in (early, middle + late, middle, late):
        table, most = stage_table(sub, stages)
        bases[tuple(stages)] = base, most
        tables.append(table)
        base += table.shape[1]
    info = jnp.concatenate([me[None], jnp.asarray(np.concatenate(tables, axis=1))[place]])
    own = [None] * 3
    came = {}

    def make(u, after):
        own[u], token = hidden_rows(gate_pre, up_pre, starts[u], sizes[u], after)
        came[1, u] = onward([own[u], own[u]], 1)
        return [token]

    def pass_on(u, first, last):
        for d in range(first, last + 1):
            came[d, u] = onward(came[d - 1, u], d)

    def matmul(us, stages, prior, start, final, after):
        inputs = []
        for d in stages:
            if d == 0:
                inputs.append([own[u] for u in us])
            else:
                inputs += [[came[d, u][side] for u in us] for side in range(2)]
        base, most = bases[tuple(stages)]
        return matmul_stage(
            info, base, most, tp, inputs, down_weight, prior, start, final, after
        )

    def hold(keys, after):
        values, token = gate([value for key in keys for value in came[key]], after)
        for n, key in enumerate(keys):
            came[key] = values[2 * n : 2 * n + 2]
        return token

    mid = middle[-1]
    first = gate_pre[: sizes[0]].astype(jnp.float32), up_pre[: sizes[0]].astype(jnp.float32)
    own[0] = (jax.nn.silu(first[0]) * first[1]).astype(jnp.bfloat16)
    came[1, 0] = onward([own[0], own[0]], 1)
    token = make(1, [own[0]])
    (*came[1, 0], mine, signs_own), token = gate([*came[1, 0], mine, signs_own], token)
    pass_on(0, 2, mid)
    token = make(2, token)
    part, *token = matmul([0], early, None, 0, False, token)
    hold([(1, 1)], token)
    pass_on(1, 2, mid)
    token = hold([(mid, 0), (1, 2)], token)
    pass_on(0, sub - 1, sub - 1)
    parts, *token = matmul([1, 2], early, None, 0, False, token)
    token = hold([(1, 2), (mid, 1)], token)
    pass_on(2, 2, mid)
    *sums, token = matmul([0], middle + late, part, 0, True, token)
    begin_sums(0, sums)
    token = hold([(mid, 1)], [token])
    pass_on(1, sub - 1, sub - 1)
    token = halve_sums(0, token)
    token = hold([(mid, 2)], token)
    pass_on(2, sub - 1, sub - 1)
    parts, *token = matmul([1, 2], middle, parts, 0, False, token)
    token = finish(0, token)
    *sums, token = matmul([1], late, parts, 0, True, token)
    begin_sums(1, sums)
    token = spread(0, [token])
    token = halve_sums(1, token)
    *sums, token = matmul([2], late, parts, sizes[1], True, token)
    begin_sums(2, sums)
    token = finish(1, [token])
    token = halve_sums(2, token)
    token = finish(2, token)
    along = sum_along(jnp.concatenate([squares[u] for u in range(3)], axis=1))
    spread(1, token)
    spread(2, [along])
    normalise([0, 1, 2], sum_across(along), token)
    return (streams[0], normed[0])


def solution(mesh):
    return jax.shard_map(
        functools.partial(shards, mesh.shape["sub"], mesh.shape["tp"]),
        mesh=mesh,
        in_specs=(
            P("groups", ("tp", "sub")),
            P("groups", ("tp", "sub")),
            P("tp", "sub"),
            P("groups", ("sub", "tp")),
            P("sub"),
            P("groups"),
            P("sub"),
        ),
        out_specs=(P("groups", ("sub", "tp")), P("groups", "sub")),
        check_vma=False,
    )
```

```python
import functools

import jax
import jax.numpy as jnp
import numpy as np
from jax import lax
from jax.experimental import pallas as pl
from jax.experimental.pallas import tpu as pltpu
from jax.sharding import PartitionSpec as P

D = 16384
H_SCALE = 0.08838834764831845
VMEM = 48 * 1024 * 1024
TOKEN = (8, 128)


def hadamard_signs():
    index = jnp.arange(128, dtype=jnp.int32)
    common = index[:, None] & index[None, :]
    parity = sum((common >> shift & 1 for shift in range(7)))
    return jnp.where(parity % 2 == 0, 1.0, -1.0).astype(jnp.bfloat16)


def row_units(rows):
    return [rows // 3, rows // 3, rows // 3]


def lanes(rows):
    return -(-rows // 128) * 128


def params():
    return pltpu.CompilerParams(vmem_limit_bytes=VMEM)


def anywhere():
    return pl.BlockSpec(memory_space=pl.ANY)


def token_spec():
    return pl.BlockSpec(TOKEN, lambda *_: (0, 0))


TOKEN_SHAPE = jax.ShapeDtypeStruct(TOKEN, jnp.float32)


def hidden_kernel(start, more, gate, up, *refs):
    out, token, held, sems = refs[more:]
    copies = [
        pltpu.make_async_copy(
            source.at[start : start + out.shape[0]], held.at[n], sems.at[n]
        )
        for n, source in enumerate((gate, up))
    ]
    for copy in copies:
        copy.start()
    for copy in copies:
        copy.wait()
    value = held[0].astype(jnp.float32)
    value = value / (1.0 + jnp.exp(-value)) * held[1].astype(jnp.float32)
    out[...] = value.astype(jnp.bfloat16)
    token[...] = jnp.zeros(TOKEN, jnp.float32)


def hidden_rows(gate, up, start, rows, after):
    columns = gate.shape[1]
    return pl.pallas_call(
        functools.partial(hidden_kernel, start, len(after)),
        grid=(1,),
        in_specs=[pl.BlockSpec(memory_space=pltpu.HBM)] * 2 + [token_spec()] * len(after),
        out_specs=[pl.BlockSpec((rows, columns), lambda i: (0, 0)), token_spec()],
        out_shape=[jax.ShapeDtypeStruct((rows, columns), jnp.bfloat16), TOKEN_SHAPE],
        scratch_shapes=[
            pltpu.VMEM((2, rows, columns), jnp.bfloat16),
            pltpu.SemaphoreType.DMA((2,)),
        ],
        compiler_params=params(),
        cost_estimate=pl.CostEstimate(flops=1, bytes_accessed=1, transcendentals=0),
        name="hidden_rows",
    )(gate, up, *after)


def stage_table(sub, stages):
    found = []
    for place in range(sub):
        entries, source = [], 0
        for d in stages:
            if d == 0:
                entries.append((source, place))
                source += 1
                continue
            if place >= d:
                entries.append((source, place - d))
            if place + d < sub:
                entries.append((source + 1, place + d))
            source += 2
        found.append(entries)
    most = max(len(entries) for entries in found)
    table = np.zeros((sub, 1 + 2 * most), np.int32)
    for place, entries in enumerate(found):
        table[place, 0] = len(entries)
        for p in range(most):
            if entries:
                source, piece = entries[min(p, len(entries) - 1)]
                table[place, 1 + p] = source
                table[place, 1 + most + p] = piece
    return table, most


def matmul_kernel(plan, info, *refs):
    base, most, tp, spans, sources, prior_at, final, skip = plan
    parts = len(spans)
    count = sources * parts
    inputs = [refs[s * parts : (s + 1) * parts] for s in range(sources)]
    weight = refs[count]
    at = count + 1
    prior = refs[at] if prior_at is not None else None
    at += (prior_at is not None) + skip
    number = tp if final else 1
    outs = refs[at : at + number]
    token = refs[at + number]
    held, total, sems, early_sems, late_sems = refs[at + number + 1 :]
    rows = total.shape[1]
    step = pl.program_id(0)
    p = step // tp
    t = step % tp
    me = info[0]
    pieces = info[base]

    def load_prior(t):
        return pltpu.make_async_copy(
            prior.at[t, prior_at : prior_at + rows], total.at[t], early_sems.at[t]
        )

    def store(t):
        return pltpu.make_async_copy(total.at[t], outs[0].at[t], late_sems.at[t])

    @pl.when(step == 0)
    def _():
        for q in range(most):
            for s in range(sources):

                @pl.when((q < pieces) & (info[base + 1 + q] == s))
                def _():
                    for n, (first, size) in enumerate(spans):
                        pltpu.make_async_copy(
                            inputs[s][n], held.at[q, first : first + size], sems.at[q, n]
                        ).start()

        if prior is not None:
            for k in range(tp):
                load_prior(k).start()

    if prior is not None:

        @pl.when(p == 0)
        def _():
            load_prior(t).wait()

    @pl.when(p < pieces)
    def _():
        @pl.when(t == 0)
        def _():
            for n, (first, size) in enumerate(spans):
                pltpu.make_async_copy(
                    inputs[0][n], held.at[p, first : first + size], sems.at[p, n]
                ).wait()

        product = jnp.dot(held[p], weight[...], preferred_element_type=jnp.float32)
        if prior is not None:
            total[t] += product
        else:

            @pl.when(p == 0)
            def _():
                total[t] = product

            @pl.when(p != 0)
            def _():
                total[t] += product

        if not final:

            @pl.when(p == pieces - 1)
            def _():
                store(t).start()

    @pl.when(step == most * tp - 1)
    def _():
        if final:
            for k in range(tp // 2):
                outs[k][...] = total[me ^ (2 * k)]
                outs[tp // 2 + k][...] = total[me ^ (2 * k + 1)].astype(jnp.bfloat16)
        else:
            for k in range(tp):
                store(k).wait()
        token[...] = jnp.zeros(TOKEN, jnp.float32)


def matmul_stage(info, base, most, tp, inputs, weight, prior, prior_at, final, after):
    flat = [part for source in inputs for part in source]
    sizes = [part.shape[0] for part in inputs[0]]
    rows = sum(sizes)
    spans = [(sum(sizes[:n]), size) for n, size in enumerate(sizes)]
    depth = flat[0].shape[1]
    columns = weight.shape[1]
    width = columns // tp

    def weight_block(j, s):
        j = jnp.minimum(j, jnp.maximum(s[base] * tp - 1, 0))
        return s[base + 1 + most + j // tp], j % tp

    operands = [*flat, weight]
    specs = [anywhere()] * len(flat) + [pl.BlockSpec((depth, width), weight_block)]
    if prior is not None:
        operands.append(prior)
        specs.append(anywhere())
    operands += after
    specs += [token_spec()] * len(after)
    if final:
        out_specs = [pl.BlockSpec((rows, width), lambda j, s: (0, 0))] * tp
        out_shape = [jax.ShapeDtypeStruct((rows, width), jnp.float32)] * (tp // 2)
        out_shape += [jax.ShapeDtypeStruct((rows, width), jnp.bfloat16)] * (tp // 2)
    else:
        out_specs = [anywhere()]
        out_shape = [jax.ShapeDtypeStruct((tp, rows, width), jnp.float32)]
    plan = (
        base,
        most,
        tp,
        spans,
        len(inputs),
        None if prior is None else prior_at,
        final,
        len(after),
    )
    return pl.pallas_call(
        functools.partial(matmul_kernel, plan),
        grid_spec=pltpu.PrefetchScalarGridSpec(
            num_scalar_prefetch=1,
            grid=(most * tp,),
            in_specs=specs,
            out_specs=out_specs + [token_spec()],
            scratch_shapes=[
                pltpu.VMEM((most, rows, depth), jnp.bfloat16),
                pltpu.VMEM((tp, rows, width), jnp.float32),
                pltpu.SemaphoreType.DMA((most, len(sizes))),
                pltpu.SemaphoreType.DMA((tp,)),
                pltpu.SemaphoreType.DMA((tp,)),
            ],
        ),
        out_shape=out_shape + [TOKEN_SHAPE],
        compiler_params=params(),
        cost_estimate=pl.CostEstimate(flops=1, bytes_accessed=1, transcendentals=0),
        name="matmul_stage",
    )(info, *operands)


def gate_kernel(count, *refs):
    refs[-1][...] = jnp.zeros(TOKEN, jnp.float32)


def gate(values, after):
    count = len(values)
    outs = pl.pallas_call(
        functools.partial(gate_kernel, count),
        grid=(1,),
        in_specs=[anywhere()] * count + [token_spec()] * len(after),
        out_specs=[anywhere()] * count + [token_spec()],
        out_shape=[jax.ShapeDtypeStruct(v.shape, v.dtype) for v in values] + [TOKEN_SHAPE],
        input_output_aliases={n: n for n in range(count)},
        compiler_params=params(),
        cost_estimate=pl.CostEstimate(flops=1, bytes_accessed=1, transcendentals=0),
        name="gate",
    )(*values, *after)
    return list(outs[:count]), [outs[count]]


def halve_kernel(half, cut, more, *refs):
    keep = refs[: 2 * half] if half > 1 else [None, refs[0]]
    got = refs[len(keep) : len(keep) + 2 * half] if half > 1 else [None, refs[1]]
    outs = refs[(4 * half if half > 1 else 2) + more :]
    for k in range(half):
        value = keep[2 * k + 1][...] + got[2 * k + 1][...].astype(jnp.float32)
        value = value.astype(jnp.bfloat16)
        size = value.shape[0] // cut
        for n in range(cut):
            outs[k * cut + n][...] = value[n * size : (n + 1) * size]
        if half > 1:
            outs[half * cut + k][...] = keep[2 * k][...] + got[2 * k][...].astype(jnp.float32)
    outs[-1][...] = jnp.zeros(TOKEN, jnp.float32)


def halve(keep, got, cut, after):
    half = len(keep) // 2
    rows, width = keep[0].shape
    operands = [*keep, *got] if half > 1 else [keep[1], got[1]]
    flat = lambda n: pl.BlockSpec((n, width), lambda i: (0, 0))
    out_specs = [flat(rows // cut)] * (half * cut)
    out_shape = [jax.ShapeDtypeStruct((rows // cut, width), jnp.bfloat16)] * (half * cut)
    if half > 1:
        out_specs += [flat(rows)] * half
        out_shape += [jax.ShapeDtypeStruct((rows, width), jnp.float32)] * half
    outs = pl.pallas_call(
        functools.partial(halve_kernel, half, cut, len(after)),
        grid=(1,),
        in_specs=[flat(rows)] * len(operands) + [token_spec()] * len(after),
        out_specs=out_specs + [token_spec()],
        out_shape=out_shape + [TOKEN_SHAPE],
        compiler_params=params(),
        cost_estimate=pl.CostEstimate(flops=1, bytes_accessed=1, transcendentals=0),
        name="halve",
    )(*operands, *after)
    return outs[: half * cut], outs[half * cut : -1], outs[-1]


def stream_kernel(cut, more, keep, first, *refs):
    last = jnp.concatenate([part[...] for part in refs[:cut]], axis=0)
    signs, matrix, residual = refs[cut : cut + 3]
    stream, chunk, squares = refs[cut + 3 + more :]
    total = keep[...] + first[...].astype(jnp.float32) + last.astype(jnp.float32)
    total = total * signs[...].astype(jnp.float32)
    rows, width = total.shape
    turn = matrix[...]
    for b in range(width // 128):
        piece = total[:, b * 128 : (b + 1) * 128]
        rotated = jnp.zeros((rows, 128), jnp.float32)
        for _ in range(3):
            part = piece.astype(jnp.bfloat16)
            rotated = rotated + jnp.dot(part, turn, preferred_element_type=jnp.float32)
            piece = piece - part.astype(jnp.float32)
        kept = residual[:, b * 128 : (b + 1) * 128].astype(jnp.float32)
        value = (kept + rotated * H_SCALE).astype(jnp.bfloat16)
        stream[:, b * 128 : (b + 1) * 128] = value
        chunk[:, b * 128 : (b + 1) * 128] = value
    local = chunk[...].astype(jnp.float32)
    squares[...] = jnp.zeros_like(squares)
    squares[:, 0:rows] = lax.dot_general(
        jnp.ones((8, width), jnp.float32),
        local * local,
        (((1,), (1,)), ((), ())),
        precision=lax.Precision.HIGHEST,
        preferred_element_type=jnp.float32,
    )


def stream_rows(keep, first, last, signs, matrix, residual, so_far, start, after):
    rows, width = keep.shape
    place = start // rows
    line = pl.BlockSpec((rows, width), lambda i: (place, 0))
    cut = len(last)
    flat = lambda n: pl.BlockSpec((n, width), lambda i: (0, 0))
    operands = [keep, first, *last, signs, matrix, residual]
    specs = [flat(rows)] * 2 + [flat(rows // cut)] * cut
    specs += [
        pl.BlockSpec((1, width), lambda i: (0, 0)),
        pl.BlockSpec((128, 128), lambda i: (0, 0)),
        line,
    ]
    aliases = {}
    if so_far is not None:
        aliases = {len(operands): 0}
        operands.append(so_far)
        specs.append(anywhere())
    operands += after
    specs += [token_spec()] * len(after)
    return pl.pallas_call(
        functools.partial(stream_kernel, cut, len(aliases) + len(after)),
        grid=(1,),
        in_specs=specs,
        out_specs=[
            line,
            pl.BlockSpec((rows, width), lambda i: (0, 0)),
            pl.BlockSpec((8, lanes(rows)), lambda i: (0, 0)),
        ],
        out_shape=[
            jax.ShapeDtypeStruct(residual.shape, jnp.bfloat16),
            jax.ShapeDtypeStruct((rows, width), jnp.bfloat16),
            jax.ShapeDtypeStruct((8, lanes(rows)), jnp.float32),
        ],
        input_output_aliases=aliases,
        compiler_params=params(),
        cost_estimate=pl.CostEstimate(flops=1, bytes_accessed=1, transcendentals=0),
        name="stream_rows",
    )(*operands)


def norm_kernel(places, sums, more, info, *refs):
    tp = len(places)
    pieces = refs[:tp]
    squares = refs[tp : tp + sums]
    gain = refs[tp + sums]
    out, token = refs[tp + sums + 1 + more :]
    token[...] = jnp.zeros(TOKEN, jnp.float32)
    total = 0.0
    for values in squares:
        for first in range(0, values.shape[0], 8):
            total = total + values[first : first + 8]
    inverse = lax.rsqrt(total / D + 1e-05)
    rows, width = pieces[0].shape
    scale = jnp.transpose(inverse)[0:rows, 0:1]
    for e, piece in zip(places, pieces):
        at = pl.ds(pl.multiple_of((info[0] ^ e) * width, width), width)
        value = piece[...].astype(jnp.float32) * scale * gain[:, at]
        out[:, at] = value.astype(jnp.bfloat16)


def norm_rows(info, pieces, squares, gain, so_far, start, all_rows, after):
    tp = len(pieces)
    rows, width = pieces[0][1].shape
    place = start // rows
    operands = [piece for _, piece in pieces] + [*squares, gain]
    specs = (
        [pl.BlockSpec((rows, width), lambda i, s: (0, 0))] * tp
        + [pl.BlockSpec(values.shape, lambda i, s: (0, 0)) for values in squares]
        + [pl.BlockSpec((1, tp * width), lambda i, s: (0, 0))]
    )
    aliases = {}
    if so_far is not None:
        aliases = {1 + len(operands): 0}
        operands.append(so_far)
        specs.append(anywhere())
    operands += after
    specs += [token_spec()] * len(after)
    more = len(aliases) + len(after)
    return pl.pallas_call(
        functools.partial(norm_kernel, [e for e, _ in pieces], len(squares), more),
        grid_spec=pltpu.PrefetchScalarGridSpec(
            num_scalar_prefetch=1,
            grid=(1,),
            in_specs=specs,
            out_specs=[
                pl.BlockSpec((rows, tp * width), lambda i, s: (place, 0)),
                token_spec(),
            ],
        ),
        out_shape=[jax.ShapeDtypeStruct((all_rows, tp * width), jnp.bfloat16), TOKEN_SHAPE],
        input_output_aliases=aliases,
        compiler_params=params(),
        cost_estimate=pl.CostEstimate(flops=1, bytes_accessed=1, transcendentals=0),
        name="norm_rows",
    )(info, *operands)


def shards(sub, tp, gate_pre, up_pre, down_weight, residual, signs, row_slot, norm_gain):
    rows = gate_pre.shape[0]
    width = residual.shape[1]
    place = lax.axis_index("sub").astype(jnp.int32)
    me = lax.axis_index("tp").astype(jnp.int32)
    matrix = hadamard_signs()
    mine = jnp.take(residual, row_slot, axis=0, mode="clip")
    signs_own = lax.dynamic_slice_in_dim(signs, me * width, width, 0).reshape(1, width)
    gain = norm_gain.reshape(1, -1)
    bits = [1 << b for b in range(tp.bit_length() - 1)]

    sizes = row_units(rows)
    starts = [sum(sizes[:u]) for u in range(len(sizes))]

    def swap(value, d):
        return lax.ppermute(value, "tp", [(i, i ^ d) for i in range(tp)])

    def onward(pair, d):
        up = lax.ppermute(pair[0], "sub", [(i, i + 1) for i in range(d - 1, sub - 1)])
        down = lax.ppermute(pair[1], "sub", [(i, i - 1) for i in range(1, sub - d + 1)])
        return [up, down]

    def matmul(stages, inputs, prior, start, final, after):
        base, most = bases[tuple(stages)]
        return matmul_stage(
            info, base, most, tp, inputs, down_weight, prior, start, final, after
        )

    terms, held = {}, {}
    streams = [None]
    pieces, squares = {}, {}

    def begin_sums(u, sums):
        terms[u] = [sums[: tp // 2], [swap(value, bits[0]) for value in sums[tp // 2 :]]]

    def halve_sums(u, after, cut=1):
        keep, got = terms[u]
        for bit in bits[1:]:
            send, kept, token = halve(keep, got, cut if bit == bits[-1] else 1, after)
            after = [token]
            arrived = [swap(value, bit) for value in send]
            if kept:
                keep, got = kept, arrived
        terms[u] = [keep[0], got[0], arrived]
        return after

    def finish(u, after):
        streams[0], chunk, squares[u] = stream_rows(
            *terms[u], signs_own, matrix, mine, streams[0], starts[u], after
        )
        pieces[u] = [(0, chunk)]
        for bit in reversed(bits[1:]):
            pieces[u] += [(e | bit, swap(value, bit)) for e, value in pieces[u]]
        return [squares[u]]

    def spread(u, after):
        token = after
        if after:
            values, token = gate([value for _, value in pieces[u][1:]], after)
            pieces[u][1:] = [(e, value) for (e, _), value in zip(pieces[u][1:], values)]
        pieces[u] += [(e | bits[0], swap(value, bits[0])) for e, value in pieces[u]]
        return token

    def sum_along(local):
        total = local
        for d in range(1, sub):
            total = total + lax.ppermute(local, "sub", [(i, (i + d) % sub) for i in range(sub)])
        return total

    def sum_across(total):
        for bit in reversed(bits[1:]):
            total = total + swap(total, bit)
        return [total, swap(total, bits[0])]

    normed = [None]

    def normalise(u, totals, after):
        normed[0], token = norm_rows(
            info, pieces[u], totals, gain, normed[0], starts[u], rows, after
        )
        return [token]

    def gather_squares(u):
        return [lax.all_gather(squares[u], ("sub", "tp"), axis=0, tiled=True)]

    early, middle, late = [0, 1], list(range(2, sub - 1)), [sub - 1]
    bases, tables, base = {}, [], 1
    for stages in (early, middle + late, middle, late):
        table, most = stage_table(sub, stages)
        bases[tuple(stages)] = base, most
        tables.append(table)
        base += table.shape[1]
    info = jnp.concatenate([me[None], jnp.asarray(np.concatenate(tables, axis=1))[place]])
    own = [None] * 3
    came = {}

    def make(u, after):
        own[u], token = hidden_rows(gate_pre, up_pre, starts[u], sizes[u], after)
        came[1, u] = onward([own[u], own[u]], 1)
        return [token]

    def pass_on(u, first, last):
        for d in range(first, last + 1):
            came[d, u] = onward(came[d - 1, u], d)

    def matmul(us, stages, prior, start, final, after):
        inputs = []
        for d in stages:
            if d == 0:
                inputs.append([own[u] for u in us])
            else:
                inputs += [[came[d, u][side] for u in us] for side in range(2)]
        base, most = bases[tuple(stages)]
        return matmul_stage(
            info, base, most, tp, inputs, down_weight, prior, start, final, after
        )

    def hold(keys, after):
        values, token = gate([value for key in keys for value in came[key]], after)
        for n, key in enumerate(keys):
            came[key] = values[2 * n : 2 * n + 2]
        return token

    mid = middle[-1]
    first = gate_pre[: sizes[0]].astype(jnp.float32), up_pre[: sizes[0]].astype(jnp.float32)
    own[0] = (jax.nn.silu(first[0]) * first[1]).astype(jnp.bfloat16)
    came[1, 0] = onward([own[0], own[0]], 1)
    token = make(1, [own[0]])
    (*came[1, 0], mine, signs_own), token = gate([*came[1, 0], mine, signs_own], token)
    pass_on(0, 2, mid)
    token = make(2, token)
    part, *token = matmul([0], early, None, 0, False, token)
    hold([(1, 1)], token)
    pass_on(1, 2, mid)
    token = hold([(mid, 0), (1, 2)], token)
    pass_on(0, sub - 1, sub - 1)
    parts, *token = matmul([1, 2], early, None, 0, False, token)
    token = hold([(1, 2), (mid, 1)], token)
    pass_on(2, 2, mid)
    *sums, token = matmul([0], middle + late, part, 0, True, token)
    begin_sums(0, sums)
    token = hold([(mid, 1)], [token])
    pass_on(1, sub - 1, sub - 1)
    token = halve_sums(0, token)
    token = hold([(mid, 2)], token)
    pass_on(2, sub - 1, sub - 1)
    parts, *token = matmul([1, 2], middle, parts, 0, False, token)
    token = finish(0, token)
    sums_0 = gather_squares(0)
    *sums, token = matmul([1], late, parts, 0, True, token)
    begin_sums(1, sums)
    token = spread(0, [token])
    token = halve_sums(1, token, 2)
    token = finish(1, token)
    sums_1 = gather_squares(1)
    *sums, token = matmul([2], late, parts, sizes[1], True, token)
    begin_sums(2, sums)
    token = spread(1, [token])
    token = halve_sums(2, token)
    token = finish(2, token)
    along = sum_along(squares[2])
    token = normalise(0, sums_0, token)
    token = normalise(1, sums_1, token)
    spread(2, [along, *token])
    normalise(2, sum_across(along), token)
    return (streams[0], normed[0])


def solution(mesh):
    return jax.shard_map(
        functools.partial(shards, mesh.shape["sub"], mesh.shape["tp"]),
        mesh=mesh,
        in_specs=(
            P("groups", ("tp", "sub")),
            P("groups", ("tp", "sub")),
            P("tp", "sub"),
            P("groups", ("sub", "tp")),
            P("sub"),
            P("groups"),
            P("sub"),
        ),
        out_specs=(P("groups", ("sub", "tp")), P("groups", "sub")),
        check_vma=False,
    )
```

```python
import functools

import jax
import jax.numpy as jnp
import numpy as np
from jax import lax
from jax.experimental import pallas as pl
from jax.experimental.pallas import tpu as pltpu
from jax.sharding import PartitionSpec as P

D = 16384
H_SCALE = 0.08838834764831845
VMEM = 48 * 1024 * 1024
TOKEN = (8, 128)


def hadamard_signs():
    index = jnp.arange(128, dtype=jnp.int32)
    common = index[:, None] & index[None, :]
    parity = sum((common >> shift & 1 for shift in range(7)))
    return jnp.where(parity % 2 == 0, 1.0, -1.0).astype(jnp.bfloat16)


def row_units(rows):
    return [rows // 3, rows // 3, rows // 3]


def lanes(rows):
    return -(-rows // 128) * 128


def params():
    return pltpu.CompilerParams(vmem_limit_bytes=VMEM)


def anywhere():
    return pl.BlockSpec(memory_space=pl.ANY)


def token_spec():
    return pl.BlockSpec(TOKEN, lambda *_: (0, 0))


TOKEN_SHAPE = jax.ShapeDtypeStruct(TOKEN, jnp.float32)


def hidden_kernel(start, more, gate, up, *refs):
    out, token, held, sems = refs[more:]
    copies = [
        pltpu.make_async_copy(
            source.at[start : start + out.shape[0]], held.at[n], sems.at[n]
        )
        for n, source in enumerate((gate, up))
    ]
    for copy in copies:
        copy.start()
    for copy in copies:
        copy.wait()
    value = held[0].astype(jnp.float32)
    value = value / (1.0 + jnp.exp(-value)) * held[1].astype(jnp.float32)
    out[...] = value.astype(jnp.bfloat16)
    token[...] = jnp.zeros(TOKEN, jnp.float32)


def hidden_rows(gate, up, start, rows, after):
    columns = gate.shape[1]
    return pl.pallas_call(
        functools.partial(hidden_kernel, start, len(after)),
        grid=(1,),
        in_specs=[pl.BlockSpec(memory_space=pltpu.HBM)] * 2 + [token_spec()] * len(after),
        out_specs=[pl.BlockSpec((rows, columns), lambda i: (0, 0)), token_spec()],
        out_shape=[jax.ShapeDtypeStruct((rows, columns), jnp.bfloat16), TOKEN_SHAPE],
        scratch_shapes=[
            pltpu.VMEM((2, rows, columns), jnp.bfloat16),
            pltpu.SemaphoreType.DMA((2,)),
        ],
        compiler_params=params(),
        cost_estimate=pl.CostEstimate(flops=1, bytes_accessed=1, transcendentals=0),
        name="hidden_rows",
    )(gate, up, *after)


def stage_table(sub, stages):
    found = []
    for place in range(sub):
        entries, source = [], 0
        for d in stages:
            if d == 0:
                entries.append((source, place))
                source += 1
                continue
            if place >= d:
                entries.append((source, place - d))
            if place + d < sub:
                entries.append((source + 1, place + d))
            source += 2
        found.append(entries)
    most = max(len(entries) for entries in found)
    table = np.zeros((sub, 1 + 2 * most), np.int32)
    for place, entries in enumerate(found):
        table[place, 0] = len(entries)
        for p in range(most):
            if entries:
                source, piece = entries[min(p, len(entries) - 1)]
                table[place, 1 + p] = source
                table[place, 1 + most + p] = piece
    return table, most


def matmul_kernel(plan, info, *refs):
    base, most, tp, spans, sources, prior_at, final, skip = plan
    parts = len(spans)
    count = sources * parts
    inputs = [refs[s * parts : (s + 1) * parts] for s in range(sources)]
    weight = refs[count]
    at = count + 1
    prior = refs[at] if prior_at is not None else None
    at += (prior_at is not None) + skip
    number = tp if final else 1
    outs = refs[at : at + number]
    token = refs[at + number]
    held, total, sems, early_sems, late_sems = refs[at + number + 1 :]
    rows = total.shape[1]
    step = pl.program_id(0)
    p = step // tp
    t = step % tp
    me = info[0]
    pieces = info[base]

    def load_prior(t):
        return pltpu.make_async_copy(
            prior.at[t, prior_at : prior_at + rows], total.at[t], early_sems.at[t]
        )

    def store(t):
        return pltpu.make_async_copy(total.at[t], outs[0].at[t], late_sems.at[t])

    @pl.when(step == 0)
    def _():
        for q in range(most):
            for s in range(sources):

                @pl.when((q < pieces) & (info[base + 1 + q] == s))
                def _():
                    for n, (first, size) in enumerate(spans):
                        pltpu.make_async_copy(
                            inputs[s][n], held.at[q, first : first + size], sems.at[q, n]
                        ).start()

        if prior is not None:
            for k in range(tp):
                load_prior(k).start()

    if prior is not None:

        @pl.when(p == 0)
        def _():
            load_prior(t).wait()

    @pl.when(p < pieces)
    def _():
        @pl.when(t == 0)
        def _():
            for n, (first, size) in enumerate(spans):
                pltpu.make_async_copy(
                    inputs[0][n], held.at[p, first : first + size], sems.at[p, n]
                ).wait()

        product = jnp.dot(held[p], weight[...], preferred_element_type=jnp.float32)
        if prior is not None:
            total[t] += product
        else:

            @pl.when(p == 0)
            def _():
                total[t] = product

            @pl.when(p != 0)
            def _():
                total[t] += product

        if not final:

            @pl.when(p == pieces - 1)
            def _():
                store(t).start()

    @pl.when(step == most * tp - 1)
    def _():
        if final:
            for k in range(tp // 2):
                outs[k][...] = total[me ^ (2 * k)]
                outs[tp // 2 + k][...] = total[me ^ (2 * k + 1)].astype(jnp.bfloat16)
        else:
            for k in range(tp):
                store(k).wait()
        token[...] = jnp.zeros(TOKEN, jnp.float32)


def matmul_stage(info, base, most, tp, inputs, weight, prior, prior_at, final, after):
    flat = [part for source in inputs for part in source]
    sizes = [part.shape[0] for part in inputs[0]]
    rows = sum(sizes)
    spans = [(sum(sizes[:n]), size) for n, size in enumerate(sizes)]
    depth = flat[0].shape[1]
    columns = weight.shape[1]
    width = columns // tp

    def weight_block(j, s):
        j = jnp.minimum(j, jnp.maximum(s[base] * tp - 1, 0))
        return s[base + 1 + most + j // tp], j % tp

    operands = [*flat, weight]
    specs = [anywhere()] * len(flat) + [pl.BlockSpec((depth, width), weight_block)]
    if prior is not None:
        operands.append(prior)
        specs.append(anywhere())
    operands += after
    specs += [token_spec()] * len(after)
    if final:
        out_specs = [pl.BlockSpec((rows, width), lambda j, s: (0, 0))] * tp
        out_shape = [jax.ShapeDtypeStruct((rows, width), jnp.float32)] * (tp // 2)
        out_shape += [jax.ShapeDtypeStruct((rows, width), jnp.bfloat16)] * (tp // 2)
    else:
        out_specs = [anywhere()]
        out_shape = [jax.ShapeDtypeStruct((tp, rows, width), jnp.float32)]
    plan = (
        base,
        most,
        tp,
        spans,
        len(inputs),
        None if prior is None else prior_at,
        final,
        len(after),
    )
    return pl.pallas_call(
        functools.partial(matmul_kernel, plan),
        grid_spec=pltpu.PrefetchScalarGridSpec(
            num_scalar_prefetch=1,
            grid=(most * tp,),
            in_specs=specs,
            out_specs=out_specs + [token_spec()],
            scratch_shapes=[
                pltpu.VMEM((most, rows, depth), jnp.bfloat16),
                pltpu.VMEM((tp, rows, width), jnp.float32),
                pltpu.SemaphoreType.DMA((most, len(sizes))),
                pltpu.SemaphoreType.DMA((tp,)),
                pltpu.SemaphoreType.DMA((tp,)),
            ],
        ),
        out_shape=out_shape + [TOKEN_SHAPE],
        compiler_params=params(),
        cost_estimate=pl.CostEstimate(flops=1, bytes_accessed=1, transcendentals=0),
        name="matmul_stage",
    )(info, *operands)


def gate_kernel(count, *refs):
    refs[-1][...] = jnp.zeros(TOKEN, jnp.float32)


def gate(values, after):
    count = len(values)
    outs = pl.pallas_call(
        functools.partial(gate_kernel, count),
        grid=(1,),
        in_specs=[anywhere()] * count + [token_spec()] * len(after),
        out_specs=[anywhere()] * count + [token_spec()],
        out_shape=[jax.ShapeDtypeStruct(v.shape, v.dtype) for v in values] + [TOKEN_SHAPE],
        input_output_aliases={n: n for n in range(count)},
        compiler_params=params(),
        cost_estimate=pl.CostEstimate(flops=1, bytes_accessed=1, transcendentals=0),
        name="gate",
    )(*values, *after)
    return list(outs[:count]), [outs[count]]


def halve_kernel(half, more, *refs):
    keep = refs[: 2 * half] if half > 1 else [None, refs[0]]
    got = refs[len(keep) : len(keep) + 2 * half] if half > 1 else [None, refs[1]]
    outs = refs[(4 * half if half > 1 else 2) + more :]
    for k in range(half):
        value = keep[2 * k + 1][...] + got[2 * k + 1][...].astype(jnp.float32)
        outs[k][...] = value.astype(jnp.bfloat16)
        if half > 1:
            outs[half + k][...] = keep[2 * k][...] + got[2 * k][...].astype(jnp.float32)
    outs[-1][...] = jnp.zeros(TOKEN, jnp.float32)


def halve(keep, got, after):
    half = len(keep) // 2
    rows, width = keep[0].shape
    operands = [*keep, *got] if half > 1 else [keep[1], got[1]]
    flat = pl.BlockSpec((rows, width), lambda i: (0, 0))
    out_shape = [jax.ShapeDtypeStruct((rows, width), jnp.bfloat16)] * half
    if half > 1:
        out_shape += [jax.ShapeDtypeStruct((rows, width), jnp.float32)] * half
    outs = pl.pallas_call(
        functools.partial(halve_kernel, half, len(after)),
        grid=(1,),
        in_specs=[flat] * len(operands) + [token_spec()] * len(after),
        out_specs=[flat] * len(out_shape) + [token_spec()],
        out_shape=out_shape + [TOKEN_SHAPE],
        compiler_params=params(),
        cost_estimate=pl.CostEstimate(flops=1, bytes_accessed=1, transcendentals=0),
        name="halve",
    )(*operands, *after)
    return outs[:half], outs[half:-1], outs[-1]


def stream_kernel(more, keep, first, last, signs, matrix, residual, *refs):
    stream, chunk, squares = refs[more:]
    total = keep[...] + first[...].astype(jnp.float32) + last[...].astype(jnp.float32)
    total = total * signs[...].astype(jnp.float32)
    rows, width = total.shape
    turn = matrix[...]
    for b in range(width // 128):
        piece = total[:, b * 128 : (b + 1) * 128]
        rotated = jnp.zeros((rows, 128), jnp.float32)
        for _ in range(3):
            part = piece.astype(jnp.bfloat16)
            rotated = rotated + jnp.dot(part, turn, preferred_element_type=jnp.float32)
            piece = piece - part.astype(jnp.float32)
        kept = residual[:, b * 128 : (b + 1) * 128].astype(jnp.float32)
        value = (kept + rotated * H_SCALE).astype(jnp.bfloat16)
        stream[:, b * 128 : (b + 1) * 128] = value
        chunk[:, b * 128 : (b + 1) * 128] = value
    local = chunk[...].astype(jnp.float32)
    squares[...] = jnp.zeros_like(squares)
    squares[:, 0:rows] = lax.dot_general(
        jnp.ones((8, width), jnp.float32),
        local * local,
        (((1,), (1,)), ((), ())),
        precision=lax.Precision.HIGHEST,
        preferred_element_type=jnp.float32,
    )


def stream_rows(keep, first, last, signs, matrix, residual, so_far, start, after):
    rows, width = keep.shape
    place = start // rows
    line = pl.BlockSpec((rows, width), lambda i: (place, 0))
    operands = [keep, first, last, signs, matrix, residual]
    specs = [pl.BlockSpec((rows, width), lambda i: (0, 0))] * 3 + [
        pl.BlockSpec((1, width), lambda i: (0, 0)),
        pl.BlockSpec((128, 128), lambda i: (0, 0)),
        line,
    ]
    aliases = {}
    if so_far is not None:
        aliases = {len(operands): 0}
        operands.append(so_far)
        specs.append(anywhere())
    operands += after
    specs += [token_spec()] * len(after)
    return pl.pallas_call(
        functools.partial(stream_kernel, len(aliases) + len(after)),
        grid=(1,),
        in_specs=specs,
        out_specs=[
            line,
            pl.BlockSpec((rows, width), lambda i: (0, 0)),
            pl.BlockSpec((8, lanes(rows)), lambda i: (0, 0)),
        ],
        out_shape=[
            jax.ShapeDtypeStruct(residual.shape, jnp.bfloat16),
            jax.ShapeDtypeStruct((rows, width), jnp.bfloat16),
            jax.ShapeDtypeStruct((8, lanes(rows)), jnp.float32),
        ],
        input_output_aliases=aliases,
        compiler_params=params(),
        cost_estimate=pl.CostEstimate(flops=1, bytes_accessed=1, transcendentals=0),
        name="stream_rows",
    )(*operands)


def norm_kernel(places, more, info, *refs):
    tp = len(places)
    pieces = refs[:tp]
    first, second, gain = refs[tp : tp + 3]
    out, token = refs[tp + 3 + more :]
    token[...] = jnp.zeros(TOKEN, jnp.float32)
    inverse = lax.rsqrt((first[...] + second[...]) / D + 1e-05)
    rows, width = pieces[0].shape
    scale = jnp.transpose(inverse)[0:rows, 0:1]
    for e, piece in zip(places, pieces):
        at = pl.ds(pl.multiple_of((info[0] ^ e) * width, width), width)
        value = piece[...].astype(jnp.float32) * scale * gain[:, at]
        out[:, at] = value.astype(jnp.bfloat16)


def norm_rows(info, pieces, squares, column, gain, so_far, start, all_rows, after):
    tp = len(pieces)
    rows, width = pieces[0][1].shape
    place = start // rows
    small = pl.BlockSpec((8, lanes(rows)), lambda i, s: (0, column))
    operands = [piece for _, piece in pieces] + [*squares, gain]
    specs = (
        [pl.BlockSpec((rows, width), lambda i, s: (0, 0))] * tp
        + [small] * 2
        + [pl.BlockSpec((1, tp * width), lambda i, s: (0, 0))]
    )
    aliases = {}
    if so_far is not None:
        aliases = {1 + len(operands): 0}
        operands.append(so_far)
        specs.append(anywhere())
    operands += after
    specs += [token_spec()] * len(after)
    return pl.pallas_call(
        functools.partial(norm_kernel, [e for e, _ in pieces], len(aliases) + len(after)),
        grid_spec=pltpu.PrefetchScalarGridSpec(
            num_scalar_prefetch=1,
            grid=(1,),
            in_specs=specs,
            out_specs=[
                pl.BlockSpec((rows, tp * width), lambda i, s: (place, 0)),
                token_spec(),
            ],
        ),
        out_shape=[jax.ShapeDtypeStruct((all_rows, tp * width), jnp.bfloat16), TOKEN_SHAPE],
        input_output_aliases=aliases,
        compiler_params=params(),
        cost_estimate=pl.CostEstimate(flops=1, bytes_accessed=1, transcendentals=0),
        name="norm_rows",
    )(info, *operands)


def shards(sub, tp, gate_pre, up_pre, down_weight, residual, signs, row_slot, norm_gain):
    rows = gate_pre.shape[0]
    width = residual.shape[1]
    place = lax.axis_index("sub").astype(jnp.int32)
    me = lax.axis_index("tp").astype(jnp.int32)
    matrix = hadamard_signs()
    mine = jnp.take(residual, row_slot, axis=0, mode="clip")
    signs_own = lax.dynamic_slice_in_dim(signs, me * width, width, 0).reshape(1, width)
    gain = norm_gain.reshape(1, -1)
    bits = [1 << b for b in range(tp.bit_length() - 1)]

    sizes = row_units(rows)
    starts = [sum(sizes[:u]) for u in range(len(sizes))]

    def swap(value, d):
        return lax.ppermute(value, "tp", [(i, i ^ d) for i in range(tp)])

    def onward(pair, d):
        up = lax.ppermute(pair[0], "sub", [(i, i + 1) for i in range(d - 1, sub - 1)])
        down = lax.ppermute(pair[1], "sub", [(i, i - 1) for i in range(1, sub - d + 1)])
        return [up, down]

    def matmul(stages, inputs, prior, start, final, after):
        base, most = bases[tuple(stages)]
        return matmul_stage(
            info, base, most, tp, inputs, down_weight, prior, start, final, after
        )

    terms, held = {}, {}
    streams = [None]
    pieces, squares = {}, {}

    def begin_sums(u, sums):
        terms[u] = [sums[: tp // 2], [swap(value, bits[0]) for value in sums[tp // 2 :]]]

    def halve_sums(u, after):
        keep, got = terms[u]
        for bit in bits[1:]:
            send, kept, token = halve(keep, got, after)
            after = [token]
            arrived = [swap(value, bit) for value in send]
            if kept:
                keep, got = kept, arrived
        terms[u] = [keep[0], got[0], arrived[0]]
        return after

    def finish(u, after):
        streams[0], chunk, squares[u] = stream_rows(
            *terms[u], signs_own, matrix, mine, streams[0], starts[u], after
        )
        pieces[u] = [(0, chunk)]
        for bit in reversed(bits[1:]):
            pieces[u] += [(e | bit, swap(value, bit)) for e, value in pieces[u]]
        return [squares[u]]

    def spread(u, after):
        token = after
        if after:
            values, token = gate([value for _, value in pieces[u][1:]], after)
            pieces[u][1:] = [(e, value) for (e, _), value in zip(pieces[u][1:], values)]
        pieces[u] += [(e | bits[0], swap(value, bits[0])) for e, value in pieces[u]]
        return token

    def sum_along(local):
        total = local
        for d in range(1, sub):
            total = total + lax.ppermute(local, "sub", [(i, (i + d) % sub) for i in range(sub)])
        return total

    def sum_across(total):
        for bit in reversed(bits[1:]):
            total = total + swap(total, bit)
        return [total, swap(total, bits[0])]

    normed = [None]

    def normalise(us, totals, after):
        for n, u in enumerate(us):
            normed[0], token = norm_rows(
                info,
                pieces[u],
                totals,
                sum(lanes(sizes[b]) for b in us[:n]) // lanes(sizes[u]),
                gain,
                normed[0],
                starts[u],
                rows,
                after,
            )
            after = [token]
        return after

    early, middle, late = [0, 1], list(range(2, sub - 1)), [sub - 1]
    bases, tables, base = {}, [], 1
    for stages in (early, middle + late, middle, late):
        table, most = stage_table(sub, stages)
        bases[tuple(stages)] = base, most
        tables.append(table)
        base += table.shape[1]
    info = jnp.concatenate([me[None], jnp.asarray(np.concatenate(tables, axis=1))[place]])
    own = [None] * 3
    came = {}

    def make(u, after):
        own[u], token = hidden_rows(gate_pre, up_pre, starts[u], sizes[u], after)
        came[1, u] = onward([own[u], own[u]], 1)
        return [token]

    def pass_on(u, first, last):
        for d in range(first, last + 1):
            came[d, u] = onward(came[d - 1, u], d)

    def matmul(us, stages, prior, start, final, after):
        inputs = []
        for d in stages:
            if d == 0:
                inputs.append([own[u] for u in us])
            else:
                inputs += [[came[d, u][side] for u in us] for side in range(2)]
        base, most = bases[tuple(stages)]
        return matmul_stage(
            info, base, most, tp, inputs, down_weight, prior, start, final, after
        )

    def hold(keys, after):
        values, token = gate([value for key in keys for value in came[key]], after)
        for n, key in enumerate(keys):
            came[key] = values[2 * n : 2 * n + 2]
        return token

    mid = middle[-1]
    first = gate_pre[: sizes[0]].astype(jnp.float32), up_pre[: sizes[0]].astype(jnp.float32)
    own[0] = (jax.nn.silu(first[0]) * first[1]).astype(jnp.bfloat16)
    came[1, 0] = onward([own[0], own[0]], 1)
    token = make(1, [own[0]])
    (*came[1, 0], mine, signs_own), token = gate([*came[1, 0], mine, signs_own], token)
    pass_on(0, 2, mid)
    token = make(2, token)
    part, *token = matmul([0], early, None, 0, False, token)
    hold([(1, 1)], token)
    pass_on(1, 2, mid)
    token = hold([(mid, 0), (1, 2)], token)
    pass_on(0, sub - 1, sub - 1)
    parts, *token = matmul([1, 2], early, None, 0, False, token)
    token = hold([(1, 2), (mid, 1)], token)
    pass_on(2, 2, mid)
    *sums, token = matmul([0], middle + late, part, 0, True, token)
    begin_sums(0, sums)
    token = hold([(mid, 1)], [token])
    pass_on(1, sub - 1, sub - 1)
    token = halve_sums(0, token)
    token = hold([(mid, 2)], token)
    pass_on(2, sub - 1, sub - 1)
    parts, *token = matmul([1, 2], middle, parts, 0, False, token)
    token = finish(0, token)
    *sums, token = matmul([1], late, parts, 0, True, token)
    begin_sums(1, sums)
    token = spread(0, [token])
    token = halve_sums(1, token)
    *sums, token = matmul([2], late, parts, sizes[1], True, token)
    begin_sums(2, sums)
    token = finish(1, [token])
    token = halve_sums(2, token)
    token = finish(2, token)
    along = sum_along(jnp.concatenate([squares[u] for u in range(3)], axis=1))
    spread(1, token)
    spread(2, [along])
    normalise([0, 1, 2], sum_across(along), token)
    return (streams[0], normed[0])


def solution(mesh):
    return jax.shard_map(
        functools.partial(shards, mesh.shape["sub"], mesh.shape["tp"]),
        mesh=mesh,
        in_specs=(
            P("groups", ("tp", "sub")),
            P("groups", ("tp", "sub")),
            P("tp", "sub"),
            P("groups", ("sub", "tp")),
            P("sub"),
            P("groups"),
            P("sub"),
        ),
        out_specs=(P("groups", ("sub", "tp")), P("groups", "sub")),
        check_vma=False,
    )
```
